32 devices in a mesh: dp: 4 (over z), fsdp: 8 (over y, x, core).
Axes of the slice: x: 2, y: 2, z: 4, core: 2. Of those that a mesh axis runs over, the one named last changes fastest.
Arguments:
- latents: bfloat16 [2, 32, 256, 384], P(None, ('dp', 'fsdp')), may hold values from -6 to 6
- condition: bfloat16 [2, 32, 384], P(None, ('dp', 'fsdp')), may hold values from -6 to 6
- cotangent: bfloat16 [2, 32, 256, 384], P(None, ('dp', 'fsdp')), may hold values from -6 to 6
- counts: int32 [2, 32], P(None, ('dp', 'fsdp')), may hold values from 0 to 1, as said below
- ada_weight: bfloat16 [384, 2304], P('fsdp'), may hold values from -0.3125 to 0.3125
- ada_bias: bfloat16 [2304], P('fsdp'), may hold values from -4 to 4
- qkv_weight: bfloat16 [384, 1152], P('fsdp'), may hold values from -0.4375 to 0.4375
- qv_bias: bfloat16 [768], P('fsdp'), may hold values from -4 to 4
- proj_weight: bfloat16 [384, 384], P('fsdp'), may hold values from -0.875 to 0.875
- proj_bias: bfloat16 [384], P('fsdp'), may hold values from -4 to 4
- fc1_weight: bfloat16 [384, 1536], P('fsdp'), may hold values from -0.3125 to 0.3125
- fc1_bias: bfloat16 [1536], P('fsdp'), may hold values from -4 to 4
- fc2_weight: bfloat16 [1536, 384], P('fsdp'), may hold values from -0.15625 to 0.15625
- fc2_bias: bfloat16 [384], P('fsdp'), may hold values from -4 to 4
Outputs:
- block_out: bfloat16 [2, 32, 256, 384], P(None, ('dp', 'fsdp'))
- latents_grad: bfloat16 [2, 32, 256, 384], P(None, ('dp', 'fsdp'))
- condition_grad: bfloat16 [2, 32, 384], P(None, ('dp', 'fsdp'))
- ada_weight_grad: float32 [384, 2304], P('fsdp')
- ada_bias_grad: float32 [2304], P('fsdp')
- qkv_weight_grad: float32 [384, 1152], P('fsdp')
- qv_bias_grad: float32 [768], P('fsdp')
- proj_weight_grad: float32 [384, 384], P('fsdp')
- proj_bias_grad: float32 [384], P('fsdp')
- fc1_weight_grad: float32 [384, 1536], P('fsdp')
- fc1_bias_grad: float32 [1536], P('fsdp')
- fc2_weight_grad: float32 [1536, 384], P('fsdp')
- fc2_bias_grad: float32 [384], P('fsdp')
The draws below stay inside these ranges and needn't reach their ends.
Inputs may be any that keep to these rules, and one draw needn't show every extreme that they name: `counts`: the live latents of a device in a micro-batch are its first slots; a device may have none; in every micro-batch some device has all 1 slots live.
All inputs are finite; a program needn't handle non-finite values.
Results may differ from the reference program's by a relative error of at most 0.019.
The reference program's roundings to bfloat16 on the way count: a program that leaves them out, or rounds other values in their place, can miss the bound.
Values may be sent and summed in bfloat16 or wider, within the bound.
No kernel may reach another device: no remote copies, remote signals or barrier semaphores. Data moves between devices by JAX's collectives and lax.ppermute only.
A program may use at most 64 MiB of HBM per device.

```python
import math
import jax
import jax.numpy as jnp
from jax import lax

D = 384
HEADS = 6
FF = 1536
SEQ = 256
MB = 2
LAT_SLOT = 1
LATENTS = 32


def draw_counts(key, part):
    key = jax.random.fold_in(key, 11)
    first_key, second_key = jax.random.split(key)
    device_total = LATENTS // LAT_SLOT
    drawn_counts = jax.random.randint(first_key, (MB, device_total), 0, LAT_SLOT + 1)
    fullest = jax.random.randint(second_key, (MB, 1), 0, device_total)
    places = jnp.arange(device_total, dtype=jnp.int32)[None, :]
    return jnp.where(places == fullest, LAT_SLOT, drawn_counts).astype(jnp.int32)


def levels(key, shape, cuts, low, top_value):
    gain = 1.0
    for dim, parts in cuts:
        heights = jax.random.uniform(jax.random.fold_in(jax.random.fold_in(key, 6), dim), (parts,), jnp.float32, low / len(cuts), top_value / len(cuts))
        gain = gain * jnp.repeat(jnp.exp(heights), shape[dim] // parts).reshape((-1,) + (1,) * (len(shape) - 1 - dim))
    return gain


def gaussian(stream_key, extent, scale, reach, cuts=(), kind=jnp.bfloat16):
    gain = levels(stream_key, extent, cuts, -0.22, 0.18) if cuts else 1.0
    entries = jax.random.normal(stream_key, extent, jnp.float32) * scale * gain
    return jnp.minimum(jnp.maximum(entries, -reach), reach).astype(kind)


def setup_inputs(seed: int = 0) -> dict:
    splits = jax.random.split(jax.random.key(seed), 15)
    latents = gaussian(splits[0], (MB, LATENTS, SEQ, D), 1.0, 6.0, ((1, 32),))
    condition = gaussian(splits[1], (MB, LATENTS, D), 1.0, 6.0, ((1, 32),))
    cotangent = gaussian(splits[2], (MB, LATENTS, SEQ, D), 1.0, 6.0, ((1, 32),))
    counts = draw_counts(jax.random.fold_in(splits[14], 71), 0)
    ada_weight = gaussian(splits[4], (D, 6 * D), D ** -0.5, 0.3125, ((0, 8),))
    ada_bias = gaussian(splits[5], (6 * D,), 0.3, 4.0, ((0, 8),))
    qkv_weight = gaussian(splits[6], (D, 3 * D), (D // 2) ** -0.5, 0.4375, ((0, 8),))
    qv_bias = gaussian(splits[7], (2 * D,), 0.3, 4.0, ((0, 8),))
    proj_weight = gaussian(splits[8], (D, D), (D // 8) ** -0.5, 0.875, ((0, 8),))
    proj_bias = gaussian(splits[9], (D,), 0.3, 4.0, ((0, 8),))
    fc1_weight = gaussian(splits[10], (D, FF), D ** -0.5, 0.3125, ((0, 8),))
    fc1_bias = gaussian(splits[11], (FF,), 0.3, 4.0, ((0, 8),))
    fc2_weight = gaussian(splits[12], (FF, D), FF ** -0.5, 0.15625, ((0, 8),))
    fc2_bias = gaussian(splits[13], (D,), 0.3, 4.0, ((0, 8),))
    return dict(latents=latents, condition=condition, cotangent=cotangent, counts=counts, ada_weight=ada_weight, ada_bias=ada_bias, qkv_weight=qkv_weight, qv_bias=qv_bias, proj_weight=proj_weight, proj_bias=proj_bias, fc1_weight=fc1_weight, fc1_bias=fc1_bias, fc2_weight=fc2_weight, fc2_bias=fc2_bias)


EPSILON = 1e-06
HIGH = lax.Precision.HIGHEST

@jax.custom_vjp
def low(v):
    return lax.optimization_barrier(v.astype(jnp.bfloat16)).astype(jnp.float32)

@jax.custom_vjp
def low_back(v):
    return v

def low_keep(v):
    return (low(v), None)

def low_pass(kept, grad):
    return (grad,)

def back_keep(v):
    return (v, None)

def back_low(kept, grad):
    return (low(grad),)
low.defvjp(low_keep, low_pass)
low_back.defvjp(back_keep, back_low)

def modulated(inputs, shift, scale):
    center = inputs - lax.optimization_barrier(jnp.mean(inputs, axis=-1, keepdims=True))
    spread = lax.optimization_barrier(jnp.mean(center * center, axis=-1, keepdims=True))
    return center * lax.rsqrt(spread + EPSILON) * (1.0 + scale) + shift

def block_forward(params, inputs, condition, live_slots):
    ada_weight, ada_bias, qkv_weight, qv_bias, proj_weight, proj_bias, fc1_weight, fc1_bias, fc2_weight, fc2_bias = params
    group_size, length, model_width = inputs.shape
    head_size = model_width // HEADS
    cond_act = low(jax.nn.silu(condition))
    modulation = low_back(jnp.dot(cond_act, ada_weight, precision=HIGH) + ada_bias)
    shift_attn, scale_attn, gate_attn, shift_mlp, scale_mlp, gate_mlp = jnp.split(modulation[:, None, :], 6, axis=-1)
    attn_in = low(modulated(inputs, shift_attn, scale_attn))
    full_bias = jnp.concatenate([qv_bias[:model_width], jnp.zeros((model_width,), jnp.float32), qv_bias[model_width:]])
    projected = low_back(low(jnp.einsum('gsd,de->gse', attn_in, qkv_weight, precision=HIGH) + full_bias))
    queries, key_rows, value_rows = [section.reshape(group_size, length, HEADS, head_size) for section in jnp.split(projected, 3, axis=-1)]
    scores = low_back(jnp.einsum('gqhd,gkhd->ghqk', queries, key_rows, precision=HIGH) * head_size ** (-0.5))
    probabilities = jax.nn.softmax(scores, axis=-1)
    mixed = jnp.einsum('ghqk,gkhd->gqhd', low(probabilities), value_rows, precision=HIGH)
    mixed = low_back(low(mixed)).reshape(group_size, length, model_width)
    attn_out = low_back(jnp.einsum('gsd,de->gse', mixed, proj_weight, precision=HIGH) + proj_bias)
    middle = inputs + gate_attn * attn_out
    mlp_in = low(modulated(middle, shift_mlp, scale_mlp))
    hidden_pre = low_back(jnp.einsum('gsd,df->gsf', mlp_in, fc1_weight, precision=HIGH) + fc1_bias)
    hidden_act = low(jax.nn.gelu(hidden_pre, approximate=True))
    mlp_out = low_back(jnp.einsum('gsf,fd->gsd', hidden_act, fc2_weight, precision=HIGH) + fc2_bias)
    return (middle + gate_mlp * mlp_out) * live_slots[:, None, None]

def reference(latents, condition, cotangent, counts, ada_weight, ada_bias, qkv_weight, qv_bias, proj_weight, proj_bias, fc1_weight, fc1_bias, fc2_weight, fc2_bias):
    params = tuple((weight.astype(jnp.float32) for weight in (ada_weight, ada_bias, qkv_weight, qv_bias, proj_weight, proj_bias, fc1_weight, fc1_bias, fc2_weight, fc2_bias)))
    total_slots = MB * LATENTS
    group_size = math.gcd(16, total_slots)
    group_count = total_slots // group_size
    slot_ids = jnp.arange(LATENTS, dtype=jnp.int32)
    owner_ids = slot_ids // LAT_SLOT
    live_slots = ((slot_ids % LAT_SLOT)[None, :] < counts[:, owner_ids]).astype(jnp.float32)
    live_slots = live_slots.reshape(group_count, group_size)
    input_groups = latents.astype(jnp.float32).reshape(group_count, group_size, SEQ, D)
    cond_groups = condition.astype(jnp.float32).reshape(group_count, group_size, D)
    upstream_groups = cotangent.astype(jnp.float32).reshape(group_count, group_size, SEQ, D)
    start_grads = tuple((jnp.zeros_like(param) for param in params))

    def one_group(running, group_data):
        inputs, cond_group, upstream, live_group = group_data

        def forward_only(params_in, inputs_in, condition_in):
            return block_forward(params_in, inputs_in, condition_in, live_group)
        block_value, pullback = jax.vjp(forward_only, params, inputs, cond_group)
        param_grads, input_grads, cond_grads = pullback(upstream)
        running = tuple((summed + fresh for summed, fresh in zip(running, param_grads)))
        return (running, (block_value.astype(jnp.bfloat16), input_grads.astype(jnp.bfloat16), cond_grads.astype(jnp.bfloat16)))
    summed_grads, (outputs, input_grads, cond_grads) = lax.scan(one_group, start_grads, (input_groups, cond_groups, upstream_groups, live_slots))
    return (outputs.reshape(MB, LATENTS, SEQ, D), input_grads.reshape(MB, LATENTS, SEQ, D), cond_grads.reshape(MB, LATENTS, D), summed_grads[0], summed_grads[1], summed_grads[2], summed_grads[3], summed_grads[4], summed_grads[5], summed_grads[6], summed_grads[7], summed_grads[8], summed_grads[9])
```

```python
import functools

import jax
import jax.numpy as jnp
from jax import lax
from jax.experimental import pallas as pl
from jax.experimental.pallas import tpu as pltpu
from jax.sharding import PartitionSpec as P

HEADS = 6
EPSILON = 1e-06
BF = jnp.bfloat16
F32 = jnp.float32
SQRT_2_PI = 0.7978845608028654
CUBIC = 0.044715
MOD_ROWS = 16
VMEM_BYTES = 56 * 1024 * 1024


def dot(a, b):
    return lax.dot_general(a, b, (((1,), (0,)), ((), ())), preferred_element_type=F32)


def dot_nt(a, b):
    return lax.dot_general(a, b, (((1,), (1,)), ((), ())), preferred_element_type=F32)


def dot_tn(a, b):
    return lax.dot_general(a, b, (((0,), (0,)), ((), ())), preferred_element_type=F32)


def normalize(inputs):
    center = inputs - jnp.mean(inputs, axis=-1, keepdims=True)
    spread = jnp.mean(center * center, axis=-1, keepdims=True)
    inv_root = lax.rsqrt(spread + EPSILON)
    return center * inv_root, inv_root


def norm_back(grad_norm, normed, inv_root):
    first_mean = jnp.mean(grad_norm, axis=-1, keepdims=True)
    second_mean = jnp.mean(grad_norm * normed, axis=-1, keepdims=True)
    return inv_root * (grad_norm - first_mean - normed * second_mean)


def silu(v):
    return v / (1.0 + jnp.exp(-v))


def call(body, outs, ins, scratch=(), smem=(), flops=1 << 24, moved=1 << 20):
    specs = [
        pl.BlockSpec(memory_space=pltpu.SMEM if i in smem else pltpu.VMEM) for i in range(len(ins))
    ]
    return pl.pallas_call(
        body,
        out_shape=[jax.ShapeDtypeStruct(shape, kind) for shape, kind in outs],
        in_specs=specs,
        out_specs=[pl.BlockSpec(memory_space=pltpu.VMEM)] * len(outs),
        scratch_shapes=list(scratch),
        compiler_params=pltpu.CompilerParams(vmem_limit_bytes=VMEM_BYTES),
        cost_estimate=pl.CostEstimate(flops=flops, bytes_accessed=moved, transcendentals=0),
    )(*ins)


class Plan:
    def __init__(self, latents, ada_weight, fc1_weight, fsdp, dp):
        self.fsdp, self.dp = fsdp, dp
        self.mb, self.slots, self.seq, self.d = latents.shape
        self.group = self.mb * self.slots
        self.tokens = self.group * self.seq
        self.ff = fc1_weight.shape[1]
        self.ffb = self.ff // self.d
        own = ada_weight.shape[0]
        power = fsdp >= 2 and fsdp & (fsdp - 1) == 0 and dp & (dp - 1) == 0 and dp >= 2
        self.direct = power and own % 16 == 0 and (own * 4) % (16 * dp) == 0 and self.group == 2
        self.shards = fsdp if self.direct else 1
        self.rows = own if self.direct else self.d
        self.peers = [2 * m for m in range(fsdp // 2)]


def shard_of(plan, k):
    if not plan.direct:
        return 0
    return lax.axis_index("fsdp") ^ k


def pack_body(plan, ada, qkv, proj, fc1, bias, first, second, rows_s):
    d, r = plan.d, plan.rows
    me = lax.axis_index("fsdp") if plan.direct else 0
    blocks = [qkv[:, j * d : (j + 1) * d] for j in range(3)]
    blocks += [ada[:, j * d : (j + 1) * d] for j in range(2)]
    for j, block in enumerate(blocks):
        first[j * r : (j + 1) * r, :] = block
    blocks = [fc1[:, j * d : (j + 1) * d] for j in range(plan.ffb)]
    blocks += [ada[:, j * d : (j + 1) * d] for j in range(2, 6)]
    blocks += [proj[...]]
    for j, block in enumerate(blocks):
        second[j * r : (j + 1) * r, :] = block
    rows_s[...] = jnp.zeros_like(rows_s)
    at = 0
    for row, count in ((0, 6), (1, 2), (2, 1), (3, plan.ffb), (4, 1)):
        wide = bias[:, : count * d]
        if plan.direct:
            wide = pltpu.roll(wide, me * (count * d // plan.fsdp), 1)
        for j in range(count):
            rows_s[at + j : at + j + 1, :] = wide[row : row + 1, j * d : (j + 1) * d]
        at += count
    first[5 * r : 5 * r + 16, :] = rows_s[...].astype(BF)


def place(plan, shards, block, target, column):
    d, r = plan.d, plan.rows
    for k, shard in enumerate(shards):
        at = pl.multiple_of(shard_of(plan, k) * r, 16)
        target[pl.ds(at, r), column * d : (column + 1) * d] = shard[block * r : (block + 1) * r, :]


def emit(plan, grads, blocks, send, keep, rows):
    r = plan.rows
    for name, xor in ((keep, 0),) if send is None else ((send, 1), (keep, 0)):
        for m in range(len(plan.peers) if plan.direct else 1):
            owner = shard_of(plan, 2 * m + xor)
            for at, ref, column, stride, offset in blocks:
                start = pl.multiple_of(owner * (stride * r) + offset * r, 16)
                name[m * rows + at * r : m * rows + (at + 1) * r, :] = ref[
                    pl.ds(start, r), column * plan.d : (column + 1) * plan.d
                ]


def attn_forward(plan, *refs):
    s = plan.shards
    x, cond = refs[:2]
    shards = refs[2 : 2 + s]
    projected, mixed, attn_in, modulation, bias, qkv, ada = refs[2 + s : 9 + s]
    d, length = plan.d, plan.seq
    for j in range(3):
        place(plan, shards, j, qkv, j)
    for j in range(2):
        place(plan, shards, 3 + j, ada, j)
    total = shards[0][5 * plan.rows : 5 * plan.rows + 16, :].astype(F32)
    for shard in shards[1:]:
        total = total + shard[5 * plan.rows : 5 * plan.rows + 16, :].astype(F32)
    bias[...] = total
    cond_act = silu(cond[...].astype(F32)).astype(BF)
    mod = dot(cond_act, ada[...])
    for j in range(2):
        modulation[:, j * d : (j + 1) * d] = mod[:, j * d : (j + 1) * d] + bias[j : j + 1, :]
    left = lax.broadcasted_iota(jnp.int32, (1, 128), 1) < 64

    def latent(g, carry):
        at = pl.ds(pl.multiple_of(g * length, length), length)
        shift = modulation[pl.ds(g, 1), 0:d]
        scale = modulation[pl.ds(g, 1), d : 2 * d]
        normed, _ = normalize(x[at, :].astype(F32))
        rounded = (normed * (1.0 + scale) + shift).astype(BF)
        attn_in[at, :] = rounded
        for j in range(3):
            piece = dot(rounded, qkv[:, j * d : (j + 1) * d])
            if j != 1:
                piece = piece + bias[6 + j // 2 : 7 + j // 2, :]
            projected[at, j * d : (j + 1) * d] = piece.astype(BF)
        for pair in range(HEADS // 2):
            lanes = slice(pair * 128, (pair + 1) * 128)
            q = projected[at, lanes] * jnp.asarray(0.125, BF)
            k = projected[at, d + pair * 128 : d + (pair + 1) * 128]
            v = projected[at, 2 * d + pair * 128 : 2 * d + (pair + 1) * 128]
            halves = []
            for side in (left, ~left):
                scores = dot_nt(jnp.where(side, q, jnp.zeros_like(q)), k)
                exponent = jnp.exp(scores - jnp.max(scores, axis=-1, keepdims=True))
                probs = exponent * (1.0 / jnp.sum(exponent, axis=-1, keepdims=True))
                halves.append(dot(probs.astype(BF), v))
            mixed[at, lanes] = jnp.where(left, halves[0], halves[1]).astype(BF)
        return carry

    lax.fori_loop(0, plan.group, latent, 0)


def mlp_first(plan, *refs):
    s = plan.shards
    counts, x, cond, cot, mixed, bias = refs[:6]
    shards = refs[6 : 6 + s]
    outs = refs[6 + s :]
    (send, outs) = (outs[0], outs[1:]) if plan.direct else (None, outs)
    keep, act, gelu_back, mlp_in, grad_out, middle, attn_out, modulation, fc1, ada, proj = outs[:11]
    grad_fc2 = outs[11]
    d, length, ffb = plan.d, plan.seq, plan.ffb
    for j in range(ffb):
        place(plan, shards, j, fc1, j)
    for j in range(4):
        place(plan, shards, ffb + j, ada, j)
    place(plan, shards, ffb + 4, proj, 0)
    cond_act = silu(cond[...].astype(F32)).astype(BF)
    mod = dot(cond_act, ada[...])
    for j in range(4):
        modulation[:, j * d : (j + 1) * d] = mod[:, j * d : (j + 1) * d] + bias[2 + j : 3 + j, :]

    def latent(g, carry):
        at = pl.ds(pl.multiple_of(g * length, length), length)
        gate_attn, shift, scale, gate = [
            modulation[pl.ds(g, 1), j * d : (j + 1) * d] for j in range(4)
        ]
        live = jnp.where(g % plan.slots < counts[g // plan.slots, 0], 1.0, 0.0).astype(F32)
        out = dot(mixed[at, :], proj[...]) + bias[8:9, :]
        attn_out[at, :] = out
        mid = x[at, :].astype(F32) + gate_attn * out
        middle[at, :] = mid
        normed, _ = normalize(mid)
        mlp_in[at, :] = (normed * (1.0 + scale) + shift).astype(BF)
        grad_out[at, :] = ((gate * live) * cot[at, :].astype(F32)).astype(BF)
        return carry

    lax.fori_loop(0, plan.group, latent, 0)
    step = 256
    for c in range(plan.ff // step):
        cols = slice(c * step, (c + 1) * step)
        row, lane = divmod(c * step, d)
        pieces = []
        start, rest = c * step, step
        while rest:
            row, lane = divmod(start, d)
            width = min(rest, d - lane)
            pieces.append(bias[9 + row : 10 + row, lane : lane + width])
            start, rest = start + width, rest - width
        shift = pieces[0] if len(pieces) == 1 else jnp.concatenate(pieces, axis=1)
        pre = dot(mlp_in[...], fc1[:, cols]) + shift
        square = pre * pre
        bend = jnp.tanh(pre * (SQRT_2_PI + (SQRT_2_PI * CUBIC) * square))
        half = 0.5 + 0.5 * bend
        value = (pre * half).astype(BF)
        act[:, cols] = value
        slope = (0.5 * SQRT_2_PI) + (1.5 * SQRT_2_PI * CUBIC) * square
        gelu_back[:, cols] = half + pre * (1.0 - bend * bend) * slope
        grad_fc2[cols, :] = dot_tn(value, grad_out[...]).astype(BF)
    emit(plan, None, [(j, grad_fc2, 0, 4, j) for j in range(ffb)], send, keep, ffb * plan.rows)


def mlp_second(plan, *refs):
    s = plan.shards
    grad_out, gelu_back, mlp_in = refs[:3]
    shards = refs[3 : 3 + s]
    outs = refs[3 + s :]
    (send, outs) = (outs[0], outs[1:]) if plan.direct else (None, outs)
    keep, grad_pre, fc2 = outs[:3]
    turned, grad_fc1 = outs[3:]
    r4 = plan.rows * plan.ffb
    for k, shard in enumerate(shards):
        fc2[pl.ds(pl.multiple_of(shard_of(plan, k) * r4, 16), r4), :] = shard[...]
    turned[...] = mlp_in[...].T
    step = 256
    for c in range(plan.ff // step):
        cols = slice(c * step, (c + 1) * step)
        grad = (dot_nt(grad_out[...], fc2[cols, :]) * gelu_back[:, cols]).astype(BF)
        grad_pre[:, cols] = grad
        grad_fc1[:, cols] = dot(turned[...], grad).astype(BF)
    emit(plan, None, [(j, grad_fc1, j, 1, 0) for j in range(plan.ffb)], send, keep, r4)


def mlp_back(plan, *refs):
    (counts, cot, act, fc2, grad_pre, fc1, middle, attn_out, modulation, bias, mixed, proj,
     grad_out) = refs[:13]
    block_out, grad_mixed, grad_middle, grad_proj, misc, grad_mod = refs[13:19]
    d, length = plan.d, plan.seq
    grad_gates = refs[19]
    misc[...] = jnp.zeros_like(misc)
    sums = jnp.sum(grad_pre[...].astype(F32), axis=0, keepdims=True)
    for j in range(plan.ffb):
        misc[3 + j : 4 + j, :] = sums[:, j * d : (j + 1) * d]
    misc[3 + plan.ffb : 4 + plan.ffb, :] = jnp.sum(
        grad_out[...].astype(F32), axis=0, keepdims=True
    )

    def latent(g, carry):
        at = pl.ds(pl.multiple_of(g * length, length), length)
        gate_attn, _, scale, gate = [modulation[pl.ds(g, 1), j * d : (j + 1) * d] for j in range(4)]
        live = jnp.where(g % plan.slots < counts[g // plan.slots, 0], 1.0, 0.0).astype(F32)
        upstream = cot[at, :].astype(F32) * live
        mid = middle[at, :]
        mlp_out = dot(act[at, :], fc2[...]) + bias[9 + plan.ffb : 10 + plan.ffb, :]
        block_out[at, :] = (live * (mid + gate * mlp_out)).astype(BF)
        normed, rstd = normalize(mid)
        grad_in = dot_nt(grad_pre[at, :], fc1[...])
        grad_mid = upstream + norm_back(grad_in * (1.0 + scale), normed, rstd)
        grad_middle[at, :] = grad_mid
        rounded = (gate_attn * grad_mid).astype(BF)
        grad_gates[at, :] = rounded
        grad_mixed[at, :] = dot_nt(rounded, proj[...]).astype(BF)
        pieces = [grad_mid * attn_out[at, :], grad_in, grad_in * normed, upstream * mlp_out]
        for j, piece in enumerate(pieces):
            grad_mod[pl.ds(g, 1), j * d : (j + 1) * d] = jnp.sum(piece, axis=0, keepdims=True)
        return carry

    lax.fori_loop(0, plan.group, latent, 0)
    misc[2:3, :] = jnp.sum(grad_gates[...].astype(F32), axis=0, keepdims=True)
    grad_proj[...] = dot_tn(mixed[...], grad_gates[...]).astype(BF)


def attn_back(plan, *refs):
    (x, cond, projected, grad_mixed, grad_middle, attn_in, qkv, modulation, grad_proj, misc,
     grad_mod) = refs[:11]
    outs = refs[11:]
    (send, outs) = (outs[0], outs[1:]) if plan.direct else (None, outs)
    keep, latents_grad, mods = outs[:3]
    grad_proj_in, grad_qkv, rows_s, misc_s, cond_s = outs[3:]
    d, length, r = plan.d, plan.seq, plan.rows
    left = lax.broadcasted_iota(jnp.int32, (1, 128), 1) < 64
    misc_s[...] = misc[...]
    rows_s[...] = jnp.zeros_like(rows_s)
    cond_s[...] = silu(cond[...].astype(F32))

    def latent(g, carry):
        at = pl.ds(pl.multiple_of(g * length, length), length)
        scale = modulation[pl.ds(g, 1), d : 2 * d]
        for pair in range(HEADS // 2):
            lanes = slice(pair * 128, (pair + 1) * 128)
            q = projected[at, lanes] * jnp.asarray(0.125, BF)
            k = projected[at, d + pair * 128 : d + (pair + 1) * 128]
            v = projected[at, 2 * d + pair * 128 : 2 * d + (pair + 1) * 128]
            gm = grad_mixed[at, lanes]
            grads_q, grads_k, grads_v = [], [], []
            for side in (left, ~left):
                scores = dot_nt(jnp.where(side, q, jnp.zeros_like(q)), k)
                exponent = jnp.exp(scores - jnp.max(scores, axis=-1, keepdims=True))
                probs = exponent * (1.0 / jnp.sum(exponent, axis=-1, keepdims=True))
                grad_probs = dot_nt(jnp.where(side, gm, jnp.zeros_like(gm)), v)
                inner = jnp.sum(probs * grad_probs, axis=-1, keepdims=True)
                grad_scores = (probs * (grad_probs - inner)).astype(BF)
                grads_q.append(dot(grad_scores, k))
                grads_k.append(dot_tn(grad_scores, q))
                grads_v.append(dot_tn(probs.astype(BF), gm))
            for j, (pieces, factor) in enumerate(((grads_q, 0.125), (grads_k, 1.0), (grads_v, 1.0))):
                merged = jnp.where(left, pieces[0], pieces[1]) * factor
                grad_proj_in[at, j * d + pair * 128 : j * d + (pair + 1) * 128] = merged.astype(BF)
        normed, rstd = normalize(x[at, :].astype(F32))
        grad_in = dot_nt(grad_proj_in[at, :], qkv[...])
        grad = grad_middle[at, :] + norm_back(grad_in * (1.0 + scale), normed, rstd)
        latents_grad[at, :] = grad.astype(BF)
        base = g * 7
        pieces = [cond_s[pl.ds(g, 1), :], jnp.sum(grad_in, axis=0, keepdims=True)]
        pieces += [jnp.sum(grad_in * normed, axis=0, keepdims=True)]
        pieces += [grad_mod[pl.ds(g, 1), j * d : (j + 1) * d] for j in range(4)]
        for j, piece in enumerate(pieces):
            rows_s[pl.ds(base + j, 1), :] = piece
        return carry

    lax.fori_loop(0, plan.group, latent, 0)
    mods[...] = rows_s[...].astype(BF)
    turned = attn_in[...].T
    for j in range(3):
        cols = slice(j * d, (j + 1) * d)
        grad_qkv[:, cols] = dot(turned, grad_proj_in[:, cols]).astype(BF)
        if j != 1:
            misc_s[j // 2 : j // 2 + 1, :] = jnp.sum(
                grad_proj_in[:, cols].astype(F32), axis=0, keepdims=True
            )
    blocks = [(j, grad_qkv, j, 1, 0) for j in range(3)] + [(3, grad_proj, 0, 1, 0)]
    rows = 4 * r + 16
    emit(plan, None, blocks, send, keep, rows)
    low = misc_s[...].astype(BF)
    for name in (keep,) if send is None else (send, keep):
        for m in range(len(plan.peers) if plan.direct else 1):
            name[m * rows + 4 * r : (m + 1) * rows, :] = low


def cond_back(plan, cond, mods, first, second, grad):
    d = plan.d
    rows = mods[...].astype(F32)
    total = None
    kept = []
    for g in range(plan.group):
        total = jnp.zeros((1, d), F32)
        for j in range(6):
            weight = first[:, j * d : (j + 1) * d] if j < 2 else second[:, (j - 2) * d : (j - 1) * d]
            line = jnp.broadcast_to(rows[g * 7 + 1 + j : g * 7 + 2 + j, :], (8, d)).astype(BF)
            total = total + dot_nt(line, weight)[0:1, :]
        kept.append(total)
    for g in range(plan.group):
        v = cond[g : g + 1, :].astype(F32)
        gate = 1.0 / (1.0 + jnp.exp(-v))
        grad[g : g + 1, :] = (kept[g] * (gate * (1.0 + v * (1.0 - gate)))).astype(BF)


def add_siblings(peers, rows, *refs):
    keep, received, own = refs[:3]
    outs = refs[3:]
    for m in range(peers):
        at = slice(m * rows, (m + 1) * rows)
        total = keep[at, :].astype(F32) + received[at, :].astype(F32)
        if m == 0:
            own[...] = total
        else:
            outs[m - 1][...] = total.astype(BF)


def add_chips(count, dp, quarter, own, *refs):
    received, mine, outs = refs[:count], refs[count], refs[count + 1 : count + dp]
    total_s = refs[count + dp]
    total = own[...]
    for piece in received:
        total = total + piece[...].astype(F32)
    total_s[...] = total
    me = lax.axis_index("dp")
    for j in range(dp):
        part = total_s[pl.ds(pl.multiple_of((me ^ j) * quarter, 16), quarter), :]
        if j == 0:
            mine[...] = part
        else:
            outs[j - 1][...] = part.astype(BF)


def add_groups(dp, *refs):
    total = refs[0][...]
    for piece in refs[1:dp]:
        total = total + piece[...].astype(F32)
    refs[dp][...] = total.astype(BF)


def gather_groups(dp, quarter, layout, *refs):
    pieces, outs, rows_s = refs[:dp], refs[dp:-1], refs[-1]
    me = lax.axis_index("dp")
    for j, piece in enumerate(pieces):
        rows_s[pl.ds(pl.multiple_of((me ^ j) * quarter, 16), quarter), :] = piece[...].astype(F32)
    d = rows_s.shape[1]
    at = 0
    for out, (blocks, rows) in zip(outs, layout):
        for j in range(blocks):
            out[:, j * d : (j + 1) * d] = rows_s[at : at + rows, :]
            at += rows


def last_sibling(peers, rows, *refs):
    keep, received, mods, mods_in, own = refs[:5]
    outs = refs[5:]
    for m in range(peers):
        at = slice(m * rows, (m + 1) * rows)
        total = keep[at, :].astype(F32) + received[at, :].astype(F32)
        if m == 0:
            own[0:rows, :] = total
            own[rows : rows + MOD_ROWS, :] = mods[...].astype(F32)
            own[rows + MOD_ROWS : rows + 2 * MOD_ROWS, :] = mods_in[...].astype(F32)
        else:
            outs[m - 1][0:rows, :] = total.astype(BF)
            outs[m - 1][rows : rows + MOD_ROWS, :] = mods[...]
            outs[m - 1][rows + MOD_ROWS : rows + 2 * MOD_ROWS, :] = mods_in[...]


def last_chips(count, dp, quarter, rows, own, *refs):
    received, mine, outs = refs[:count], refs[count], refs[count + 1 : count + dp]
    total_s, tail_s = refs[count + dp :]
    total = own[0 : rows, :]
    for piece in received:
        total = total + piece[0:rows, :].astype(F32)
    total_s[...] = total[: rows - 16]
    tail_s[0:16, :] = total[rows - 16 :].astype(BF)
    tail_s[16 : 16 + 2 * MOD_ROWS, :] = own[rows:, :].astype(BF)
    for i, piece in enumerate(received):
        at = 16 + (i + 1) * 2 * MOD_ROWS
        tail_s[at : at + 2 * MOD_ROWS, :] = piece[rows:, :]
    me = lax.axis_index("dp")
    for j in range(dp):
        part = total_s[pl.ds(pl.multiple_of((me ^ j) * quarter, 16), quarter), :]
        name = mine if j == 0 else outs[j - 1]
        name[0:quarter, :] = part.astype(name.dtype)
        name[quarter:, :] = tail_s[...].astype(name.dtype)


def last_groups(dp, quarter, *refs):
    pieces, low = refs[:dp], refs[dp]
    total = pieces[0][0:quarter, :]
    for piece in pieces[1:]:
        total = total + piece[0:quarter, :].astype(F32)
    low[...] = total.astype(BF)


def ada_grads(plan, quarter, *refs):
    dp, d, r = plan.dp, plan.d, plan.rows
    pieces = refs[:dp]
    ada, ada_bias, qv, proj, fc1, fc2 = refs[dp : dp + 6]
    rows_s, turned_s = refs[dp + 6 :]
    each = plan.fsdp * MOD_ROWS
    total = pieces[0][quarter : quarter + 16, :].astype(F32)
    for piece in pieces[1:]:
        total = total + piece[quarter : quarter + 16, :].astype(F32)
    for j, piece in enumerate(pieces):
        rows_s[j * each : (j + 1) * each, :] = piece[quarter + 16 :, :].astype(BF)
    count = dp * each
    row = lax.broadcasted_iota(jnp.int32, (count, count), 0)
    column = lax.broadcasted_iota(jnp.int32, (count, count), 1)
    slot = row % MOD_ROWS
    source = row - slot + jnp.where(slot >= 7, 7, 0)
    pick = ((column == source) & (slot < 14)).astype(BF)
    turned_s[...] = dot(pick, rows_s[...]).T
    me = lax.axis_index("fsdp")
    mine = turned_s[pl.ds(pl.multiple_of(me * r, 16), r), :].astype(BF)
    lane = lax.broadcasted_iota(jnp.int32, (1, count), 1) % MOD_ROWS
    tall = lax.broadcasted_iota(jnp.int32, (count, 1), 0) % MOD_ROWS
    values = rows_s[...]
    sums = []
    for j in range(6):
        here = (lane == 1 + j) | (lane == 8 + j)
        ada[:, j * d : (j + 1) * d] = dot(jnp.where(here, mine, jnp.zeros_like(mine)), values)
        there = (tall == 1 + j) | (tall == 8 + j)
        sums.append(
            jnp.sum(jnp.where(there, values.astype(F32), 0.0), axis=0, keepdims=True)
        )
    lists = [
        (ada_bias, sums),
        (qv, [total[0:1], total[1:2]]),
        (proj, [total[2:3]]),
        (fc1, [total[3 + j : 4 + j] for j in range(plan.ffb)]),
        (fc2, [total[3 + plan.ffb : 4 + plan.ffb]]),
    ]
    for out, lines in lists:
        wide = lines[0] if len(lines) == 1 else jnp.concatenate(lines, axis=1)
        width = wide.shape[1]
        own = width // plan.fsdp
        wide = jnp.broadcast_to(wide, (8, width))
        wide = pltpu.roll(wide, lax.rem(width - me * own, width), 1)
        out[...] = wide[0:1, :own]


def swap(plan, value, k, axis="fsdp"):
    size = plan.fsdp if axis == "fsdp" else plan.dp
    return lax.ppermute(value, axis, [(i, i ^ k) for i in range(size)])


def gather_shards(plan, value):
    if not plan.direct:
        return [value]
    chips = [value] + [swap(plan, value, k) for k in plan.peers[1:]]
    cores = [swap(plan, shard, 1) for shard in chips]
    return [shard for pair in zip(chips, cores) for shard in pair]


def reduce_chunk(plan, send, keep, layout):
    d, dp, peers = plan.d, plan.dp, len(plan.peers)
    rows = keep.shape[0] // peers
    quarter = rows // dp
    received = swap(plan, send, 1)
    own, *pieces = call(
        functools.partial(add_siblings, peers, rows),
        [((rows, d), F32)] + [((rows, d), BF)] * (peers - 1),
        [keep, received],
    )
    pieces = [swap(plan, piece, k) for piece, k in zip(pieces, plan.peers[1:])]
    mine, *quarters = call(
        functools.partial(add_chips, peers - 1, dp, quarter),
        [((quarter, d), F32)] + [((quarter, d), BF)] * (dp - 1),
        [own] + pieces,
        [pltpu.VMEM((rows, d), F32)],
    )
    quarters = [swap(plan, part, j + 1, "dp") for j, part in enumerate(quarters)]
    (low,) = call(functools.partial(add_groups, dp), [((quarter, d), BF)], [mine] + quarters)
    parts = [low] + [swap(plan, low, j, "dp") for j in range(1, dp)]
    return call(
        functools.partial(gather_groups, dp, quarter, layout),
        [((height, blocks * d), F32) for blocks, height in layout],
        parts,
        [pltpu.VMEM((rows, d), F32)],
    )


def reduce_last(plan, send, keep, mods):
    d, dp, peers, r = plan.d, plan.dp, len(plan.peers), plan.rows
    rows = keep.shape[0] // peers
    quarter = (rows - 16) // dp
    received, mods_in = swap(plan, send, 1), swap(plan, mods, 1)
    long = rows + 2 * MOD_ROWS
    own, *pieces = call(
        functools.partial(last_sibling, peers, rows),
        [((long, d), F32)] + [((long, d), BF)] * (peers - 1),
        [keep, received, mods, mods_in],
    )
    pieces = [swap(plan, piece, k) for piece, k in zip(pieces, plan.peers[1:])]
    tail = 16 + plan.fsdp * MOD_ROWS
    mine, *quarters = call(
        functools.partial(last_chips, peers - 1, dp, quarter, rows),
        [((quarter + tail, d), F32)] + [((quarter + tail, d), BF)] * (dp - 1),
        [own] + pieces,
        [pltpu.VMEM((rows - 16, d), F32), pltpu.VMEM((tail, d), BF)],
    )
    quarters = [swap(plan, part, j + 1, "dp") for j, part in enumerate(quarters)]
    (low,) = call(functools.partial(last_groups, dp, quarter), [((quarter, d), BF)], [mine] + quarters)
    parts = [low] + [swap(plan, low, j, "dp") for j in range(1, dp)]
    widths = [6, 2, 1, plan.ffb, 1]
    ada, *biases = call(
        functools.partial(ada_grads, plan, quarter),
        [((r, 6 * d), F32)] + [((1, w * d // plan.fsdp), F32) for w in widths],
        [mine] + quarters,
        [
            pltpu.VMEM((dp * plan.fsdp * MOD_ROWS, d), BF),
            pltpu.VMEM((d, dp * plan.fsdp * MOD_ROWS), F32),
        ],
    )
    qkv, proj = call(
        functools.partial(gather_groups, dp, quarter, ((3, r), (1, r))),
        [((r, 3 * d), F32), ((r, d), F32)],
        parts,
        [pltpu.VMEM((rows - 16, d), F32)],
    )
    return qkv, proj, ada, [bias.reshape(-1) for bias in biases]


def reduce_whole(plan, fc2_rows, fc1_rows, last, mods):
    d, ffb = plan.d, plan.ffb

    def unpack(rows, blocks):
        return rows.reshape(blocks, d, d).transpose(1, 0, 2).reshape(d, blocks * d)

    mods = mods[: 7 * plan.group].reshape(plan.group, 7, d)
    cond_act, grad_mod = mods[:, 0], mods[:, 1:].reshape(plan.group, 6 * d)
    ada = jnp.dot(cond_act.T, grad_mod, preferred_element_type=F32)
    misc = last[4 * d : 4 * d + 16]
    grads = (
        ada,
        jnp.sum(grad_mod.astype(F32), axis=0),
        unpack(last[: 3 * d], 3),
        misc[0:2].reshape(-1),
        last[3 * d : 4 * d],
        misc[2],
        unpack(fc1_rows, ffb),
        misc[3 : 3 + ffb].reshape(-1),
        fc2_rows,
        misc[3 + ffb],
    )
    owned = [
        lax.psum_scatter(grad.astype(BF), "fsdp", scatter_dimension=0, tiled=True) for grad in grads
    ]
    return [lax.psum(grad, "dp").astype(F32) for grad in owned]


def shards(
    fsdp,
    dp,
    latents,
    condition,
    cotangent,
    counts,
    ada_weight,
    ada_bias,
    qkv_weight,
    qv_bias,
    proj_weight,
    proj_bias,
    fc1_weight,
    fc1_bias,
    fc2_weight,
    fc2_bias,
):
    plan = Plan(latents, ada_weight, fc1_weight, fsdp, dp)
    d, n, group, ff, r = plan.d, plan.tokens, plan.group, plan.ff, plan.rows
    x = latents.reshape(n, d)
    cot = cotangent.reshape(n, d)
    cond = condition.reshape(group, d)
    biases = [ada_bias, qv_bias, proj_bias, fc1_bias, fc2_bias]
    weights = [ada_weight, qkv_weight, proj_weight, fc1_weight]
    third = fc2_weight
    if not plan.direct:
        def whole(v):
            return lax.all_gather(v, "fsdp", axis=0, tiled=True)

        biases, weights, third = [whole(v) for v in biases], [whole(v) for v in weights], whole(third)
    rows = [jnp.pad(bias.astype(F32), (0, 6 * d - bias.shape[0])) for bias in biases]
    rows = jnp.stack(rows + [jnp.zeros_like(rows[0])] * 3)
    first, second = call(
        functools.partial(pack_body, plan),
        [((5 * r + 16, d), BF), (((plan.ffb + 5) * r, d), BF)],
        weights + [rows],
        [pltpu.VMEM((16, d), F32)],
    )
    first, second, third = [gather_shards(plan, v) for v in (first, second, third)]

    projected, mixed, attn_in, mod_first, bias, qkv, ada_first = call(
        functools.partial(attn_forward, plan),
        [
            ((n, 3 * d), BF),
            ((n, d), BF),
            ((n, d), BF),
            ((group, 2 * d), F32),
            ((16, d), F32),
            ((d, 3 * d), BF),
            ((d, 2 * d), BF),
        ],
        [x, cond] + first,
        flops=1 << 30,
        moved=1 << 24,
    )
    halves = len(plan.peers) if plan.direct else 1
    sides = 2 if plan.direct else 1
    outs = call(
        functools.partial(mlp_first, plan),
        [((halves * plan.ffb * r, d), BF)] * sides
        + [
            ((n, ff), BF),
            ((n, ff), F32),
            ((n, d), BF),
            ((n, d), BF),
            ((n, d), F32),
            ((n, d), F32),
            ((group, 4 * d), F32),
            ((d, ff), BF),
            ((d, 4 * d), BF),
            ((d, d), BF),
        ],
        [counts, x, cond, cot, mixed, bias] + second,
        [pltpu.VMEM((ff, d), BF)],
        smem=(0,),
        flops=1 << 30,
        moved=1 << 24,
    )
    fc2_chunk = outs[:sides]
    act, gelu_back, mlp_in, grad_out, middle, attn_out, mod_second, fc1, ada_second, proj = outs[sides:]
    outs = call(
        functools.partial(mlp_second, plan),
        [((halves * plan.ffb * r, d), BF)] * sides + [((n, ff), BF), ((ff, d), BF)],
        [grad_out, gelu_back, mlp_in] + third,
        [pltpu.VMEM((d, n), BF), pltpu.VMEM((d, ff), BF)],
        flops=1 << 30,
        moved=1 << 24,
    )
    fc1_chunk = outs[:sides]
    grad_pre, fc2 = outs[sides:]
    block_out, grad_mixed, grad_middle, grad_proj, misc, grad_mod = call(
        functools.partial(mlp_back, plan),
        [
            ((n, d), BF),
            ((n, d), BF),
            ((n, d), F32),
            ((d, d), BF),
            ((16, d), F32),
            ((group, 4 * d), F32),
        ],
        [counts, cot, act, fc2, grad_pre, fc1, middle, attn_out, mod_second, bias, mixed, proj, grad_out],
        [pltpu.VMEM((n, d), BF)],
        smem=(0,),
        flops=1 << 30,
        moved=1 << 24,
    )
    outs = call(
        functools.partial(attn_back, plan),
        [((halves * (4 * r + 16), d), BF)] * sides + [((n, d), BF), ((MOD_ROWS, d), BF)],
        [x, cond, projected, grad_mixed, grad_middle, attn_in, qkv, mod_first, grad_proj, misc, grad_mod],
        [
            pltpu.VMEM((n, 3 * d), BF),
            pltpu.VMEM((d, 3 * d), BF),
            pltpu.VMEM((MOD_ROWS, d), F32),
            pltpu.VMEM((16, d), F32),
            pltpu.VMEM((group, d), F32),
        ],
        flops=1 << 30,
        moved=1 << 24,
    )
    last_chunk = outs[:sides]
    latents_grad, mods = outs[sides:]
    (cond_grad,) = call(
        functools.partial(cond_back, plan), [((group, d), BF)], [cond, mods, ada_first, ada_second]
    )
    if plan.direct:
        (fc2_grad,) = reduce_chunk(plan, *fc2_chunk, ((1, plan.ffb * r),))
        (fc1_grad,) = reduce_chunk(plan, *fc1_chunk, ((plan.ffb, r),))
        qkv_grad, proj_grad, ada_grad, bias_grads = reduce_last(plan, *last_chunk, mods)
        weight_grads = [ada_grad, qkv_grad, proj_grad, fc1_grad, fc2_grad]
        grads = [grad for pair in zip(weight_grads, bias_grads) for grad in pair]
    else:
        grads = reduce_whole(plan, fc2_chunk[0], fc1_chunk[0], last_chunk[0], mods)
    return (
        block_out.reshape(latents.shape),
        latents_grad.reshape(latents.shape),
        cond_grad.reshape(condition.shape),
        *grads,
    )


def solution(mesh):
    tokens = P(None, ("dp", "fsdp"), None, None)
    per_latent = P(None, ("dp", "fsdp"), None)
    weight, bias = P("fsdp", None), P("fsdp")
    in_specs = (tokens, per_latent, tokens, P(None, ("dp", "fsdp"))) + (weight, bias) * 5
    out_specs = (tokens, tokens, per_latent) + (weight, bias) * 5
    body = functools.partial(shards, mesh.shape["fsdp"], mesh.shape["dp"])
    return jax.shard_map(body, mesh=mesh, in_specs=in_specs, out_specs=out_specs, check_vma=False)
```

```python
import functools
import math

import jax
import jax.numpy as jnp
from jax import lax
from jax.experimental import pallas as pl
from jax.experimental.pallas import tpu as pltpu
from jax.sharding import PartitionSpec as P

HEADS = 6
EPSILON = 1e-06
BF = jnp.bfloat16
F32 = jnp.float32
SQRT_2_PI = 0.7978845608028654
CUBIC = 0.044715
MARGIN = 0.25
PACK_LIMIT = 56 * 1024 * 1024
MOD_ROWS = 16


def dot(a, b):
    return lax.dot_general(a, b, (((1,), (0,)), ((), ())), preferred_element_type=F32)


def dot_nt(a, b):
    return lax.dot_general(a, b, (((1,), (1,)), ((), ())), preferred_element_type=F32)


def dot_tn(a, b):
    return lax.dot_general(a, b, (((0,), (0,)), ((), ())), preferred_element_type=F32)


def normalize(inputs):
    center = inputs - jnp.mean(inputs, axis=-1, keepdims=True)
    spread = jnp.mean(center * center, axis=-1, keepdims=True)
    inv_root = lax.rsqrt(spread + EPSILON)
    return center * inv_root, inv_root


def norm_back(grad_norm, normed, inv_root):
    first_mean = jnp.mean(grad_norm, axis=-1, keepdims=True)
    second_mean = jnp.mean(grad_norm * normed, axis=-1, keepdims=True)
    return inv_root * (grad_norm - first_mean - normed * second_mean)


def silu(v):
    return v / (1.0 + jnp.exp(-v))


def call(body, outs, ins, scratch=(), smem=(), far=(), far_outs=(), room=2, micros=0.2, limit=0):
    specs = [
        pl.BlockSpec(
            memory_space=pltpu.SMEM if i in smem else pltpu.HBM if i in far else pltpu.VMEM
        )
        for i in range(len(ins))
    ]
    def size(shape, kind):
        width = -(-shape[-1] // 128) * 128
        return math.prod(shape[:-1]) * width * jnp.dtype(kind).itemsize

    held = sum(size(v.shape, v.dtype) for v in scratch if len(v.shape) > 1)
    held += MARGIN * (sum(size(v.shape, v.dtype) for v in ins) + sum(size(*out) for out in outs))
    return pl.pallas_call(
        body,
        out_shape=[jax.ShapeDtypeStruct(shape, kind) for shape, kind in outs],
        in_specs=specs,
        out_specs=[
            pl.BlockSpec(memory_space=pltpu.HBM if i in far_outs else pltpu.VMEM)
            for i in range(len(outs))
        ],
        scratch_shapes=list(scratch),
        compiler_params=pltpu.CompilerParams(vmem_limit_bytes=limit or int(held) + room * 1024 * 1024),
        cost_estimate=pl.CostEstimate(
            flops=0, bytes_accessed=int(micros * 3.69e6), transcendentals=0
        ),
    )(*ins)


class Plan:
    def __init__(self, latents, ada_weight, fc1_weight, fsdp, dp):
        self.fsdp, self.dp = fsdp, dp
        self.mb, self.slots, self.seq, self.d = latents.shape
        self.group = self.mb * self.slots
        self.tokens = self.group * self.seq
        self.ff = fc1_weight.shape[1]
        self.ffb = self.ff // self.d
        own = ada_weight.shape[0]
        power = fsdp >= 2 and fsdp & (fsdp - 1) == 0 and dp & (dp - 1) == 0 and dp >= 2
        self.direct = power and own % 16 == 0 and (own * 4) % (16 * dp) == 0 and self.group == 2
        self.shards = fsdp if self.direct else 1
        self.rows = own if self.direct else self.d
        self.peers = [2 * m for m in range(fsdp // 2)]
        self.sides = 2 if self.direct else 1
        self.bias_rows = [6, 2, 1, self.ffb, 1]


def shard_of(plan, k):
    if not plan.direct:
        return 0
    return lax.axis_index("fsdp") ^ k


def pack_weights(plan, ada, qkv, proj, fc1, fc2, biases, first, second, rows_s, sems):
    d, r = plan.d, plan.rows

    def cut(ref, start, stop):
        return [ref.at[:, pl.ds(j * d, d)] for j in range(start, stop)]

    copies = []
    for packed, blocks in (
        (first, cut(qkv, 0, 3) + cut(ada, 0, 2)),
        (second, cut(fc1, 0, plan.ffb) + cut(ada, 2, 6) + [proj, fc2]),
    ):
        at = 0
        for block in blocks:
            target = packed.at[pl.ds(at, block.shape[0]), :]
            copies.append(pltpu.make_async_copy(block, target, sems.at[len(copies)]))
            at += block.shape[0]
    for copy in copies:
        copy.start()
    rows_s[...] = jnp.zeros_like(rows_s)
    line = jnp.broadcast_to(biases[...], (8, biases.shape[1]))
    at, start = 0, 0
    for count in plan.bias_rows:
        width = max(count * d, line.shape[1])
        wide = line
        if width > line.shape[1]:
            wide = jnp.concatenate([line, jnp.zeros((8, width - line.shape[1]), F32)], axis=1)
        if plan.direct:
            own = count * d // plan.fsdp
            me = lax.axis_index("fsdp")
            wide = pltpu.roll(wide, lax.rem(me * own + (width - start), width), 1)
            lane = lax.broadcasted_iota(jnp.int32, (8, width), 1)
            wide = jnp.where((lane >= me * own) & (lane < (me + 1) * own), wide, 0.0)
            start += own
        else:
            wide = line[:, start : start + count * d]
            start += count * d
        for j in range(count):
            rows_s[at + j : at + j + 1, :] = wide[0:1, j * d : (j + 1) * d]
        at += count
    first[5 * r : 5 * r + 16, :] = rows_s[...].astype(BF)
    for copy in copies:
        copy.wait()


def join(count, gate, *refs):
    del gate
    out = refs[count]
    rows = refs[0].shape[0]
    for m, shard in enumerate(refs[:count]):
        out[m * rows : (m + 1) * rows, :] = shard[...]


def views(plan, joined):
    count = plan.shards // len(joined)
    rows = joined[0].shape[0] // count
    return [ref.at[pl.ds(m * rows, rows), :] for m in range(count) for ref in joined]


def place(plan, shards, block, target, column):
    d, r = plan.d, plan.rows
    for k, shard in enumerate(shards):
        at = pl.multiple_of(shard_of(plan, k) * r, 16)
        target[pl.ds(at, r), column * d : (column + 1) * d] = shard[block * r : (block + 1) * r, :]


def emit(plan, grads, blocks, send, keep, rows):
    r = plan.rows
    for name, xor in ((keep, 0),) if send is None else ((send, 1), (keep, 0)):
        for m in range(len(plan.peers) if plan.direct else 1):
            owner = shard_of(plan, 2 * m + xor)
            for at, ref, column, stride, offset in blocks:
                start = pl.multiple_of(owner * (stride * r) + offset * r, 16)
                name[m * rows + at * r : m * rows + (at + 1) * r, :] = ref[
                    pl.ds(start, r), column * plan.d : (column + 1) * plan.d
                ]


def attn_forward(plan, *refs):
    s = plan.shards
    x, cond = refs[:2]
    shards = refs[2 : 2 + s]
    projected, mixed, modulation, bias, qkv_out, ada_out, qkv, ada, sems = refs[2 + s :]
    d, length, r = plan.d, plan.seq, plan.rows
    for j in range(3):
        place(plan, shards, j, qkv, j)
    for j in range(2):
        place(plan, shards, 3 + j, ada, j)
    copies = [
        pltpu.make_async_copy(qkv, qkv_out, sems.at[0]),
        pltpu.make_async_copy(ada, ada_out, sems.at[1]),
    ]
    for copy in copies:
        copy.start()
    total = shards[0][5 * r : 5 * r + 16, :].astype(F32)
    for shard in shards[1:]:
        total = total + shard[5 * r : 5 * r + 16, :].astype(F32)
    bias[...] = total
    cond_act = silu(cond[...].astype(F32)).astype(BF)
    mod = dot(cond_act, ada[...])
    for j in range(2):
        modulation[:, j * d : (j + 1) * d] = mod[:, j * d : (j + 1) * d] + bias[j : j + 1, :]
    left = lax.broadcasted_iota(jnp.int32, (1, 128), 1) < 64

    def latent(g, carry):
        at = pl.ds(pl.multiple_of(g * length, length), length)
        shift = modulation[pl.ds(g, 1), 0:d]
        scale = modulation[pl.ds(g, 1), d : 2 * d]
        normed, _ = normalize(x[at, :].astype(F32))
        rounded = (normed * (1.0 + scale) + shift).astype(BF)
        for j in range(3):
            piece = dot(rounded, qkv[:, j * d : (j + 1) * d])
            if j != 1:
                piece = piece + bias[6 + j // 2 : 7 + j // 2, :]
            projected[at, j * d : (j + 1) * d] = piece.astype(BF)
        for pair in range(HEADS // 2):
            lanes = slice(pair * 128, (pair + 1) * 128)
            q = projected[at, lanes] * jnp.asarray(0.125, BF)
            k = projected[at, d + pair * 128 : d + (pair + 1) * 128]
            v = projected[at, 2 * d + pair * 128 : 2 * d + (pair + 1) * 128]
            halves = []
            for side in (left, ~left):
                scores = dot_nt(jnp.where(side, q, jnp.zeros_like(q)), k)
                exponent = jnp.exp(scores - jnp.max(scores, axis=-1, keepdims=True))
                probs = exponent * (1.0 / jnp.sum(exponent, axis=-1, keepdims=True))
                halves.append(dot(probs.astype(BF), v))
            mixed[at, lanes] = jnp.where(left, halves[0], halves[1]).astype(BF)
        return carry

    lax.fori_loop(0, plan.group, latent, 0)
    for copy in copies:
        copy.wait()


def mlp_first(plan, *refs):
    s = plan.sides
    counts, x, cond, cot, mixed, bias = refs[:6]
    shards = views(plan, refs[6 : 6 + s])
    (act, gelu_back, mlp_in, grad_out, middle, attn_out, modulation, fc1, ada_out, proj, grad_fc2,
     fc2, ada, sems) = refs[6 + s :]
    d, length, ffb = plan.d, plan.seq, plan.ffb
    for j in range(ffb):
        place(plan, shards, j, fc1, j)
    for j in range(4):
        place(plan, shards, ffb + j, ada, j)
    copy = pltpu.make_async_copy(ada, ada_out, sems.at[0])
    copy.start()
    place(plan, shards, ffb + 4, proj, 0)
    r, r4 = plan.rows, plan.rows * ffb
    for k, shard in enumerate(shards):
        at = pl.multiple_of(shard_of(plan, k) * r4, 16)
        fc2[pl.ds(at, r4), :] = shard[(ffb + 5) * r : (ffb + 5) * r + r4, :]
    cond_act = silu(cond[...].astype(F32)).astype(BF)
    mod = dot(cond_act, ada[...])
    for j in range(4):
        modulation[:, j * d : (j + 1) * d] = mod[:, j * d : (j + 1) * d] + bias[2 + j : 3 + j, :]

    def latent(g, carry):
        at = pl.ds(pl.multiple_of(g * length, length), length)
        gate_attn, shift, scale, gate = [
            modulation[pl.ds(g, 1), j * d : (j + 1) * d] for j in range(4)
        ]
        live = jnp.where(g % plan.slots < counts[g // plan.slots, 0], 1.0, 0.0).astype(F32)
        out = dot(mixed[at, :], proj[...]) + bias[8:9, :]
        attn_out[at, :] = out
        mid = x[at, :].astype(F32) + gate_attn * out
        middle[at, :] = mid
        normed, _ = normalize(mid)
        mlp_in[at, :] = (normed * (1.0 + scale) + shift).astype(BF)
        grad_out[at, :] = ((gate * live) * cot[at, :].astype(F32)).astype(BF)
        return carry

    lax.fori_loop(0, plan.group, latent, 0)
    step = 256
    for c in range(plan.ff // step):
        cols = slice(c * step, (c + 1) * step)
        row, lane = divmod(c * step, d)
        pieces = []
        start, rest = c * step, step
        while rest:
            row, lane = divmod(start, d)
            width = min(rest, d - lane)
            pieces.append(bias[9 + row : 10 + row, lane : lane + width])
            start, rest = start + width, rest - width
        shift = pieces[0] if len(pieces) == 1 else jnp.concatenate(pieces, axis=1)
        pre = dot(mlp_in[...], fc1[:, cols]) + shift
        square = pre * pre
        bend = jnp.tanh(pre * (SQRT_2_PI + (SQRT_2_PI * CUBIC) * square))
        half = 0.5 + 0.5 * bend
        value = (pre * half).astype(BF)
        act[:, cols] = value
        slope = (0.5 * SQRT_2_PI) + (1.5 * SQRT_2_PI * CUBIC) * square
        gelu_back[:, cols] = half + pre * (1.0 - bend * bend) * slope
        grad_fc2[cols, :] = dot_tn(value, grad_out[...]).astype(BF)
    copy.wait()


def mlp_second(plan, *refs):
    grad_out, gelu_back, mlp_in, grad_fc2, fc2 = refs[:5]
    outs = refs[5:]
    (send, outs) = (outs[0], outs[1:]) if plan.direct else (None, outs)
    keep, grad_pre, turned, grad_fc1 = outs
    r4 = plan.rows * plan.ffb
    turned[...] = mlp_in[...].T
    step = 256
    for c in range(plan.ff // step):
        cols = slice(c * step, (c + 1) * step)
        grad = (dot_nt(grad_out[...], fc2[cols, :]) * gelu_back[:, cols]).astype(BF)
        grad_pre[:, cols] = grad
        grad_fc1[:, cols] = dot(turned[...], grad).astype(BF)
    blocks = [(j, grad_fc1, j, 1, 0) for j in range(plan.ffb)]
    blocks += [(plan.ffb + j, grad_fc2, 0, plan.ffb, j) for j in range(plan.ffb)]
    emit(plan, None, blocks, send, keep, 2 * r4)


def mlp_close(plan, counts, cot, act, fc2, middle, modulation, bias, block_out, grad_gate):
    d, length = plan.d, plan.seq

    def latent(g, carry):
        at = pl.ds(pl.multiple_of(g * length, length), length)
        gate = modulation[pl.ds(g, 1), 3 * d : 4 * d]
        live = jnp.where(g % plan.slots < counts[g // plan.slots, 0], 1.0, 0.0).astype(F32)
        mlp_out = dot(act[at, :], fc2[...]) + bias[9 + plan.ffb : 10 + plan.ffb, :]
        block_out[at, :] = (live * (middle[at, :] + gate * mlp_out)).astype(BF)
        upstream = cot[at, :].astype(F32) * live
        grad_gate[pl.ds(g, 1), :] = jnp.sum(upstream * mlp_out, axis=0, keepdims=True)
        return carry

    lax.fori_loop(0, plan.group, latent, 0)


def mlp_back(plan, counts, cot, grad_pre, fc1, middle, attn_out, modulation, mixed, proj, grad_out,
             grad_mixed, grad_middle, grad_proj, misc, grad_mod, grad_gates):
    d, length = plan.d, plan.seq
    misc[...] = jnp.zeros_like(misc)
    sums = jnp.sum(grad_pre[...].astype(F32), axis=0, keepdims=True)
    for j in range(plan.ffb):
        misc[3 + j : 4 + j, :] = sums[:, j * d : (j + 1) * d]
    misc[3 + plan.ffb : 4 + plan.ffb, :] = jnp.sum(
        grad_out[...].astype(F32), axis=0, keepdims=True
    )

    def latent(g, carry):
        at = pl.ds(pl.multiple_of(g * length, length), length)
        gate_attn, _, scale = [modulation[pl.ds(g, 1), j * d : (j + 1) * d] for j in range(3)]
        live = jnp.where(g % plan.slots < counts[g // plan.slots, 0], 1.0, 0.0).astype(F32)
        upstream = cot[at, :].astype(F32) * live
        normed, rstd = normalize(middle[at, :])
        grad_in = dot_nt(grad_pre[at, :], fc1[...])
        grad_mid = upstream + norm_back(grad_in * (1.0 + scale), normed, rstd)
        grad_middle[at, :] = grad_mid
        rounded = (gate_attn * grad_mid).astype(BF)
        grad_gates[at, :] = rounded
        grad_mixed[at, :] = dot_nt(rounded, proj[...]).astype(BF)
        pieces = [grad_mid * attn_out[at, :], grad_in, grad_in * normed]
        for j, piece in enumerate(pieces):
            grad_mod[pl.ds(g, 1), j * d : (j + 1) * d] = jnp.sum(piece, axis=0, keepdims=True)
        return carry

    lax.fori_loop(0, plan.group, latent, 0)
    misc[2:3, :] = jnp.sum(grad_gates[...].astype(F32), axis=0, keepdims=True)
    grad_proj[...] = dot_tn(mixed[...], grad_gates[...]).astype(BF)


def attn_core_back(plan, at, projected, grad_mixed, out, where):
    d = plan.d
    left = lax.broadcasted_iota(jnp.int32, (1, 128), 1) < 64
    for pair in range(HEADS // 2):
        lanes = slice(pair * 128, (pair + 1) * 128)
        q = projected[at, lanes] * jnp.asarray(0.125, BF)
        k = projected[at, d + pair * 128 : d + (pair + 1) * 128]
        v = projected[at, 2 * d + pair * 128 : 2 * d + (pair + 1) * 128]
        gm = grad_mixed[at, lanes]
        grads_q, grads_k, grads_v = [], [], []
        for side in (left, ~left):
            scores = dot_nt(jnp.where(side, q, jnp.zeros_like(q)), k)
            exponent = jnp.exp(scores - jnp.max(scores, axis=-1, keepdims=True))
            probs = exponent * (1.0 / jnp.sum(exponent, axis=-1, keepdims=True))
            grad_probs = dot_nt(jnp.where(side, gm, jnp.zeros_like(gm)), v)
            inner = jnp.sum(probs * grad_probs, axis=-1, keepdims=True)
            grad_scores = (probs * (grad_probs - inner)).astype(BF)
            grads_q.append(dot(grad_scores, k))
            grads_k.append(dot_tn(grad_scores, q))
            grads_v.append(dot_tn(probs.astype(BF), gm))
        for j, (pieces, factor) in enumerate(((grads_q, 0.125), (grads_k, 1.0), (grads_v, 1.0))):
            merged = jnp.where(left, pieces[0], pieces[1]) * factor
            out[where, j * d + pair * 128 : j * d + (pair + 1) * 128] = merged.astype(BF)


def attn_back(plan, g, projected, grad_mixed, out):
    at = slice(g * plan.seq, (g + 1) * plan.seq)
    attn_core_back(plan, at, projected, grad_mixed, out, slice(0, plan.seq))


def attn_close(plan, *refs):
    (x, cond, grad_middle, qkv, modulation, grad_proj, misc, grad_mod,
     grad_gate) = refs[:9]
    parts, outs = refs[9 : 9 + plan.group], refs[9 + plan.group :]
    (send, outs) = (outs[0], outs[1:]) if plan.direct else (None, outs)
    keep, latents_grad, mods = outs[:3]
    grad_proj_in, grad_qkv, rows_s, misc_s, cond_s, attn_in = outs[3:]
    d, length, r = plan.d, plan.seq, plan.rows
    misc_s[...] = misc[...]
    rows_s[...] = jnp.zeros_like(rows_s)
    cond_s[...] = silu(cond[...].astype(F32))
    for g, part in enumerate(parts):
        grad_proj_in[g * length : (g + 1) * length, :] = part[...]

    def latent(g, carry):
        at = pl.ds(pl.multiple_of(g * length, length), length)
        shift = modulation[pl.ds(g, 1), 0:d]
        scale = modulation[pl.ds(g, 1), d : 2 * d]
        normed, rstd = normalize(x[at, :].astype(F32))
        attn_in[at, :] = (normed * (1.0 + scale) + shift).astype(BF)
        grad_in = dot_nt(grad_proj_in[at, :], qkv[...])
        grad = grad_middle[at, :] + norm_back(grad_in * (1.0 + scale), normed, rstd)
        latents_grad[at, :] = grad.astype(BF)
        base = g * 7
        pieces = [cond_s[pl.ds(g, 1), :], jnp.sum(grad_in, axis=0, keepdims=True)]
        pieces += [jnp.sum(grad_in * normed, axis=0, keepdims=True)]
        pieces += [grad_mod[pl.ds(g, 1), j * d : (j + 1) * d] for j in range(3)]
        pieces += [grad_gate[pl.ds(g, 1), :]]
        for j, piece in enumerate(pieces):
            rows_s[pl.ds(base + j, 1), :] = piece
        return carry

    lax.fori_loop(0, plan.group, latent, 0)
    mods[...] = rows_s[...].astype(BF)
    turned = attn_in[...].T
    for j in range(3):
        cols = slice(j * d, (j + 1) * d)
        grad_qkv[:, cols] = dot(turned, grad_proj_in[:, cols]).astype(BF)
        if j != 1:
            misc_s[j // 2 : j // 2 + 1, :] = jnp.sum(
                grad_proj_in[:, cols].astype(F32), axis=0, keepdims=True
            )
    blocks = [(j, grad_qkv, j, 1, 0) for j in range(3)] + [(3, grad_proj, 0, 1, 0)]
    rows = 4 * r + 16
    emit(plan, None, blocks, send, keep, rows)
    low = misc_s[...].astype(BF)
    for name in (keep,) if send is None else (send, keep):
        for m in range(len(plan.peers) if plan.direct else 1):
            name[m * rows + 4 * r : (m + 1) * rows, :] = low


def cond_back(plan, cond, mods, first, second, grad):
    d = plan.d
    rows = mods[...].astype(F32)
    total = None
    kept = []
    for g in range(plan.group):
        total = jnp.zeros((1, d), F32)
        for j in range(6):
            weight = first[:, j * d : (j + 1) * d] if j < 2 else second[:, (j - 2) * d : (j - 1) * d]
            line = jnp.broadcast_to(rows[g * 7 + 1 + j : g * 7 + 2 + j, :], (8, d)).astype(BF)
            total = total + dot_nt(line, weight)[0:1, :]
        kept.append(total)
    for g in range(plan.group):
        v = cond[g : g + 1, :].astype(F32)
        gate = 1.0 / (1.0 + jnp.exp(-v))
        grad[g : g + 1, :] = (kept[g] * (gate * (1.0 + v * (1.0 - gate)))).astype(BF)


def add_siblings(peers, rows, *refs):
    keep, received, own = refs[:3]
    outs = refs[3:]
    for m in range(peers):
        at = slice(m * rows, (m + 1) * rows)
        total = keep[at, :].astype(F32) + received[at, :].astype(F32)
        if m == 0:
            own[...] = total
        else:
            outs[m - 1][...] = total.astype(BF)


def add_chips(count, dp, quarter, own, *refs):
    received, mine, outs = refs[:count], refs[count], refs[count + 1 : count + dp]
    total_s = refs[count + dp]
    total = own[...]
    for piece in received:
        total = total + piece[...].astype(F32)
    total_s[...] = total
    me = lax.axis_index("dp")
    for j in range(dp):
        part = total_s[pl.ds(pl.multiple_of((me ^ j) * quarter, 16), quarter), :]
        if j == 0:
            mine[...] = part
        else:
            outs[j - 1][...] = part.astype(BF)


def add_groups(dp, *refs):
    total = refs[0][...]
    for piece in refs[1:dp]:
        total = total + piece[...].astype(F32)
    refs[dp][...] = total.astype(BF)


def gather_groups(dp, quarter, layout, *refs):
    pieces, outs, rows_s = refs[:dp], refs[dp:-1], refs[-1]
    me = lax.axis_index("dp")
    for j, piece in enumerate(pieces):
        rows_s[pl.ds(pl.multiple_of((me ^ j) * quarter, 16), quarter), :] = piece[...].astype(F32)
    d = rows_s.shape[1]
    at = 0
    for out, (blocks, rows) in zip(outs, layout):
        for j in range(blocks):
            out[:, j * d : (j + 1) * d] = rows_s[at : at + rows, :]
            at += rows


def last_sibling(peers, rows, keep, received, mods, own, *outs):
    for m in range(peers):
        at = slice(m * rows, (m + 1) * rows)
        total = keep[at, :].astype(F32) + received[at, :].astype(F32)
        if m == 0:
            own[0:rows, :] = total
            own[rows : rows + MOD_ROWS, :] = mods[...].astype(F32)
        else:
            outs[m - 1][0:rows, :] = total.astype(BF)
            outs[m - 1][rows : rows + MOD_ROWS, :] = mods[...]


def last_chips(count, dp, quarter, rows, own, *refs):
    received, mine, outs = refs[:count], refs[count], refs[count + 1 : count + dp]
    total_s, tail_s = refs[count + dp :]
    total = own[0:rows, :]
    for piece in received:
        total = total + piece[0:rows, :].astype(F32)
    total_s[...] = total[: rows - 16]
    tail_s[0:16, :] = total[rows - 16 :].astype(BF)
    tail_s[16 : 16 + MOD_ROWS, :] = own[rows:, :].astype(BF)
    for i, piece in enumerate(received):
        at = 16 + (i + 1) * MOD_ROWS
        tail_s[at : at + MOD_ROWS, :] = piece[rows:, :]
    me = lax.axis_index("dp")
    for j in range(dp):
        part = total_s[pl.ds(pl.multiple_of((me ^ j) * quarter, 16), quarter), :]
        name = mine if j == 0 else outs[j - 1]
        name[0:quarter, :] = part.astype(name.dtype)
        name[quarter:, :] = tail_s[...].astype(name.dtype)


def last_groups(dp, quarter, *refs):
    pieces, low, mods = refs[:dp], refs[dp], refs[dp + 1]
    total = pieces[0][0:quarter, :]
    for piece in pieces[1:]:
        total = total + piece[0:quarter, :].astype(F32)
    low[...] = total.astype(BF)
    each = pieces[0].shape[0] - quarter - 16
    for j, piece in enumerate(pieces):
        mods[j * each : (j + 1) * each, :] = piece[quarter + 16 :, :].astype(BF)


def ada_grads(plan, quarter, *refs):
    dp, d, r = plan.dp, plan.d, plan.rows
    pieces, mods = refs[:dp], refs[dp : dp + 2]
    ada, ada_bias, qv, proj, fc1, fc2 = refs[dp + 2 : dp + 8]
    rows_s, turned_s = refs[dp + 8 :]
    each = dp * plan.fsdp * MOD_ROWS // 2
    total = pieces[0][quarter : quarter + 16, :].astype(F32)
    for piece in pieces[1:]:
        total = total + piece[quarter : quarter + 16, :].astype(F32)
    for j, rows in enumerate(mods):
        rows_s[j * each : (j + 1) * each, :] = rows[...]
    count = 2 * each
    row = lax.broadcasted_iota(jnp.int32, (count, count), 0)
    column = lax.broadcasted_iota(jnp.int32, (count, count), 1)
    slot = row % MOD_ROWS
    source = row - slot + jnp.where(slot >= 7, 7, 0)
    pick = ((column == source) & (slot < 14)).astype(BF)
    turned_s[...] = dot(pick, rows_s[...]).T
    me = lax.axis_index("fsdp")
    mine = turned_s[pl.ds(pl.multiple_of(me * r, 16), r), :].astype(BF)
    lane = lax.broadcasted_iota(jnp.int32, (1, count), 1) % MOD_ROWS
    tall = lax.broadcasted_iota(jnp.int32, (count, 1), 0) % MOD_ROWS
    values = rows_s[...]
    sums = []
    for j in range(6):
        here = (lane == 1 + j) | (lane == 8 + j)
        ada[:, j * d : (j + 1) * d] = dot(jnp.where(here, mine, jnp.zeros_like(mine)), values)
        there = (tall == 1 + j) | (tall == 8 + j)
        sums.append(
            jnp.sum(jnp.where(there, values.astype(F32), 0.0), axis=0, keepdims=True)
        )
    lists = [
        (ada_bias, sums),
        (qv, [total[0:1], total[1:2]]),
        (proj, [total[2:3]]),
        (fc1, [total[3 + j : 4 + j] for j in range(plan.ffb)]),
        (fc2, [total[3 + plan.ffb : 4 + plan.ffb]]),
    ]
    for out, lines in lists:
        wide = lines[0] if len(lines) == 1 else jnp.concatenate(lines, axis=1)
        width = wide.shape[1]
        own = width // plan.fsdp
        wide = jnp.broadcast_to(wide, (8, width))
        wide = pltpu.roll(wide, lax.rem(width - me * own, width), 1)
        out[...] = wide[0:1, :own]


def swap(plan, value, k, axis="fsdp"):
    size = plan.fsdp if axis == "fsdp" else plan.dp
    return lax.ppermute(value, axis, [(i, i ^ k) for i in range(size)])


def behind(values, *gates):
    gates = [gate for gate in gates if gate is not None]
    return list(lax.optimization_barrier((tuple(values), tuple(gates)))[0])


def gather_chips(plan, value):
    if not plan.direct:
        return [value]
    return [value] + [swap(plan, value, k) for k in plan.peers[1:]]


def gather_joined(plan, chips, gate):
    if not plan.direct:
        return chips
    rows, d = chips[0].shape
    (mine,) = call(
        functools.partial(join, len(chips)),
        [((len(chips) * rows, d), BF)],
        [gate] + chips,
        micros=0.4,
    )
    return [mine, swap(plan, mine, 1)]


def gather_cores(plan, chips):
    if not plan.direct:
        return chips
    cores = [swap(plan, shard, 1) for shard in chips]
    return [shard for pair in zip(chips, cores) for shard in pair]


def chunk_siblings(plan, send, keep, gate):
    d, peers = plan.d, len(plan.peers)
    rows = keep.shape[0] // peers
    received = swap(plan, send, 1)
    keep, received = behind([keep, received], gate)
    own, *pieces = call(
        functools.partial(add_siblings, peers, rows),
        [((rows, d), F32)] + [((rows, d), BF)] * (peers - 1),
        [keep, received],
    )
    return own, [swap(plan, piece, k) for piece, k in zip(pieces, plan.peers[1:])]


def chunk_chips(plan, own, pieces):
    d, dp = plan.d, plan.dp
    rows = own.shape[0]
    quarter = rows // dp
    mine, *quarters = call(
        functools.partial(add_chips, len(pieces), dp, quarter),
        [((quarter, d), F32)] + [((quarter, d), BF)] * (dp - 1),
        [own] + pieces,
        [pltpu.VMEM((rows, d), F32)],
    )
    return mine, [swap(plan, part, j + 1, "dp") for j, part in enumerate(quarters)]


def chunk_groups(plan, mine, quarters, layout):
    d, dp = plan.d, plan.dp
    quarter = mine.shape[0]
    (low,) = call(functools.partial(add_groups, dp), [((quarter, d), BF)], [mine] + quarters)
    parts = [low] + [swap(plan, low, j, "dp") for j in range(1, dp)]
    return call(
        functools.partial(gather_groups, dp, quarter, layout),
        [((height, blocks * d), F32) for blocks, height in layout],
        parts,
        [pltpu.VMEM((quarter * dp, d), F32)],
    )


def reduce_last(plan, send, keep, mods):
    d, dp, peers, r = plan.d, plan.dp, len(plan.peers), plan.rows
    rows = keep.shape[0] // peers
    quarter = (rows - 16) // dp
    received = swap(plan, send, 1)
    long = rows + MOD_ROWS
    own, *pieces = call(
        functools.partial(last_sibling, peers, rows),
        [((long, d), F32)] + [((long, d), BF)] * (peers - 1),
        [keep, received, mods],
    )
    pieces = [swap(plan, piece, k) for piece, k in zip(pieces, plan.peers[1:])]
    tail = 16 + peers * MOD_ROWS
    mine, *quarters = call(
        functools.partial(last_chips, peers - 1, dp, quarter, rows),
        [((quarter + tail, d), F32)] + [((quarter + tail, d), BF)] * (dp - 1),
        [own] + pieces,
        [pltpu.VMEM((rows - 16, d), F32), pltpu.VMEM((tail, d), BF)],
    )
    quarters = [swap(plan, part, j + 1, "dp") for j, part in enumerate(quarters)]
    half = dp * peers * MOD_ROWS
    low, mods = call(
        functools.partial(last_groups, dp, quarter),
        [((quarter, d), BF), ((half, d), BF)],
        [mine] + quarters,
    )
    parts = [low] + [swap(plan, low, j, "dp") for j in range(1, dp)]
    widths = plan.bias_rows
    ada, *biases = call(
        functools.partial(ada_grads, plan, quarter),
        [((r, 6 * d), F32)] + [((1, w * d // plan.fsdp), F32) for w in widths],
        [mine] + quarters + [mods, swap(plan, mods, 1)],
        [pltpu.VMEM((2 * half, d), BF), pltpu.VMEM((d, 2 * half), F32)],
        micros=2,
    )
    qkv, proj = call(
        functools.partial(gather_groups, dp, quarter, ((3, r), (1, r))),
        [((r, 3 * d), F32), ((r, d), F32)],
        parts,
        [pltpu.VMEM((rows - 16, d), F32)],
    )
    return qkv, proj, ada, [bias.reshape(-1) for bias in biases]


def reduce_whole(plan, mlp, last, mods):
    d, ffb = plan.d, plan.ffb
    fc1_rows, fc2_rows = mlp[: ffb * d], mlp[ffb * d :]

    def unpack(rows, blocks):
        return rows.reshape(blocks, d, d).transpose(1, 0, 2).reshape(d, blocks * d)

    mods = mods[: 7 * plan.group].reshape(plan.group, 7, d)
    cond_act, grad_mod = mods[:, 0], mods[:, 1:].reshape(plan.group, 6 * d)
    ada = jnp.dot(cond_act.T, grad_mod, preferred_element_type=F32)
    misc = last[4 * d : 4 * d + 16]
    grads = (
        ada,
        jnp.sum(grad_mod.astype(F32), axis=0),
        unpack(last[: 3 * d], 3),
        misc[0:2].reshape(-1),
        last[3 * d : 4 * d],
        misc[2],
        unpack(fc1_rows, ffb),
        misc[3 : 3 + ffb].reshape(-1),
        fc2_rows,
        misc[3 + ffb],
    )
    owned = [
        lax.psum_scatter(grad.astype(BF), "fsdp", scatter_dimension=0, tiled=True) for grad in grads
    ]
    return [lax.psum(grad, "dp").astype(F32) for grad in owned]


def shards(
    fsdp,
    dp,
    latents,
    condition,
    cotangent,
    counts,
    ada_weight,
    ada_bias,
    qkv_weight,
    qv_bias,
    proj_weight,
    proj_bias,
    fc1_weight,
    fc1_bias,
    fc2_weight,
    fc2_bias,
):
    plan = Plan(latents, ada_weight, fc1_weight, fsdp, dp)
    d, n, group, ff, r = plan.d, plan.tokens, plan.group, plan.ff, plan.rows
    x = latents.reshape(n, d)
    cot = cotangent.reshape(n, d)
    cond = condition.reshape(group, d)
    biases = [ada_bias, qv_bias, proj_bias, fc1_bias, fc2_bias]
    weights = [ada_weight, qkv_weight, proj_weight, fc1_weight]
    third = fc2_weight
    if not plan.direct:
        def whole(v):
            return lax.all_gather(v, "fsdp", axis=0, tiled=True)

        biases, weights, third = [whole(v) for v in biases], [whole(v) for v in weights], whole(third)
    lengths = [bias.shape[0] for bias in biases]
    width = -(-sum(lengths) // 128) * 128
    line = sum(
        jnp.pad(bias.astype(F32), (sum(lengths[:i]), width - sum(lengths[: i + 1])))
        for i, bias in enumerate(biases)
    )
    first, second = call(
        functools.partial(pack_weights, plan),
        [((5 * r + 16, d), BF), (((2 * plan.ffb + 5) * r, d), BF)],
        weights + [third, line[None, :]],
        [pltpu.VMEM((16, d), F32), pltpu.SemaphoreType.DMA((plan.ffb + 11,))],
        far=(0, 1, 2, 3, 4),
        limit=PACK_LIMIT,
        micros=1.0,
    )
    first = gather_cores(plan, gather_chips(plan, first))
    second = gather_chips(plan, second)

    projected, mixed, mod_first, bias, qkv, ada_first = call(
        functools.partial(attn_forward, plan),
        [
            ((n, 3 * d), BF),
            ((n, d), BF),
            ((group, 2 * d), F32),
            ((16, d), F32),
            ((d, 3 * d), BF),
            ((d, 2 * d), BF),
        ],
        [x, cond] + first,
        [
            pltpu.VMEM((d, 3 * d), BF),
            pltpu.VMEM((d, 2 * d), BF),
            pltpu.SemaphoreType.DMA((2,)),
        ],
        far_outs=(4, 5),
        room=8,
        micros=4,
    )
    second = gather_joined(plan, second, mod_first)
    halves = len(plan.peers) if plan.direct else 1
    sides = plan.sides
    (act, gelu_back, mlp_in, grad_out, middle, attn_out, mod_second, fc1, ada_second, proj,
     grad_fc2, fc2) = call(
        functools.partial(mlp_first, plan),
        [
            ((n, ff), BF),
            ((n, ff), F32),
            ((n, d), BF),
            ((n, d), BF),
            ((n, d), F32),
            ((n, d), F32),
            ((group, 4 * d), F32),
            ((d, ff), BF),
            ((d, 4 * d), BF),
            ((d, d), BF),
            ((ff, d), BF),
            ((ff, d), BF),
        ],
        [counts, x, cond, cot, mixed, bias] + second,
        [pltpu.VMEM((d, 4 * d), BF), pltpu.SemaphoreType.DMA((1,))],
        smem=(0,),
        far_outs=(8,),
        room=8,
        micros=6,
    )
    outs = call(
        functools.partial(mlp_second, plan),
        [((halves * 2 * plan.ffb * r, d), BF)] * sides + [((n, ff), BF)],
        [grad_out, gelu_back, mlp_in, grad_fc2, fc2],
        [pltpu.VMEM((d, n), BF), pltpu.VMEM((d, ff), BF)],
        room=8,
        micros=4,
    )
    mlp_chunk = outs[:sides]
    (grad_pre,) = outs[sides:]
    block_out, grad_gate = call(
        functools.partial(mlp_close, plan),
        [((n, d), BF), ((group, d), F32)],
        [counts, cot, act, fc2, middle, mod_second, bias],
        smem=(0,),
        room=8,
        micros=1.5,
    )
    if plan.direct:
        mlp_own, mlp_pieces = chunk_siblings(plan, *mlp_chunk, grad_gate)
        (grad_pre,) = behind([grad_pre], mlp_own)
    grad_mixed, grad_middle, grad_proj, misc, grad_mod = call(
        functools.partial(mlp_back, plan),
        [
            ((n, d), BF),
            ((n, d), F32),
            ((d, d), BF),
            ((16, d), F32),
            ((group, 3 * d), F32),
        ],
        [counts, cot, grad_pre, fc1, middle, attn_out, mod_second, mixed, proj, grad_out],
        [pltpu.VMEM((n, d), BF)],
        smem=(0,),
        room=8,
        micros=3,
    )
    parts = []
    for g in range(group):
        parts += call(
            functools.partial(attn_back, plan, g),
            [((plan.seq, 3 * d), BF)],
            [projected, behind([grad_mixed], *parts)[0]],
            room=8,
            micros=3.3,
        )
    if plan.direct:
        mlp_mine, mlp_quarters = chunk_chips(plan, mlp_own, mlp_pieces)
        parts = behind(parts, *mlp_pieces)
    outs = call(
        functools.partial(attn_close, plan),
        [((halves * (4 * r + 16), d), BF)] * sides + [((n, d), BF), ((MOD_ROWS, d), BF)],
        [x, cond, grad_middle, qkv, mod_first, grad_proj, misc, grad_mod, grad_gate] + parts,
        [
            pltpu.VMEM((n, 3 * d), BF),
            pltpu.VMEM((d, 3 * d), BF),
            pltpu.VMEM((MOD_ROWS, d), F32),
            pltpu.VMEM((16, d), F32),
            pltpu.VMEM((group, d), F32),
            pltpu.VMEM((n, d), BF),
        ],
        room=8,
        micros=3,
    )
    last_chunk = outs[:sides]
    latents_grad, mods = outs[sides:]
    (cond_grad,) = call(
        functools.partial(cond_back, plan), [((group, d), BF)], [cond, mods, ada_first, ada_second],
        micros=2,
    )
    if plan.direct:
        layout = ((plan.ffb, r), (1, plan.ffb * r))
        fc1_grad, fc2_grad = chunk_groups(plan, mlp_mine, mlp_quarters, layout)
        qkv_grad, proj_grad, ada_grad, bias_grads = reduce_last(plan, *last_chunk, mods)
        weight_grads = [ada_grad, qkv_grad, proj_grad, fc1_grad, fc2_grad]
        grads = [grad for pair in zip(weight_grads, bias_grads) for grad in pair]
    else:
        grads = reduce_whole(plan, mlp_chunk[0], last_chunk[0], mods)
    return (
        block_out.reshape(latents.shape),
        latents_grad.reshape(latents.shape),
        cond_grad.reshape(condition.shape),
        *grads,
    )


def solution(mesh):
    tokens = P(None, ("dp", "fsdp"), None, None)
    per_latent = P(None, ("dp", "fsdp"), None)
    weight, bias = P("fsdp", None), P("fsdp")
    in_specs = (tokens, per_latent, tokens, P(None, ("dp", "fsdp"))) + (weight, bias) * 5
    out_specs = (tokens, tokens, per_latent) + (weight, bias) * 5
    body = functools.partial(shards, mesh.shape["fsdp"], mesh.shape["dp"])
    return jax.shard_map(body, mesh=mesh, in_specs=in_specs, out_specs=out_specs, check_vma=False)
```

```python
import functools
import math

import jax
import jax.numpy as jnp
from jax import lax
from jax.experimental import pallas as pl
from jax.experimental.pallas import tpu as pltpu
from jax.sharding import PartitionSpec as P

HEADS = 6
EPSILON = 1e-06
BF = jnp.bfloat16
F32 = jnp.float32
SQRT_2_PI = 0.7978845608028654
CUBIC = 0.044715
MARGIN = 0.0
PACK_LIMIT = 56 * 1024 * 1024
MOD_ROWS = 16


def dot(a, b):
    return lax.dot_general(a, b, (((1,), (0,)), ((), ())), preferred_element_type=F32)


def dot_nt(a, b):
    return lax.dot_general(a, b, (((1,), (1,)), ((), ())), preferred_element_type=F32)


def dot_tn(a, b):
    return lax.dot_general(a, b, (((0,), (0,)), ((), ())), preferred_element_type=F32)


def normalize(inputs):
    center = inputs - jnp.mean(inputs, axis=-1, keepdims=True)
    spread = jnp.mean(center * center, axis=-1, keepdims=True)
    inv_root = lax.rsqrt(spread + EPSILON)
    return center * inv_root, inv_root


def norm_back(grad_norm, normed, inv_root):
    first_mean = jnp.mean(grad_norm, axis=-1, keepdims=True)
    second_mean = jnp.mean(grad_norm * normed, axis=-1, keepdims=True)
    return inv_root * (grad_norm - first_mean - normed * second_mean)


def silu(v):
    return v / (1.0 + jnp.exp(-v))


def call(body, outs, ins, scratch=(), smem=(), far=(), far_outs=(), room=2, micros=0.2, limit=0):
    specs = [
        pl.BlockSpec(
            memory_space=pltpu.SMEM if i in smem else pltpu.HBM if i in far else pltpu.VMEM
        )
        for i in range(len(ins))
    ]
    def size(shape, kind):
        width = -(-shape[-1] // 128) * 128
        return math.prod(shape[:-1]) * width * jnp.dtype(kind).itemsize

    held = sum(size(v.shape, v.dtype) for v in scratch if len(v.shape) > 1)
    held += MARGIN * (sum(size(v.shape, v.dtype) for v in ins) + sum(size(*out) for out in outs))
    made = pl.pallas_call(
        body,
        out_shape=[jax.ShapeDtypeStruct(shape, kind) for shape, kind in outs],
        in_specs=specs,
        out_specs=[
            pl.BlockSpec(memory_space=pltpu.HBM if i in far_outs else pltpu.VMEM)
            for i in range(len(outs))
        ],
        scratch_shapes=list(scratch),
        compiler_params=pltpu.CompilerParams(vmem_limit_bytes=limit or int(held) + room * 1024 * 1024),
        cost_estimate=pl.CostEstimate(
            flops=0, bytes_accessed=int(micros * 3.69e6), transcendentals=0
        ),
    )(*ins)
    return list(made)


class Plan:
    def __init__(self, latents, ada_weight, fc1_weight, fsdp, dp):
        self.fsdp, self.dp = fsdp, dp
        self.mb, self.slots, self.seq, self.d = latents.shape
        self.group = self.mb * self.slots
        self.tokens = self.group * self.seq
        self.ff = fc1_weight.shape[1]
        self.ffb = self.ff // self.d
        own = ada_weight.shape[0]
        power = fsdp >= 2 and fsdp & (fsdp - 1) == 0 and dp & (dp - 1) == 0 and dp >= 2
        self.direct = power and own % 16 == 0 and (own * 4) % (16 * dp) == 0 and self.group == 2
        self.shards = fsdp if self.direct else 1
        self.rows = own if self.direct else self.d
        self.peers = [2 * m for m in range(fsdp // 2)]
        self.sides = 2 if self.direct else 1
        self.bias_rows = [6, 2, 1, self.ffb, 1]


def shard_of(plan, k):
    if not plan.direct:
        return 0
    return lax.axis_index("fsdp") ^ k


def pack_weights(
    plan, ada, qkv, proj, fc1, fc2, biases, counts, first, second, live, rows_s, sems
):
    d, r = plan.d, plan.rows

    def cut(ref, start, stop):
        return [ref.at[:, pl.ds(j * d, d)] for j in range(start, stop)]

    copies = []
    for packed, blocks in (
        (first, cut(qkv, 0, 3) + cut(ada, 0, 2)),
        (second, cut(fc1, 0, plan.ffb) + cut(ada, 2, 6) + [proj, fc2]),
    ):
        at = 0
        for block in blocks:
            target = packed.at[pl.ds(at, block.shape[0]), :]
            copies.append(pltpu.make_async_copy(block, target, sems.at[len(copies)]))
            at += block.shape[0]
    for copy in copies:
        copy.start()
    for g in range(plan.group):
        alive = jnp.where(g % plan.slots < counts[0, g // plan.slots], 1.0, 0.0).astype(F32)
        live[g : g + 1, :] = jnp.full((1, 128), alive)
    rows_s[...] = jnp.zeros_like(rows_s)
    line = jnp.broadcast_to(biases[...], (8, biases.shape[1]))
    at, start = 0, 0
    for count in plan.bias_rows:
        width = max(count * d, line.shape[1])
        wide = line
        if width > line.shape[1]:
            wide = jnp.concatenate([line, jnp.zeros((8, width - line.shape[1]), F32)], axis=1)
        if plan.direct:
            own = count * d // plan.fsdp
            me = lax.axis_index("fsdp")
            wide = pltpu.roll(wide, lax.rem(me * own + (width - start), width), 1)
            lane = lax.broadcasted_iota(jnp.int32, (8, width), 1)
            wide = jnp.where((lane >= me * own) & (lane < (me + 1) * own), wide, 0.0)
            start += own
        else:
            wide = line[:, start : start + count * d]
            start += count * d
        for j in range(count):
            rows_s[at + j : at + j + 1, :] = wide[0:1, j * d : (j + 1) * d]
        at += count
    first[5 * r : 5 * r + 16, :] = rows_s[...].astype(BF)
    for copy in copies:
        copy.wait()


def join(*refs):
    out, at = refs[-1], 0
    for ref in refs[:-1]:
        out[at : at + ref.shape[0], :] = ref[...]
        at += ref.shape[0]


def views(plan, joined):
    if not plan.direct:
        return joined
    found = []
    rows = sum(ref.shape[0] for ref in joined) // plan.shards
    for mine, sibling in zip(joined[::2], joined[1::2]):
        for m in range(mine.shape[0] // rows):
            found += [ref.at[pl.ds(m * rows, rows), :] for ref in (mine, sibling)]
    return found


def place(plan, shards, block, target, column):
    d, r = plan.d, plan.rows
    for k, shard in enumerate(shards):
        at = pl.multiple_of(shard_of(plan, k) * r, 16)
        target[pl.ds(at, r), column * d : (column + 1) * d] = shard[block * r : (block + 1) * r, :]


def emit(plan, grads, blocks, send, keep, rows):
    r = plan.rows
    for name, xor in ((keep, 0),) if send is None else ((send, 1), (keep, 0)):
        for m in range(len(plan.peers) if plan.direct else 1):
            owner = shard_of(plan, 2 * m + xor)
            for at, ref, column, stride, offset in blocks:
                start = pl.multiple_of(owner * (stride * r) + offset * r, 16)
                name[m * rows + at * r : m * rows + (at + 1) * r, :] = ref[
                    pl.ds(start, r), column * plan.d : (column + 1) * plan.d
                ]


def attn_forward(plan, *refs):
    s = plan.shards
    x, cond, cot = refs[:3]
    shards = refs[3 : 3 + s]
    (projected, mixed, modulation, bias, qkv_out, ada_out, x_out, cot_out, qkv, ada,
     sems) = refs[3 + s :]
    x_out[...] = x[...]
    cot_out[...] = cot[...]
    d, length, r = plan.d, plan.seq, plan.rows
    for j in range(3):
        place(plan, shards, j, qkv, j)
    for j in range(2):
        place(plan, shards, 3 + j, ada, j)
    copies = [
        pltpu.make_async_copy(qkv, qkv_out, sems.at[0]),
        pltpu.make_async_copy(ada, ada_out, sems.at[1]),
    ]
    for copy in copies:
        copy.start()
    total = shards[0][5 * r : 5 * r + 16, :].astype(F32)
    for shard in shards[1:]:
        total = total + shard[5 * r : 5 * r + 16, :].astype(F32)
    bias[...] = total
    cond_act = silu(cond[...].astype(F32)).astype(BF)
    mod = dot(cond_act, ada[...])
    for j in range(2):
        modulation[:, j * d : (j + 1) * d] = mod[:, j * d : (j + 1) * d] + bias[j : j + 1, :]
    left = lax.broadcasted_iota(jnp.int32, (1, 128), 1) < 64

    def latent(g, carry):
        at = pl.ds(pl.multiple_of(g * length, length), length)
        shift = modulation[pl.ds(g, 1), 0:d]
        scale = modulation[pl.ds(g, 1), d : 2 * d]
        normed, _ = normalize(x[at, :].astype(F32))
        rounded = (normed * (1.0 + scale) + shift).astype(BF)
        for j in range(3):
            piece = dot(rounded, qkv[:, j * d : (j + 1) * d])
            if j != 1:
                piece = piece + bias[6 + j // 2 : 7 + j // 2, :]
            projected[at, j * d : (j + 1) * d] = piece.astype(BF)
        for pair in range(HEADS // 2):
            lanes = slice(pair * 128, (pair + 1) * 128)
            q = projected[at, lanes] * jnp.asarray(0.125, BF)
            k = projected[at, d + pair * 128 : d + (pair + 1) * 128]
            v = projected[at, 2 * d + pair * 128 : 2 * d + (pair + 1) * 128]
            halves = []
            for side in (left, ~left):
                scores = dot_nt(jnp.where(side, q, jnp.zeros_like(q)), k)
                exponent = jnp.exp(scores - jnp.max(scores, axis=-1, keepdims=True))
                probs = exponent * (1.0 / jnp.sum(exponent, axis=-1, keepdims=True))
                halves.append(dot(probs.astype(BF), v))
            mixed[at, lanes] = jnp.where(left, halves[0], halves[1]).astype(BF)
        return carry

    lax.fori_loop(0, plan.group, latent, 0)
    for copy in copies:
        copy.wait()


def mlp_both(plan, *refs):
    s = 4 if plan.direct else 1
    lives, x, cot, mixed, bias, cond = refs[:6]
    shards, refs = views(plan, refs[6 : 6 + s]), refs[6 + s :]
    (send, refs) = (refs[0], refs[1:]) if plan.direct else (None, refs)
    (keep, act, grad_pre, grad_out, middle, attn_out, modulation, fc1, fc2, mixed_out, cot_out,
     proj, ada_out, mlp_in, turned, grad_fc1, grad_fc2, ada, sems) = refs
    mixed_out[...] = mixed[...]
    cot_out[...] = cot[...]
    d, length, ffb, r = plan.d, plan.seq, plan.ffb, plan.rows
    r4 = r * ffb
    for j in range(ffb):
        place(plan, shards, j, fc1, j)
    for k, shard in enumerate(shards):
        at = pl.multiple_of(shard_of(plan, k) * r4, 16)
        fc2[pl.ds(at, r4), :] = shard[(ffb + 5) * r : (ffb + 5) * r + r4, :]
    for j in range(4):
        place(plan, shards, ffb + j, ada, j)
    copy = pltpu.make_async_copy(ada, ada_out, sems.at[0])
    copy.start()
    place(plan, shards, ffb + 4, proj, 0)
    mod = dot(silu(cond[...].astype(F32)).astype(BF), ada[...])
    for j in range(4):
        modulation[:, j * d : (j + 1) * d] = mod[:, j * d : (j + 1) * d] + bias[2 + j : 3 + j, :]

    def latent(g, carry):
        at = pl.ds(pl.multiple_of(g * length, length), length)
        gate_attn, shift, scale, gate = [
            modulation[pl.ds(g, 1), j * d : (j + 1) * d] for j in range(4)
        ]
        live = lives[pl.ds(g, 1), 0:1]
        out = dot(mixed[at, :], proj[...]) + bias[8:9, :]
        attn_out[at, :] = out
        mid = x[at, :].astype(F32) + gate_attn * out
        middle[at, :] = mid
        normed, _ = normalize(mid)
        mlp_in[at, :] = (normed * (1.0 + scale) + shift).astype(BF)
        grad_out[at, :] = ((gate * live) * cot[at, :].astype(F32)).astype(BF)
        return carry

    lax.fori_loop(0, plan.group, latent, 0)
    turned[...] = mlp_in[...].T
    step = 256
    for c in range(plan.ff // step):
        cols = slice(c * step, (c + 1) * step)
        pieces = []
        start, rest = c * step, step
        while rest:
            row, lane = divmod(start, d)
            width = min(rest, d - lane)
            pieces.append(bias[9 + row : 10 + row, lane : lane + width])
            start, rest = start + width, rest - width
        shift = pieces[0] if len(pieces) == 1 else jnp.concatenate(pieces, axis=1)
        pre = dot(mlp_in[...], fc1[:, cols]) + shift
        square = pre * pre
        bend = jnp.tanh(pre * (SQRT_2_PI + (SQRT_2_PI * CUBIC) * square))
        half = 0.5 + 0.5 * bend
        value = (pre * half).astype(BF)
        act[:, cols] = value
        slope = (0.5 * SQRT_2_PI) + (1.5 * SQRT_2_PI * CUBIC) * square
        gelu_back = half + pre * (1.0 - bend * bend) * slope
        grad = (dot_nt(grad_out[...], fc2[cols, :]) * gelu_back).astype(BF)
        grad_pre[:, cols] = grad
        grad_fc2[cols, :] = dot_tn(value, grad_out[...]).astype(BF)
        grad_fc1[:, cols] = dot(turned[...], grad).astype(BF)
    blocks = [(j, grad_fc1, j, 1, 0) for j in range(ffb)]
    blocks += [(ffb + j, grad_fc2, 0, ffb, j) for j in range(ffb)]
    emit(plan, None, blocks, send, keep, 2 * r4)
    copy.wait()


def mlp_close(plan, lives, cot, act, fc2, middle, modulation, bias, block_out, grad_gate):
    d, length = plan.d, plan.seq

    def latent(g, carry):
        at = pl.ds(pl.multiple_of(g * length, length), length)
        gate = modulation[pl.ds(g, 1), 3 * d : 4 * d]
        live = lives[pl.ds(g, 1), 0:1]
        mlp_out = dot(act[at, :], fc2[...]) + bias[9 + plan.ffb : 10 + plan.ffb, :]
        block_out[at, :] = (live * (middle[at, :] + gate * mlp_out)).astype(BF)
        upstream = cot[at, :].astype(F32) * live
        grad_gate[pl.ds(g, 1), :] = jnp.sum(upstream * mlp_out, axis=0, keepdims=True)
        return carry

    lax.fori_loop(0, plan.group, latent, 0)


def mlp_back(plan, lives, cot, grad_pre, fc1, middle, attn_out, modulation, mixed, proj, grad_out,
             grad_mixed, grad_middle, grad_proj, misc, grad_mod, grad_gates):
    d, length = plan.d, plan.seq
    misc[...] = jnp.zeros_like(misc)
    sums = jnp.sum(grad_pre[...].astype(F32), axis=0, keepdims=True)
    for j in range(plan.ffb):
        misc[3 + j : 4 + j, :] = sums[:, j * d : (j + 1) * d]
    misc[3 + plan.ffb : 4 + plan.ffb, :] = jnp.sum(
        grad_out[...].astype(F32), axis=0, keepdims=True
    )

    def latent(g, carry):
        at = pl.ds(pl.multiple_of(g * length, length), length)
        gate_attn, _, scale = [modulation[pl.ds(g, 1), j * d : (j + 1) * d] for j in range(3)]
        live = lives[pl.ds(g, 1), 0:1]
        upstream = cot[at, :].astype(F32) * live
        normed, rstd = normalize(middle[at, :])
        grad_in = dot_nt(grad_pre[at, :], fc1[...])
        grad_mid = upstream + norm_back(grad_in * (1.0 + scale), normed, rstd)
        grad_middle[at, :] = grad_mid
        rounded = (gate_attn * grad_mid).astype(BF)
        grad_gates[at, :] = rounded
        grad_mixed[at, :] = dot_nt(rounded, proj[...]).astype(BF)
        pieces = [grad_mid * attn_out[at, :], grad_in, grad_in * normed]
        for j, piece in enumerate(pieces):
            grad_mod[pl.ds(g, 1), j * d : (j + 1) * d] = jnp.sum(piece, axis=0, keepdims=True)
        return carry

    lax.fori_loop(0, plan.group, latent, 0)
    misc[2:3, :] = jnp.sum(grad_gates[...].astype(F32), axis=0, keepdims=True)
    grad_proj[...] = dot_tn(mixed[...], grad_gates[...]).astype(BF)


def attn_core_back(plan, at, projected, grad_mixed, out, where):
    d = plan.d
    left = lax.broadcasted_iota(jnp.int32, (1, 128), 1) < 64
    for pair in range(HEADS // 2):
        lanes = slice(pair * 128, (pair + 1) * 128)
        q = projected[at, lanes] * jnp.asarray(0.125, BF)
        k = projected[at, d + pair * 128 : d + (pair + 1) * 128]
        v = projected[at, 2 * d + pair * 128 : 2 * d + (pair + 1) * 128]
        gm = grad_mixed[at, lanes]
        grads_q, grads_k, grads_v = [], [], []
        for side in (left, ~left):
            scores = dot_nt(jnp.where(side, q, jnp.zeros_like(q)), k)
            exponent = jnp.exp(scores - jnp.max(scores, axis=-1, keepdims=True))
            probs = exponent * (1.0 / jnp.sum(exponent, axis=-1, keepdims=True))
            grad_probs = dot_nt(jnp.where(side, gm, jnp.zeros_like(gm)), v)
            inner = jnp.sum(probs * grad_probs, axis=-1, keepdims=True)
            grad_scores = (probs * (grad_probs - inner)).astype(BF)
            grads_q.append(dot(grad_scores, k))
            grads_k.append(dot_tn(grad_scores, q))
            grads_v.append(dot_tn(probs.astype(BF), gm))
        for j, (pieces, factor) in enumerate(((grads_q, 0.125), (grads_k, 1.0), (grads_v, 1.0))):
            merged = jnp.where(left, pieces[0], pieces[1]) * factor
            out[where, j * d + pair * 128 : j * d + (pair + 1) * 128] = merged.astype(BF)


def attn_back(plan, g, projected, grad_mixed, out):
    at = slice(g * plan.seq, (g + 1) * plan.seq)
    attn_core_back(plan, at, projected, grad_mixed, out, slice(0, plan.seq))


def attn_close(plan, *refs):
    (x, cond, grad_middle, qkv, modulation, grad_mod, grad_gate) = refs[:7]
    parts, outs = refs[7 : 7 + plan.group], refs[7 + plan.group :]
    latents_grad, mods, attn_in, rows_s, cond_s = outs
    d, length = plan.d, plan.seq
    rows_s[...] = jnp.zeros_like(rows_s)
    cond_s[...] = silu(cond[...].astype(F32))
    for g, part in enumerate(parts):
        at = slice(g * length, (g + 1) * length)
        shift = modulation[g : g + 1, 0:d]
        scale = modulation[g : g + 1, d : 2 * d]
        normed, rstd = normalize(x[at, :].astype(F32))
        attn_in[at, :] = (normed * (1.0 + scale) + shift).astype(BF)
        grad_in = dot_nt(part[...], qkv[...])
        grad = grad_middle[at, :] + norm_back(grad_in * (1.0 + scale), normed, rstd)
        latents_grad[at, :] = grad.astype(BF)
        pieces = [cond_s[g : g + 1, :], jnp.sum(grad_in, axis=0, keepdims=True)]
        pieces += [jnp.sum(grad_in * normed, axis=0, keepdims=True)]
        pieces += [grad_mod[g : g + 1, j * d : (j + 1) * d] for j in range(3)]
        pieces += [grad_gate[g : g + 1, :]]
        for j, piece in enumerate(pieces):
            rows_s[g * 7 + j : g * 7 + j + 1, :] = piece
    mods[...] = rows_s[...].astype(BF)


def attn_grads(plan, *refs):
    attn_in, grad_proj, misc = refs[:3]
    parts, outs = refs[3 : 3 + plan.group], refs[3 + plan.group :]
    (send, outs) = (outs[0], outs[1:]) if plan.direct else (None, outs)
    keep, grad_qkv, misc_s, turned = outs
    d, length, r = plan.d, plan.seq, plan.rows
    misc_s[...] = misc[...]
    turned[...] = attn_in[...].T
    for j in range(3):
        cols = slice(j * d, (j + 1) * d)
        total, sums = 0.0, 0.0
        for g, part in enumerate(parts):
            piece = part[:, cols]
            total = total + dot(turned[:, g * length : (g + 1) * length], piece)
            sums = sums + jnp.sum(piece.astype(F32), axis=0, keepdims=True)
        grad_qkv[:, cols] = total.astype(BF)
        if j != 1:
            misc_s[j // 2 : j // 2 + 1, :] = sums
    blocks = [(j, grad_qkv, j, 1, 0) for j in range(3)] + [(3, grad_proj, 0, 1, 0)]
    rows = 4 * r + 16
    emit(plan, None, blocks, send, keep, rows)
    low = misc_s[...].astype(BF)
    for name in (keep,) if send is None else (send, keep):
        for m in range(len(plan.peers) if plan.direct else 1):
            name[m * rows + 4 * r : (m + 1) * rows, :] = low


def cond_back(plan, cond, mods, first, second, grad):
    d = plan.d
    rows = mods[...].astype(F32)
    total = None
    kept = []
    for g in range(plan.group):
        total = jnp.zeros((1, d), F32)
        for j in range(6):
            weight = first[:, j * d : (j + 1) * d] if j < 2 else second[:, (j - 2) * d : (j - 1) * d]
            line = jnp.broadcast_to(rows[g * 7 + 1 + j : g * 7 + 2 + j, :], (8, d)).astype(BF)
            total = total + dot_nt(line, weight)[0:1, :]
        kept.append(total)
    for g in range(plan.group):
        v = cond[g : g + 1, :].astype(F32)
        gate = 1.0 / (1.0 + jnp.exp(-v))
        grad[g : g + 1, :] = (kept[g] * (gate * (1.0 + v * (1.0 - gate)))).astype(BF)


def add_siblings(peers, rows, *refs):
    keep, received, own = refs[:3]
    outs = refs[3:]
    for m in range(peers):
        at = slice(m * rows, (m + 1) * rows)
        total = keep[at, :].astype(F32) + received[at, :].astype(F32)
        if m == 0:
            own[...] = total
        else:
            outs[m - 1][...] = total.astype(BF)


def add_chips(count, dp, quarter, own, *refs):
    received, (mine, sent, total_s) = refs[:count], refs[count:]
    total = own[...]
    for piece in received:
        total = total + piece[...].astype(F32)
    total_s[...] = total
    me = lax.axis_index("dp")
    for j in range(dp):
        part = total_s[pl.ds(pl.multiple_of((me ^ j) * quarter, 16), quarter), :]
        out = sent if j % 2 else mine
        out[j // 2 * quarter : (j // 2 + 1) * quarter, :] = part.astype(out.dtype)


def halve(quarter, held, received, mine, sent):
    for j in range(held.shape[0] // quarter):
        at = slice(j * quarter, (j + 1) * quarter)
        out = sent if j % 2 else mine
        total = held[at, :] + received[at, :].astype(F32)
        out[j // 2 * quarter : (j // 2 + 1) * quarter, :] = total.astype(out.dtype)


def gather_groups(dp, sizes, layouts, *refs):
    pieces, outs, scratch = refs[:dp], refs[dp : -len(sizes)], refs[-len(sizes) :]
    me = lax.axis_index("dp")
    start, outs = 0, list(outs)
    for quarter, layout, rows_s in zip(sizes, layouts, scratch):
        for j, piece in enumerate(pieces):
            at = pl.multiple_of((me ^ j) * quarter, 16)
            rows_s[pl.ds(at, quarter), :] = piece[start : start + quarter, :].astype(F32)
        start += quarter
        d, at = rows_s.shape[1], 0
        for blocks, rows in layout:
            out = outs.pop(0)
            for j in range(blocks):
                out[:, j * d : (j + 1) * d] = rows_s[at : at + rows, :]
                at += rows


def last_sibling(peers, rows, keep, received, mods, own, *outs):
    for m in range(peers):
        at = slice(m * rows, (m + 1) * rows)
        total = keep[at, :].astype(F32) + received[at, :].astype(F32)
        if m == 0:
            own[0:rows, :] = total
            own[rows : rows + MOD_ROWS, :] = mods[...].astype(F32)
        else:
            outs[m - 1][0:rows, :] = total.astype(BF)
            outs[m - 1][rows : rows + MOD_ROWS, :] = mods[...]


def last_chips(count, dp, quarter, rows, own, *refs):
    received, mine, outs = refs[:count], refs[count], refs[count + 1 : count + dp]
    total_s, tail_s = refs[count + dp :]
    total = own[0:rows, :]
    for piece in received:
        total = total + piece[0:rows, :].astype(F32)
    total_s[...] = total[: rows - 16]
    tail_s[0:16, :] = total[rows - 16 :].astype(BF)
    tail_s[16 : 16 + MOD_ROWS, :] = own[rows:, :].astype(BF)
    for i, piece in enumerate(received):
        at = 16 + (i + 1) * MOD_ROWS
        tail_s[at : at + MOD_ROWS, :] = piece[rows:, :]
    me = lax.axis_index("dp")
    for j in range(dp):
        part = total_s[pl.ds(pl.multiple_of((me ^ j) * quarter, 16), quarter), :]
        name = mine if j == 0 else outs[j - 1]
        name[0:quarter, :] = part.astype(name.dtype)
        name[quarter:, :] = tail_s[...].astype(name.dtype)


def add_groups(dp, sizes, *refs):
    low, mods = refs[2 + dp :]
    start = 0
    for quarter, pieces in zip(sizes, (refs[:2], refs[2 : 2 + dp])):
        total = pieces[0][0:quarter, :]
        for piece in pieces[1:]:
            total = total + piece[0:quarter, :].astype(F32)
        low[start : start + quarter, :] = total.astype(BF)
        start += quarter
    each = pieces[0].shape[0] - quarter - 16
    for j, piece in enumerate(pieces):
        mods[j * each : (j + 1) * each, :] = piece[quarter + 16 :, :].astype(BF)


def ada_grads(plan, quarter, *refs):
    dp, d, r = plan.dp, plan.d, plan.rows
    pieces, mods = refs[:dp], refs[dp : dp + 2]
    ada, ada_bias, qv, proj, fc1, fc2 = refs[dp + 2 : dp + 8]
    rows_s, turned_s = refs[dp + 8 :]
    each = dp * plan.fsdp * MOD_ROWS // 2
    total = pieces[0][quarter : quarter + 16, :].astype(F32)
    for piece in pieces[1:]:
        total = total + piece[quarter : quarter + 16, :].astype(F32)
    for j, rows in enumerate(mods):
        rows_s[j * each : (j + 1) * each, :] = rows[...]
    count = 2 * each
    row = lax.broadcasted_iota(jnp.int32, (count, count), 0)
    column = lax.broadcasted_iota(jnp.int32, (count, count), 1)
    slot = row % MOD_ROWS
    source = row - slot + jnp.where(slot >= 7, 7, 0)
    pick = ((column == source) & (slot < 14)).astype(BF)
    turned_s[...] = dot(pick, rows_s[...]).T
    me = lax.axis_index("fsdp")
    mine = turned_s[pl.ds(pl.multiple_of(me * r, 16), r), :].astype(BF)
    lane = lax.broadcasted_iota(jnp.int32, (1, count), 1) % MOD_ROWS
    tall = lax.broadcasted_iota(jnp.int32, (count, 1), 0) % MOD_ROWS
    values = rows_s[...]
    sums = []
    for j in range(6):
        here = (lane == 1 + j) | (lane == 8 + j)
        ada[:, j * d : (j + 1) * d] = dot(jnp.where(here, mine, jnp.zeros_like(mine)), values)
        there = (tall == 1 + j) | (tall == 8 + j)
        sums.append(
            jnp.sum(jnp.where(there, values.astype(F32), 0.0), axis=0, keepdims=True)
        )
    lists = [
        (ada_bias, sums),
        (qv, [total[0:1], total[1:2]]),
        (proj, [total[2:3]]),
        (fc1, [total[3 + j : 4 + j] for j in range(plan.ffb)]),
        (fc2, [total[3 + plan.ffb : 4 + plan.ffb]]),
    ]
    for out, lines in lists:
        wide = lines[0] if len(lines) == 1 else jnp.concatenate(lines, axis=1)
        width = wide.shape[1]
        own = width // plan.fsdp
        wide = jnp.broadcast_to(wide, (8, width))
        wide = pltpu.roll(wide, lax.rem(width - me * own, width), 1)
        out[...] = wide[0:1, :own]


def swap(plan, value, k, axis="fsdp"):
    size = plan.fsdp if axis == "fsdp" else plan.dp
    return lax.ppermute(value, axis, [(i, i ^ k) for i in range(size)])


def behind(values, *gates):
    gates = [gate for gate in gates if gate is not None]
    return list(lax.optimization_barrier((tuple(values), tuple(gates)))[0])


def gather_chips(plan, value):
    if not plan.direct:
        return [value]
    return [value] + [swap(plan, value, k) for k in plan.peers[1:]]


def gather_joined(plan, chips):
    if not plan.direct:
        return chips
    joined = []
    count = len(chips) // 2
    for some in (chips[:count], chips[count:]):
        shape = (sum(v.shape[0] for v in some), plan.d)
        (mine,) = call(join, [(shape, BF)], some, micros=0.4)
        joined += [mine, swap(plan, mine, 1)]
    return joined


def gather_cores(plan, chips):
    if not plan.direct:
        return chips
    cores = [swap(plan, shard, 1) for shard in chips]
    return [shard for pair in zip(chips, cores) for shard in pair]


def chunk_siblings(plan, send, keep, gate):
    d, peers = plan.d, len(plan.peers)
    rows = keep.shape[0] // peers
    received = swap(plan, send, 1)
    keep, received = behind([keep, received], gate)
    own, *pieces = call(
        functools.partial(add_siblings, peers, rows),
        [((rows, d), F32)] + [((rows, d), BF)] * (peers - 1),
        [keep, received],
    )
    return own, [swap(plan, piece, k) for piece, k in zip(pieces, plan.peers[1:])]


def chunk_chips(plan, own, pieces):
    d, dp = plan.d, plan.dp
    rows = own.shape[0]
    mine, sent = call(
        functools.partial(add_chips, len(pieces), dp, rows // dp),
        [((rows // 2, d), F32), ((rows // 2, d), BF)],
        [own] + pieces,
        [pltpu.VMEM((rows, d), F32)],
    )
    return mine, swap(plan, sent, 1, "dp")


def chunk_halves(plan, mine, received):
    dp, step = plan.dp, 2
    quarter = 2 * mine.shape[0] // dp
    while mine.shape[0] > quarter:
        shape = (mine.shape[0] // 2, plan.d)
        mine, sent = call(
            functools.partial(halve, quarter), [(shape, F32), (shape, BF)], [mine, received]
        )
        received, step = swap(plan, sent, step, "dp"), 2 * step
    return mine, received


def finish(plan, mlp_own, mlp_pieces, mlp_layout, send, keep, mods, cond_grad):
    d, dp, peers, r = plan.d, plan.dp, len(plan.peers), plan.rows
    rows = keep.shape[0] // peers
    quarter = (rows - 16) // dp
    received = swap(plan, send, 1)
    mlp_mine, mlp_half = chunk_chips(plan, mlp_own, mlp_pieces)
    received, keep = behind([received, keep], mlp_mine)
    mlp_mine, mlp_half = chunk_halves(plan, mlp_mine, mlp_half)
    long = rows + MOD_ROWS
    own, *pieces = call(
        functools.partial(last_sibling, peers, rows),
        [((long, d), F32)] + [((long, d), BF)] * (peers - 1),
        [keep, received, mods],
    )
    pieces = [swap(plan, piece, k) for piece, k in zip(pieces, plan.peers[1:])]
    pieces = behind(pieces, cond_grad, mlp_half)
    tail = 16 + peers * MOD_ROWS
    mine, *quarters = call(
        functools.partial(last_chips, peers - 1, dp, quarter, rows),
        [((quarter + tail, d), F32)] + [((quarter + tail, d), BF)] * (dp - 1),
        [own] + pieces,
        [pltpu.VMEM((rows - 16, d), F32), pltpu.VMEM((tail, d), BF)],
    )
    quarters = [swap(plan, part, j + 1, "dp") for j, part in enumerate(quarters)]
    half = dp * peers * MOD_ROWS
    sizes = (mlp_mine.shape[0], quarter)
    low, mods = call(
        functools.partial(add_groups, dp, sizes),
        [((sum(sizes), d), BF), ((half, d), BF)],
        [mlp_mine, mlp_half, mine] + quarters,
    )
    parts = [swap(plan, low, j, "dp") for j in range(1, dp)]
    ada, *biases = call(
        functools.partial(ada_grads, plan, quarter),
        [((r, 6 * d), F32)] + [((1, w * d // plan.fsdp), F32) for w in plan.bias_rows],
        [mine] + quarters + [mods, swap(plan, mods, 1)],
        [pltpu.VMEM((2 * half, d), BF), pltpu.VMEM((d, 2 * half), F32)],
        micros=2,
    )
    biases = [bias.reshape(-1) for bias in biases]
    parts = behind(parts, ada, *biases)
    layouts = (mlp_layout, ((3, r), (1, r)))
    fc1, fc2, qkv, proj = call(
        functools.partial(gather_groups, dp, sizes, layouts),
        [((height, blocks * d), F32) for layout in layouts for blocks, height in layout],
        [low] + parts,
        [pltpu.VMEM((size * dp, d), F32) for size in sizes],
    )
    return [ada, qkv, proj, fc1, fc2], biases


def reduce_whole(plan, mlp, last, mods):
    d, ffb = plan.d, plan.ffb
    fc1_rows, fc2_rows = mlp[: ffb * d], mlp[ffb * d :]

    def unpack(rows, blocks):
        return rows.reshape(blocks, d, d).transpose(1, 0, 2).reshape(d, blocks * d)

    mods = mods[: 7 * plan.group].reshape(plan.group, 7, d)
    cond_act, grad_mod = mods[:, 0], mods[:, 1:].reshape(plan.group, 6 * d)
    ada = jnp.dot(cond_act.T, grad_mod, preferred_element_type=F32)
    misc = last[4 * d : 4 * d + 16]
    grads = (
        ada,
        jnp.sum(grad_mod.astype(F32), axis=0),
        unpack(last[: 3 * d], 3),
        misc[0:2].reshape(-1),
        last[3 * d : 4 * d],
        misc[2],
        unpack(fc1_rows, ffb),
        misc[3 : 3 + ffb].reshape(-1),
        fc2_rows,
        misc[3 + ffb],
    )
    owned = [
        lax.psum_scatter(grad.astype(BF), "fsdp", scatter_dimension=0, tiled=True) for grad in grads
    ]
    return [lax.psum(grad, "dp").astype(F32) for grad in owned]


def shards(
    fsdp,
    dp,
    latents,
    condition,
    cotangent,
    counts,
    ada_weight,
    ada_bias,
    qkv_weight,
    qv_bias,
    proj_weight,
    proj_bias,
    fc1_weight,
    fc1_bias,
    fc2_weight,
    fc2_bias,
):
    plan = Plan(latents, ada_weight, fc1_weight, fsdp, dp)
    d, n, group, ff, r = plan.d, plan.tokens, plan.group, plan.ff, plan.rows
    x = latents.reshape(n, d)
    cot = cotangent.reshape(n, d)
    cond = condition.reshape(group, d)
    biases = [ada_bias, qv_bias, proj_bias, fc1_bias, fc2_bias]
    weights = [ada_weight, qkv_weight, proj_weight, fc1_weight]
    third = fc2_weight
    if not plan.direct:
        def whole(v):
            return lax.all_gather(v, "fsdp", axis=0, tiled=True)

        biases, weights, third = [whole(v) for v in biases], [whole(v) for v in weights], whole(third)
    lengths = [bias.shape[0] for bias in biases]
    width = -(-sum(lengths) // 128) * 128
    line = sum(
        jnp.pad(bias.astype(F32), (sum(lengths[:i]), width - sum(lengths[: i + 1])))
        for i, bias in enumerate(biases)
    )
    first, second, live = call(
        functools.partial(pack_weights, plan),
        [((5 * r + 16, d), BF), (((2 * plan.ffb + 5) * r, d), BF), ((group, 128), F32)],
        weights + [third, line[None, :], counts.T],
        [pltpu.VMEM((16, d), F32), pltpu.SemaphoreType.DMA((plan.ffb + 11,))],
        smem=(6,),
        far=(0, 1, 2, 3, 4),
        limit=PACK_LIMIT,
        micros=1.0,
    )
    first = gather_cores(plan, gather_chips(plan, first))
    second = gather_chips(plan, second)

    projected, mixed, mod_first, bias, qkv, ada_first, x_near, cot_near = call(
        functools.partial(attn_forward, plan),
        [
            ((n, 3 * d), BF),
            ((n, d), BF),
            ((group, 2 * d), F32),
            ((16, d), F32),
            ((d, 3 * d), BF),
            ((d, 2 * d), BF),
            ((n, d), BF),
            ((n, d), BF),
        ],
        [x, cond, cot] + first,
        [
            pltpu.VMEM((d, 3 * d), BF),
            pltpu.VMEM((d, 2 * d), BF),
            pltpu.SemaphoreType.DMA((2,)),
        ],
        far_outs=(4, 5),
        room=5,
        micros=4,
    )
    if plan.direct:
        second = second[:1] + [behind([v], mod_first)[0] for v in second[1:]]
    shards = gather_joined(plan, second)
    halves = len(plan.peers) if plan.direct else 1
    sides = plan.sides
    outs = call(
        functools.partial(mlp_both, plan),
        [((halves * 2 * plan.ffb * r, d), BF)] * sides
        + [
            ((n, ff), BF),
            ((n, ff), BF),
            ((n, d), BF),
            ((n, d), F32),
            ((n, d), F32),
            ((group, 4 * d), F32),
            ((d, ff), BF),
            ((ff, d), BF),
            ((n, d), BF),
            ((n, d), BF),
            ((d, d), BF),
            ((d, 4 * d), BF),
        ],
        [live, x_near, cot_near, mixed, bias, cond] + shards,
        [
            pltpu.VMEM((n, d), BF),
            pltpu.VMEM((d, n), BF),
            pltpu.VMEM((d, ff), BF),
            pltpu.VMEM((ff, d), BF),
            pltpu.VMEM((d, 4 * d), BF),
            pltpu.SemaphoreType.DMA((1,)),
        ],
        far_outs=(sides + 11,),
        room=5,
        micros=10,
    )
    mlp_chunk = outs[:sides]
    (act, grad_pre, grad_out, middle, attn_out, mod_second, fc1, fc2, mixed, cot_near, proj,
     ada_second) = outs[sides:]
    block_out, grad_gate = call(
        functools.partial(mlp_close, plan),
        [((n, d), BF), ((group, d), F32)],
        [live, cot_near, act, fc2, middle, mod_second, bias],
        room=5,
        micros=1.5,
    )
    if plan.direct:
        mlp_own, mlp_pieces = chunk_siblings(plan, *mlp_chunk, grad_gate)
        (grad_pre,) = behind([grad_pre], mlp_own)
    grad_mixed, grad_middle, grad_proj, misc, grad_mod = call(
        functools.partial(mlp_back, plan),
        [
            ((n, d), BF),
            ((n, d), F32),
            ((d, d), BF),
            ((16, d), F32),
            ((group, 3 * d), F32),
        ],
        [live, cot_near, grad_pre, fc1, middle, attn_out, mod_second, mixed, proj, grad_out],
        [pltpu.VMEM((n, d), BF)],
        room=5,
        micros=3,
    )
    parts = []
    for g in range(group):
        parts += call(
            functools.partial(attn_back, plan, g),
            [((plan.seq, 3 * d), BF)],
            [projected, behind([grad_mixed], *parts)[0]],
            room=5,
            micros=3.3,
        )
    latents_grad, mods, attn_in = call(
        functools.partial(attn_close, plan),
        [((n, d), BF), ((MOD_ROWS, d), BF), ((n, d), BF)],
        [x, cond, grad_middle, qkv, mod_first, grad_mod, grad_gate] + parts,
        [pltpu.VMEM((MOD_ROWS, d), F32), pltpu.VMEM((group, d), F32)],
        room=5,
        micros=2,
    )
    (cond_grad,) = call(
        functools.partial(cond_back, plan),
        [((group, d), BF)],
        [cond, mods, ada_first, ada_second],
        micros=2,
    )
    if plan.direct:
        parts = behind(parts, *mlp_pieces)
    last_chunk = call(
        functools.partial(attn_grads, plan),
        [((halves * (4 * r + 16), d), BF)] * sides,
        [attn_in, grad_proj, misc] + parts,
        [
            pltpu.VMEM((d, 3 * d), BF),
            pltpu.VMEM((16, d), F32),
            pltpu.VMEM((d, n), BF),
        ],
        room=5,
        micros=1.5,
    )
    if plan.direct:
        layout = ((plan.ffb, r), (1, plan.ffb * r))
        weight_grads, bias_grads = finish(
            plan, mlp_own, mlp_pieces, layout, *last_chunk, mods, cond_grad
        )
        grads = [grad for pair in zip(weight_grads, bias_grads) for grad in pair]
    else:
        grads = reduce_whole(plan, mlp_chunk[0], last_chunk[0], mods)
    return (
        block_out.reshape(latents.shape),
        latents_grad.reshape(latents.shape),
        cond_grad.reshape(condition.shape),
        *grads,
    )


def solution(mesh):
    tokens = P(None, ("dp", "fsdp"), None, None)
    per_latent = P(None, ("dp", "fsdp"), None)
    weight, bias = P("fsdp", None), P("fsdp")
    in_specs = (tokens, per_latent, tokens, P(None, ("dp", "fsdp"))) + (weight, bias) * 5
    out_specs = (tokens, tokens, per_latent) + (weight, bias) * 5
    body = functools.partial(shards, mesh.shape["fsdp"], mesh.shape["dp"])
    return jax.shard_map(body, mesh=mesh, in_specs=in_specs, out_specs=out_specs, check_vma=False)
```

```python
import functools
import math

import jax
import jax.numpy as jnp
from jax import lax
from jax.experimental import pallas as pl
from jax.experimental.pallas import tpu as pltpu
from jax.sharding import PartitionSpec as P

HEADS = 6
EPSILON = 1e-06
BF = jnp.bfloat16
F32 = jnp.float32
SQRT_2_PI = 0.7978845608028654
CUBIC = 0.044715
MARGIN = 0.0
PACK_LIMIT = 56 * 1024 * 1024
MOD_USED = 14
MOD_ROWS = 16


def dot(a, b):
    return lax.dot_general(a, b, (((1,), (0,)), ((), ())), preferred_element_type=F32)


def dot_nt(a, b):
    return lax.dot_general(a, b, (((1,), (1,)), ((), ())), preferred_element_type=F32)


def dot_tn(a, b):
    return lax.dot_general(a, b, (((0,), (0,)), ((), ())), preferred_element_type=F32)


def normalize(inputs):
    center = inputs - jnp.mean(inputs, axis=-1, keepdims=True)
    spread = jnp.mean(center * center, axis=-1, keepdims=True)
    inv_root = lax.rsqrt(spread + EPSILON)
    return center * inv_root, inv_root


def norm_back(grad_norm, normed, inv_root):
    first_mean = jnp.mean(grad_norm, axis=-1, keepdims=True)
    second_mean = jnp.mean(grad_norm * normed, axis=-1, keepdims=True)
    return inv_root * (grad_norm - first_mean - normed * second_mean)


def silu(v):
    return v / (1.0 + jnp.exp(-v))


def call(body, outs, ins, scratch=(), smem=(), far=(), far_outs=(), room=2, micros=0.2, limit=0):
    specs = [
        pl.BlockSpec(
            memory_space=pltpu.SMEM if i in smem else pltpu.HBM if i in far else pltpu.VMEM
        )
        for i in range(len(ins))
    ]
    def size(shape, kind):
        width = -(-shape[-1] // 128) * 128
        return math.prod(shape[:-1]) * width * jnp.dtype(kind).itemsize

    held = sum(size(v.shape, v.dtype) for v in scratch if len(v.shape) > 1)
    held += MARGIN * (sum(size(v.shape, v.dtype) for v in ins) + sum(size(*out) for out in outs))
    made = pl.pallas_call(
        body,
        out_shape=[jax.ShapeDtypeStruct(shape, kind) for shape, kind in outs],
        in_specs=specs,
        out_specs=[
            pl.BlockSpec(memory_space=pltpu.HBM if i in far_outs else pltpu.VMEM)
            for i in range(len(outs))
        ],
        scratch_shapes=list(scratch),
        compiler_params=pltpu.CompilerParams(vmem_limit_bytes=limit or int(held) + room * 1024 * 1024),
        cost_estimate=pl.CostEstimate(
            flops=0, bytes_accessed=int(micros * 3.69e6), transcendentals=0
        ),
    )(*ins)
    return list(made)


class Plan:
    def __init__(self, latents, ada_weight, fc1_weight, fsdp, dp):
        self.fsdp, self.dp = fsdp, dp
        self.mb, self.slots, self.seq, self.d = latents.shape
        self.group = self.mb * self.slots
        self.tokens = self.group * self.seq
        self.ff = fc1_weight.shape[1]
        self.ffb = self.ff // self.d
        own = ada_weight.shape[0]
        power = fsdp >= 2 and fsdp & (fsdp - 1) == 0 and dp & (dp - 1) == 0 and dp >= 2
        self.direct = power and own % 16 == 0 and (own * 4) % (16 * dp) == 0 and self.group == 2
        self.shards = fsdp if self.direct else 1
        self.rows = own if self.direct else self.d
        self.peers = [2 * m for m in range(fsdp // 2)]
        self.sides = 2 if self.direct else 1
        self.bias_rows = [6, 2, 1, self.ffb, 1]


def shard_of(plan, k):
    if not plan.direct:
        return 0
    return lax.axis_index("fsdp") ^ k


def pack_weights(
    plan, ada, qkv, proj, fc1, fc2, biases, counts, first, second, live, rows_s, sems
):
    d, r = plan.d, plan.rows

    def cut(ref, start, stop):
        return [ref.at[:, pl.ds(j * d, d)] for j in range(start, stop)]

    copies = []
    for packed, blocks in (
        (first, cut(qkv, 0, 3) + cut(ada, 0, 2)),
        (second, cut(fc1, 0, plan.ffb) + cut(ada, 2, 6) + [proj, fc2]),
    ):
        at = 0
        for block in blocks:
            target = packed.at[pl.ds(at, block.shape[0]), :]
            copies.append(pltpu.make_async_copy(block, target, sems.at[len(copies)]))
            at += block.shape[0]
    for copy in copies:
        copy.start()
    for g in range(plan.group):
        alive = jnp.where(g % plan.slots < counts[0, g // plan.slots], 1.0, 0.0).astype(F32)
        live[g : g + 1, :] = jnp.full((1, 128), alive)
    rows_s[...] = jnp.zeros_like(rows_s)
    line = jnp.broadcast_to(biases[...], (8, biases.shape[1]))
    at, start = 0, 0
    for count in plan.bias_rows:
        width = max(count * d, line.shape[1])
        wide = line
        if width > line.shape[1]:
            wide = jnp.concatenate([line, jnp.zeros((8, width - line.shape[1]), F32)], axis=1)
        if plan.direct:
            own = count * d // plan.fsdp
            me = lax.axis_index("fsdp")
            wide = pltpu.roll(wide, lax.rem(me * own + (width - start), width), 1)
            lane = lax.broadcasted_iota(jnp.int32, (8, width), 1)
            wide = jnp.where((lane >= me * own) & (lane < (me + 1) * own), wide, 0.0)
            start += own
        else:
            wide = line[:, start : start + count * d]
            start += count * d
        for j in range(count):
            rows_s[at + j : at + j + 1, :] = wide[0:1, j * d : (j + 1) * d]
        at += count
    first[5 * r : 5 * r + 16, :] = rows_s[...].astype(BF)
    for copy in copies:
        copy.wait()


def join(*refs):
    out, at = refs[-1], 0
    for ref in refs[:-1]:
        out[at : at + ref.shape[0], :] = ref[...]
        at += ref.shape[0]


def views(plan, joined):
    if not plan.direct:
        return joined
    found = []
    rows = sum(ref.shape[0] for ref in joined) // plan.shards
    for mine, sibling in zip(joined[::2], joined[1::2]):
        for m in range(mine.shape[0] // rows):
            found += [ref.at[pl.ds(m * rows, rows), :] for ref in (mine, sibling)]
    return found


def place(plan, shards, block, target, column):
    d, r = plan.d, plan.rows
    for k, shard in enumerate(shards):
        at = pl.multiple_of(shard_of(plan, k) * r, 16)
        target[pl.ds(at, r), column * d : (column + 1) * d] = shard[block * r : (block + 1) * r, :]


def emit(plan, grads, blocks, send, keep, rows):
    r = plan.rows
    for name, xor in ((keep, 0),) if send is None else ((send, 1), (keep, 0)):
        for m in range(len(plan.peers) if plan.direct else 1):
            owner = shard_of(plan, 2 * m + xor)
            for at, ref, column, stride, offset in blocks:
                start = pl.multiple_of(owner * (stride * r) + offset * r, 16)
                name[m * rows + at * r : m * rows + (at + 1) * r, :] = ref[
                    pl.ds(start, r), column * plan.d : (column + 1) * plan.d
                ]


def attn_forward(plan, *refs):
    s = plan.shards
    x, cond, cot = refs[:3]
    shards = refs[3 : 3 + s]
    (projected, mixed, modulation, bias, qkv_out, ada_out, x_out, cot_out, qkv, ada,
     sems) = refs[3 + s :]
    x_out[...] = x[...]
    cot_out[...] = cot[...]
    d, length, r = plan.d, plan.seq, plan.rows
    for j in range(3):
        place(plan, shards, j, qkv, j)
    for j in range(2):
        place(plan, shards, 3 + j, ada, j)
    copies = [
        pltpu.make_async_copy(qkv, qkv_out, sems.at[0]),
        pltpu.make_async_copy(ada, ada_out, sems.at[1]),
    ]
    for copy in copies:
        copy.start()
    total = shards[0][5 * r : 5 * r + 16, :].astype(F32)
    for shard in shards[1:]:
        total = total + shard[5 * r : 5 * r + 16, :].astype(F32)
    bias[...] = total
    cond_act = silu(cond[...].astype(F32)).astype(BF)
    mod = dot(cond_act, ada[...])
    for j in range(2):
        modulation[:, j * d : (j + 1) * d] = mod[:, j * d : (j + 1) * d] + bias[j : j + 1, :]
    left = lax.broadcasted_iota(jnp.int32, (1, 128), 1) < 64

    def latent(g, carry):
        at = pl.ds(pl.multiple_of(g * length, length), length)
        shift = modulation[pl.ds(g, 1), 0:d]
        scale = modulation[pl.ds(g, 1), d : 2 * d]
        normed, _ = normalize(x[at, :].astype(F32))
        rounded = (normed * (1.0 + scale) + shift).astype(BF)
        for j in range(3):
            piece = dot(rounded, qkv[:, j * d : (j + 1) * d])
            if j != 1:
                piece = piece + bias[6 + j // 2 : 7 + j // 2, :]
            projected[at, j * d : (j + 1) * d] = piece.astype(BF)
        for pair in range(HEADS // 2):
            lanes = slice(pair * 128, (pair + 1) * 128)
            q = projected[at, lanes] * jnp.asarray(0.125, BF)
            k = projected[at, d + pair * 128 : d + (pair + 1) * 128]
            v = projected[at, 2 * d + pair * 128 : 2 * d + (pair + 1) * 128]
            halves = []
            for side in (left, ~left):
                scores = dot_nt(jnp.where(side, q, jnp.zeros_like(q)), k)
                exponent = jnp.exp(scores - jnp.max(scores, axis=-1, keepdims=True))
                probs = exponent * (1.0 / jnp.sum(exponent, axis=-1, keepdims=True))
                halves.append(dot(probs.astype(BF), v))
            mixed[at, lanes] = jnp.where(left, halves[0], halves[1]).astype(BF)
        return carry

    lax.fori_loop(0, plan.group, latent, 0)
    for copy in copies:
        copy.wait()


def mlp_both(plan, *refs):
    s = 4 if plan.direct else 1
    lives, x, cot, mixed, bias, cond = refs[:6]
    shards, refs = views(plan, refs[6 : 6 + s]), refs[6 + s :]
    (send, refs) = (refs[0], refs[1:]) if plan.direct else (None, refs)
    (keep, act, grad_pre, grad_out, middle, attn_out, modulation, fc1, fc2, mixed_out, cot_out,
     proj, ada_out, mlp_in, turned, grad_fc1, grad_fc2, ada, sems) = refs
    mixed_out[...] = mixed[...]
    cot_out[...] = cot[...]
    d, length, ffb, r = plan.d, plan.seq, plan.ffb, plan.rows
    r4 = r * ffb
    for j in range(ffb):
        place(plan, shards, j, fc1, j)
    for k, shard in enumerate(shards):
        at = pl.multiple_of(shard_of(plan, k) * r4, 16)
        fc2[pl.ds(at, r4), :] = shard[(ffb + 5) * r : (ffb + 5) * r + r4, :]
    for j in range(4):
        place(plan, shards, ffb + j, ada, j)
    copy = pltpu.make_async_copy(ada, ada_out, sems.at[0])
    copy.start()
    place(plan, shards, ffb + 4, proj, 0)
    mod = dot(silu(cond[...].astype(F32)).astype(BF), ada[...])
    for j in range(4):
        modulation[:, j * d : (j + 1) * d] = mod[:, j * d : (j + 1) * d] + bias[2 + j : 3 + j, :]

    def latent(g, carry):
        at = pl.ds(pl.multiple_of(g * length, length), length)
        gate_attn, shift, scale, gate = [
            modulation[pl.ds(g, 1), j * d : (j + 1) * d] for j in range(4)
        ]
        live = lives[pl.ds(g, 1), 0:1]
        out = dot(mixed[at, :], proj[...]) + bias[8:9, :]
        attn_out[at, :] = out
        mid = x[at, :].astype(F32) + gate_attn * out
        middle[at, :] = mid
        normed, _ = normalize(mid)
        mlp_in[at, :] = (normed * (1.0 + scale) + shift).astype(BF)
        grad_out[at, :] = ((gate * live) * cot[at, :].astype(F32)).astype(BF)
        return carry

    lax.fori_loop(0, plan.group, latent, 0)
    turned[...] = mlp_in[...].T
    step = 256
    for c in range(plan.ff // step):
        cols = slice(c * step, (c + 1) * step)
        pieces = []
        start, rest = c * step, step
        while rest:
            row, lane = divmod(start, d)
            width = min(rest, d - lane)
            pieces.append(bias[9 + row : 10 + row, lane : lane + width])
            start, rest = start + width, rest - width
        shift = pieces[0] if len(pieces) == 1 else jnp.concatenate(pieces, axis=1)
        pre = dot(mlp_in[...], fc1[:, cols]) + shift
        square = pre * pre
        bend = jnp.tanh(pre * (SQRT_2_PI + (SQRT_2_PI * CUBIC) * square))
        half = 0.5 + 0.5 * bend
        value = (pre * half).astype(BF)
        act[:, cols] = value
        slope = (0.5 * SQRT_2_PI) + (1.5 * SQRT_2_PI * CUBIC) * square
        gelu_back = half + pre * (1.0 - bend * bend) * slope
        grad = (dot_nt(grad_out[...], fc2[cols, :]) * gelu_back).astype(BF)
        grad_pre[:, cols] = grad
        grad_fc2[cols, :] = dot_tn(value, grad_out[...]).astype(BF)
        grad_fc1[:, cols] = dot(turned[...], grad).astype(BF)
    blocks = [(j, grad_fc1, j, 1, 0) for j in range(ffb)]
    blocks += [(ffb + j, grad_fc2, 0, ffb, j) for j in range(ffb)]
    emit(plan, None, blocks, send, keep, 2 * r4)
    copy.wait()


def mlp_close(plan, lives, cot, act, fc2, middle, modulation, bias, block_out, grad_gate):
    d, length = plan.d, plan.seq

    def latent(g, carry):
        at = pl.ds(pl.multiple_of(g * length, length), length)
        gate = modulation[pl.ds(g, 1), 3 * d : 4 * d]
        live = lives[pl.ds(g, 1), 0:1]
        mlp_out = dot(act[at, :], fc2[...]) + bias[9 + plan.ffb : 10 + plan.ffb, :]
        block_out[at, :] = (live * (middle[at, :] + gate * mlp_out)).astype(BF)
        upstream = cot[at, :].astype(F32) * live
        grad_gate[pl.ds(g, 1), :] = jnp.sum(upstream * mlp_out, axis=0, keepdims=True)
        return carry

    lax.fori_loop(0, plan.group, latent, 0)


def mlp_back(plan, lives, cot, grad_pre, fc1, middle, attn_out, modulation, mixed, proj, grad_out,
             grad_mixed, grad_middle, grad_proj, misc, grad_mod, grad_gates):
    d, length = plan.d, plan.seq
    misc[...] = jnp.zeros_like(misc)
    sums = jnp.sum(grad_pre[...].astype(F32), axis=0, keepdims=True)
    for j in range(plan.ffb):
        misc[3 + j : 4 + j, :] = sums[:, j * d : (j + 1) * d]
    misc[3 + plan.ffb : 4 + plan.ffb, :] = jnp.sum(
        grad_out[...].astype(F32), axis=0, keepdims=True
    )

    def latent(g, carry):
        at = pl.ds(pl.multiple_of(g * length, length), length)
        gate_attn, _, scale = [modulation[pl.ds(g, 1), j * d : (j + 1) * d] for j in range(3)]
        live = lives[pl.ds(g, 1), 0:1]
        upstream = cot[at, :].astype(F32) * live
        normed, rstd = normalize(middle[at, :])
        grad_in = dot_nt(grad_pre[at, :], fc1[...])
        grad_mid = upstream + norm_back(grad_in * (1.0 + scale), normed, rstd)
        grad_middle[at, :] = grad_mid
        rounded = (gate_attn * grad_mid).astype(BF)
        grad_gates[at, :] = rounded
        grad_mixed[at, :] = dot_nt(rounded, proj[...]).astype(BF)
        pieces = [grad_mid * attn_out[at, :], grad_in, grad_in * normed]
        for j, piece in enumerate(pieces):
            grad_mod[pl.ds(g, 1), j * d : (j + 1) * d] = jnp.sum(piece, axis=0, keepdims=True)
        return carry

    lax.fori_loop(0, plan.group, latent, 0)
    misc[2:3, :] = jnp.sum(grad_gates[...].astype(F32), axis=0, keepdims=True)
    grad_proj[...] = dot_tn(mixed[...], grad_gates[...]).astype(BF)


def attn_core_back(plan, at, projected, grad_mixed, out, where):
    d = plan.d
    left = lax.broadcasted_iota(jnp.int32, (1, 128), 1) < 64
    for pair in range(HEADS // 2):
        lanes = slice(pair * 128, (pair + 1) * 128)
        q = projected[at, lanes] * jnp.asarray(0.125, BF)
        k = projected[at, d + pair * 128 : d + (pair + 1) * 128]
        v = projected[at, 2 * d + pair * 128 : 2 * d + (pair + 1) * 128]
        gm = grad_mixed[at, lanes]
        grads_q, grads_k, grads_v = [], [], []
        for side in (left, ~left):
            scores = dot_nt(jnp.where(side, q, jnp.zeros_like(q)), k)
            exponent = jnp.exp(scores - jnp.max(scores, axis=-1, keepdims=True))
            probs = exponent * (1.0 / jnp.sum(exponent, axis=-1, keepdims=True))
            grad_probs = dot_nt(jnp.where(side, gm, jnp.zeros_like(gm)), v)
            inner = jnp.sum(probs * grad_probs, axis=-1, keepdims=True)
            grad_scores = (probs * (grad_probs - inner)).astype(BF)
            grads_q.append(dot(grad_scores, k))
            grads_k.append(dot_tn(grad_scores, q))
            grads_v.append(dot_tn(probs.astype(BF), gm))
        for j, (pieces, factor) in enumerate(((grads_q, 0.125), (grads_k, 1.0), (grads_v, 1.0))):
            merged = jnp.where(left, pieces[0], pieces[1]) * factor
            out[where, j * d + pair * 128 : j * d + (pair + 1) * 128] = merged.astype(BF)


def attn_back(plan, g, projected, grad_mixed, out):
    at = slice(g * plan.seq, (g + 1) * plan.seq)
    attn_core_back(plan, at, projected, grad_mixed, out, slice(0, plan.seq))


def attn_close(plan, *refs):
    (x, cond, grad_middle, qkv, modulation, grad_mod, grad_gate) = refs[:7]
    parts, outs = refs[7 : 7 + plan.group], refs[7 + plan.group :]
    latents_grad, mods, attn_in, rows_s, cond_s = outs
    d, length = plan.d, plan.seq
    rows_s[...] = jnp.zeros_like(rows_s)
    cond_s[...] = silu(cond[...].astype(F32))
    for g, part in enumerate(parts):
        at = slice(g * length, (g + 1) * length)
        shift = modulation[g : g + 1, 0:d]
        scale = modulation[g : g + 1, d : 2 * d]
        normed, rstd = normalize(x[at, :].astype(F32))
        attn_in[at, :] = (normed * (1.0 + scale) + shift).astype(BF)
        grad_in = dot_nt(part[...], qkv[...])
        grad = grad_middle[at, :] + norm_back(grad_in * (1.0 + scale), normed, rstd)
        latents_grad[at, :] = grad.astype(BF)
        pieces = [cond_s[g : g + 1, :], jnp.sum(grad_in, axis=0, keepdims=True)]
        pieces += [jnp.sum(grad_in * normed, axis=0, keepdims=True)]
        pieces += [grad_mod[g : g + 1, j * d : (j + 1) * d] for j in range(3)]
        pieces += [grad_gate[g : g + 1, :]]
        for j, piece in enumerate(pieces):
            rows_s[g * 7 + j : g * 7 + j + 1, :] = piece
    mods[...] = rows_s[...].astype(BF)


def attn_grads(plan, *refs):
    attn_in, grad_proj, misc = refs[:3]
    parts, outs = refs[3 : 3 + plan.group], refs[3 + plan.group :]
    (send, outs) = (outs[0], outs[1:]) if plan.direct else (None, outs)
    keep, grad_qkv, misc_s, turned = outs
    d, length, r = plan.d, plan.seq, plan.rows
    misc_s[...] = misc[...]
    turned[...] = attn_in[...].T
    for j in range(3):
        cols = slice(j * d, (j + 1) * d)
        total, sums = 0.0, 0.0
        for g, part in enumerate(parts):
            piece = part[:, cols]
            total = total + dot(turned[:, g * length : (g + 1) * length], piece)
            sums = sums + jnp.sum(piece.astype(F32), axis=0, keepdims=True)
        grad_qkv[:, cols] = total.astype(BF)
        if j != 1:
            misc_s[j // 2 : j // 2 + 1, :] = sums
    blocks = [(j, grad_qkv, j, 1, 0) for j in range(3)] + [(3, grad_proj, 0, 1, 0)]
    rows = 4 * r + 16
    emit(plan, None, blocks, send, keep, rows)
    low = misc_s[...].astype(BF)
    for name in (keep,) if send is None else (send, keep):
        for m in range(len(plan.peers) if plan.direct else 1):
            name[m * rows + 4 * r : (m + 1) * rows, :] = low


def cond_back(plan, cond, mods, first, second, grad):
    d = plan.d
    rows = mods[...].astype(F32)
    total = None
    kept = []
    for g in range(plan.group):
        total = jnp.zeros((1, d), F32)
        for j in range(6):
            weight = first[:, j * d : (j + 1) * d] if j < 2 else second[:, (j - 2) * d : (j - 1) * d]
            line = jnp.broadcast_to(rows[g * 7 + 1 + j : g * 7 + 2 + j, :], (8, d)).astype(BF)
            total = total + dot_nt(line, weight)[0:1, :]
        kept.append(total)
    for g in range(plan.group):
        v = cond[g : g + 1, :].astype(F32)
        gate = 1.0 / (1.0 + jnp.exp(-v))
        grad[g : g + 1, :] = (kept[g] * (gate * (1.0 + v * (1.0 - gate)))).astype(BF)


def add_siblings(peers, rows, *refs):
    keep, received, own = refs[:3]
    outs = refs[3:]
    for m in range(peers):
        at = slice(m * rows, (m + 1) * rows)
        total = keep[at, :].astype(F32) + received[at, :].astype(F32)
        if m == 0:
            own[...] = total
        else:
            outs[m - 1][...] = total.astype(BF)


def add_chips(count, dp, quarter, own, *refs):
    received, (mine, sent, total_s) = refs[:count], refs[count:]
    total = own[...]
    for piece in received:
        total = total + piece[...].astype(F32)
    total_s[...] = total
    me = lax.axis_index("dp")
    for j in range(dp):
        part = total_s[pl.ds(pl.multiple_of((me ^ j) * quarter, 16), quarter), :]
        out = sent if j % 2 else mine
        out[j // 2 * quarter : (j // 2 + 1) * quarter, :] = part.astype(out.dtype)


def halve(quarter, held, received, mine, sent):
    for j in range(held.shape[0] // quarter):
        at = slice(j * quarter, (j + 1) * quarter)
        out = sent if j % 2 else mine
        total = held[at, :] + received[at, :].astype(F32)
        out[j // 2 * quarter : (j // 2 + 1) * quarter, :] = total.astype(out.dtype)


def gather_groups(dp, orders, layouts, *refs):
    count = sum(len(order) for order in orders)
    arrays, outs, scratch = list(refs[:count]), list(refs[count : -len(orders)]), refs[-len(orders) :]
    me = lax.axis_index("dp")
    for order, layout, rows_s in zip(orders, layouts, scratch):
        quarter, d = rows_s.shape[0] // dp, rows_s.shape[1]
        for some in order:
            array = arrays.pop(0)
            for i, j in enumerate(some):
                at = pl.multiple_of((me ^ j) * quarter, 16)
                piece = array[i * quarter : (i + 1) * quarter, :]
                rows_s[pl.ds(at, quarter), :] = piece.astype(F32)
        at = 0
        for blocks, rows in layout:
            out = outs.pop(0)
            for j in range(blocks):
                out[:, j * d : (j + 1) * d] = rows_s[at : at + rows, :]
                at += rows


def last_sibling(peers, rows, keep, received, mods, own, *outs):
    for m in range(peers):
        at = slice(m * rows, (m + 1) * rows)
        total = keep[at, :].astype(F32) + received[at, :].astype(F32)
        if m == 0:
            own[0:rows, :] = total
            own[rows : rows + MOD_ROWS, :] = mods[...].astype(F32)
        else:
            outs[m - 1][0:rows, :] = total.astype(BF)
            outs[m - 1][rows : rows + MOD_ROWS, :] = mods[...]


def last_chips(count, dp, quarter, rows, own, *refs):
    received, mine, outs = refs[:count], refs[count], refs[count + 1 : count + dp]
    total_s, tail_s = refs[count + dp :]
    tail_s[...] = jnp.zeros_like(tail_s)
    total = own[0:rows, :]
    for piece in received:
        total = total + piece[0:rows, :].astype(F32)
    total_s[...] = total[: rows - 16]
    for i, piece in enumerate((own,) + received):
        lines = piece[rows:, :].astype(F32)
        tail_s[i * MOD_USED : (i + 1) * MOD_USED, :] = lines[0:MOD_USED]
    end = (count + 1) * MOD_USED
    tail_s[end : end + 8, :] = total[rows - 16 : rows - 8]
    me = lax.axis_index("dp")
    for j in range(dp):
        part = total_s[pl.ds(pl.multiple_of((me ^ j) * quarter, 16), quarter), :]
        name = mine if j == 0 else outs[j - 1]
        name[0:quarter, :] = part.astype(name.dtype)
        name[quarter:, :] = tail_s[...].astype(name.dtype)


def add_two(first, second, out):
    out[...] = (first[...] + second[...].astype(F32)).astype(BF)


def add_groups(dp, quarter, *refs):
    pieces, (low, mods) = refs[:dp], refs[dp:]
    total = pieces[0][0:quarter, :]
    for piece in pieces[1:]:
        total = total + piece[0:quarter, :].astype(F32)
    low[...] = total.astype(BF)
    each = pieces[0].shape[0] - quarter
    for j, piece in enumerate(pieces):
        mods[j * each : (j + 1) * each, :] = piece[quarter:, :].astype(BF)


def ada_grads(plan, quarter, *refs):
    dp, d, r = plan.dp, plan.d, plan.rows
    pieces, mods = refs[:dp], refs[dp : dp + 2]
    ada, ada_bias, qv, proj, fc1, fc2 = refs[dp + 2 : dp + 8]
    rows_s, turned_s = refs[dp + 8 :]
    block = pieces[0].shape[0] - quarter
    used = len(plan.peers) * MOD_USED
    each = dp * block
    total = pieces[0][quarter + used : quarter + used + 8, :].astype(F32)
    for piece in pieces[1:]:
        total = total + piece[quarter:, :].astype(F32)[used : used + 8]
    for j, rows in enumerate(mods):
        rows_s[j * each : (j + 1) * each, :] = rows[...]
    count = 2 * each
    row = lax.broadcasted_iota(jnp.int32, (count, count), 0)
    column = lax.broadcasted_iota(jnp.int32, (count, count), 1)
    slot = row % block
    pick = ((column == row - slot % 7) & (slot < used)).astype(BF)
    turned_s[...] = dot(pick, rows_s[...]).T
    me = lax.axis_index("fsdp")
    mine = turned_s[pl.ds(pl.multiple_of(me * r, 16), r), :].astype(BF)
    lane = lax.broadcasted_iota(jnp.int32, (1, count), 1) % block
    tall = lax.broadcasted_iota(jnp.int32, (count, 1), 0) % block
    values = rows_s[...]
    sums = []
    for j in range(6):
        here = (lane % 7 == 1 + j) & (lane < used)
        ada[:, j * d : (j + 1) * d] = dot(jnp.where(here, mine, jnp.zeros_like(mine)), values)
        there = (tall % 7 == 1 + j) & (tall < used)
        sums.append(
            jnp.sum(jnp.where(there, values.astype(F32), 0.0), axis=0, keepdims=True)
        )
    lists = [
        (ada_bias, sums),
        (qv, [total[0:1], total[1:2]]),
        (proj, [total[2:3]]),
        (fc1, [total[3 + j : 4 + j] for j in range(plan.ffb)]),
        (fc2, [total[3 + plan.ffb : 4 + plan.ffb]]),
    ]
    for out, lines in lists:
        wide = lines[0] if len(lines) == 1 else jnp.concatenate(lines, axis=1)
        width = wide.shape[1]
        own = width // plan.fsdp
        wide = jnp.broadcast_to(wide, (8, width))
        wide = pltpu.roll(wide, lax.rem(width - me * own, width), 1)
        out[...] = wide[0:1, :own]


def swap(plan, value, k, axis="fsdp"):
    size = plan.fsdp if axis == "fsdp" else plan.dp
    return lax.ppermute(value, axis, [(i, i ^ k) for i in range(size)])


def behind(values, *gates):
    gates = [gate for gate in gates if gate is not None]
    return list(lax.optimization_barrier((tuple(values), tuple(gates)))[0])


def gather_chips(plan, value):
    if not plan.direct:
        return [value]
    return [value] + [swap(plan, value, k) for k in plan.peers[1:]]


def gather_joined(plan, gate, chips):
    if not plan.direct:
        return chips
    joined = []
    count = len(chips) // 2
    for some in (chips[:count], chips[count:]):
        some = [behind([v], gate, *joined[:1])[0] for v in some]
        shape = (sum(v.shape[0] for v in some), plan.d)
        (mine,) = call(join, [(shape, BF)], some, micros=0.4)
        joined += [mine, swap(plan, mine, 1)]
    return joined


def gather_cores(plan, chips):
    if not plan.direct:
        return chips
    cores = [swap(plan, shard, 1) for shard in chips]
    return [shard for pair in zip(chips, cores) for shard in pair]


def chunk_siblings(plan, send, keep, gate):
    d, peers = plan.d, len(plan.peers)
    rows = keep.shape[0] // peers
    received = swap(plan, send, 1)
    keep, received = behind([keep, received], gate)
    own, *pieces = call(
        functools.partial(add_siblings, peers, rows),
        [((rows, d), F32)] + [((rows, d), BF)] * (peers - 1),
        [keep, received],
    )
    return own, [swap(plan, piece, k) for piece, k in zip(pieces, plan.peers[1:])]


def chunk_chips(plan, own, pieces):
    d, dp = plan.d, plan.dp
    rows = own.shape[0]
    mine, sent = call(
        functools.partial(add_chips, len(pieces), dp, rows // dp),
        [((rows // 2, d), F32), ((rows // 2, d), BF)],
        [own] + pieces,
        [pltpu.VMEM((rows, d), F32)],
    )
    return mine, swap(plan, sent, 1, "dp")


def chunk_halves(plan, mine, received):
    dp, step = plan.dp, 2
    quarter = 2 * mine.shape[0] // dp
    while mine.shape[0] > quarter:
        shape = (mine.shape[0] // 2, plan.d)
        mine, sent = call(
            functools.partial(halve, quarter), [(shape, F32), (shape, BF)], [mine, received]
        )
        received, step = swap(plan, sent, step, "dp"), 2 * step
    return mine, received


def finish(plan, mlp_own, mlp_pieces, mlp_layout, send, keep, mods, cond_grad):
    d, dp, peers, r = plan.d, plan.dp, len(plan.peers), plan.rows
    rows = keep.shape[0] // peers
    quarter = (rows - 16) // dp
    received = swap(plan, send, 1)
    mlp_mine, mlp_half = chunk_chips(plan, mlp_own, mlp_pieces)
    received, keep = behind([received, keep], mlp_mine)
    mlp_mine, mlp_half = chunk_halves(plan, mlp_mine, mlp_half)
    long = rows + MOD_ROWS
    own, *pieces = call(
        functools.partial(last_sibling, peers, rows),
        [((long, d), F32)] + [((long, d), BF)] * (peers - 1),
        [keep, received, mods],
    )
    pieces = [swap(plan, piece, k) for piece, k in zip(pieces, plan.peers[1:])]
    pieces = behind(pieces, cond_grad, mlp_half)
    tail = -(-(peers * MOD_USED + 8) // 16) * 16
    mine, *quarters = call(
        functools.partial(last_chips, peers - 1, dp, quarter, rows),
        [((quarter + tail, d), F32)] + [((quarter + tail, d), BF)] * (dp - 1),
        [own] + pieces,
        [pltpu.VMEM((rows - 16, d), F32), pltpu.VMEM((tail, d), F32)],
    )
    quarters = [swap(plan, part, j + 1, "dp") for j, part in enumerate(quarters)]
    mlp_mine, mlp_half = behind([mlp_mine, mlp_half], mine)
    (held,) = call(add_two, [(mlp_mine.shape, BF)], [mlp_mine, mlp_half])
    order, step = [0], dp // 2
    while step > 1:
        found = [held, swap(plan, held, step, "dp")]
        order, step = order + [j ^ step for j in order], step // 2
        (held,) = call(join, [((2 * held.shape[0], d), BF)], found)
    half = dp * tail
    low, mods = call(
        functools.partial(add_groups, dp, quarter),
        [((quarter, d), BF), ((half, d), BF)],
        [mine] + quarters,
    )
    parts = [swap(plan, low, j, "dp") for j in range(1, dp)] + [swap(plan, held, 1, "dp")]
    orders = ((order, [j ^ 1 for j in order]), [[j] for j in range(dp)])
    ada, *biases = call(
        functools.partial(ada_grads, plan, quarter),
        [((r, 6 * d), F32)] + [((1, w * d // plan.fsdp), F32) for w in plan.bias_rows],
        [mine] + quarters + [mods, swap(plan, mods, 1)],
        [pltpu.VMEM((2 * half, d), BF), pltpu.VMEM((d, 2 * half), F32)],
        micros=2,
    )
    biases = [bias.reshape(-1) for bias in biases]
    *parts, other = behind(parts, ada, *biases)
    layouts = (mlp_layout, ((3, r), (1, r)))
    fc1, fc2, qkv, proj = call(
        functools.partial(gather_groups, dp, orders, layouts),
        [((height, blocks * d), F32) for layout in layouts for blocks, height in layout],
        [held, other, low] + parts,
        [pltpu.VMEM((size, d), F32) for size in (held.shape[0] * 2, quarter * dp)],
    )
    return [ada, qkv, proj, fc1, fc2], biases


def reduce_whole(plan, mlp, last, mods):
    d, ffb = plan.d, plan.ffb
    fc1_rows, fc2_rows = mlp[: ffb * d], mlp[ffb * d :]

    def unpack(rows, blocks):
        return rows.reshape(blocks, d, d).transpose(1, 0, 2).reshape(d, blocks * d)

    mods = mods[: 7 * plan.group].reshape(plan.group, 7, d)
    cond_act, grad_mod = mods[:, 0], mods[:, 1:].reshape(plan.group, 6 * d)
    ada = jnp.dot(cond_act.T, grad_mod, preferred_element_type=F32)
    misc = last[4 * d : 4 * d + 16]
    grads = (
        ada,
        jnp.sum(grad_mod.astype(F32), axis=0),
        unpack(last[: 3 * d], 3),
        misc[0:2].reshape(-1),
        last[3 * d : 4 * d],
        misc[2],
        unpack(fc1_rows, ffb),
        misc[3 : 3 + ffb].reshape(-1),
        fc2_rows,
        misc[3 + ffb],
    )
    owned = [
        lax.psum_scatter(grad.astype(BF), "fsdp", scatter_dimension=0, tiled=True) for grad in grads
    ]
    return [lax.psum(grad, "dp").astype(F32) for grad in owned]


def shards(
    fsdp,
    dp,
    latents,
    condition,
    cotangent,
    counts,
    ada_weight,
    ada_bias,
    qkv_weight,
    qv_bias,
    proj_weight,
    proj_bias,
    fc1_weight,
    fc1_bias,
    fc2_weight,
    fc2_bias,
):
    plan = Plan(latents, ada_weight, fc1_weight, fsdp, dp)
    d, n, group, ff, r = plan.d, plan.tokens, plan.group, plan.ff, plan.rows
    x = latents.reshape(n, d)
    cot = cotangent.reshape(n, d)
    cond = condition.reshape(group, d)
    biases = [ada_bias, qv_bias, proj_bias, fc1_bias, fc2_bias]
    weights = [ada_weight, qkv_weight, proj_weight, fc1_weight]
    third = fc2_weight
    if not plan.direct:
        def whole(v):
            return lax.all_gather(v, "fsdp", axis=0, tiled=True)

        biases, weights, third = [whole(v) for v in biases], [whole(v) for v in weights], whole(third)
    lengths = [bias.shape[0] for bias in biases]
    width = -(-sum(lengths) // 1024) * 1024
    line = sum(
        jnp.pad(bias.astype(F32), (sum(lengths[:i]), width - sum(lengths[: i + 1])))
        for i, bias in enumerate(biases)
    )
    first, second, live = call(
        functools.partial(pack_weights, plan),
        [((5 * r + 16, d), BF), (((2 * plan.ffb + 5) * r, d), BF), ((group, 128), F32)],
        weights + [third, line.reshape(1, -1), counts.T],
        [pltpu.VMEM((16, d), F32), pltpu.SemaphoreType.DMA((plan.ffb + 11,))],
        smem=(6,),
        far=(0, 1, 2, 3, 4),
        limit=PACK_LIMIT,
        micros=1.0,
    )
    first = gather_cores(plan, gather_chips(plan, first))
    second = gather_chips(plan, second)

    projected, mixed, mod_first, bias, qkv, ada_first, x_near, cot_near = call(
        functools.partial(attn_forward, plan),
        [
            ((n, 3 * d), BF),
            ((n, d), BF),
            ((group, 2 * d), F32),
            ((16, d), F32),
            ((d, 3 * d), BF),
            ((d, 2 * d), BF),
            ((n, d), BF),
            ((n, d), BF),
        ],
        [x, cond, cot] + first,
        [
            pltpu.VMEM((d, 3 * d), BF),
            pltpu.VMEM((d, 2 * d), BF),
            pltpu.SemaphoreType.DMA((2,)),
        ],
        far_outs=(4, 5),
        room=5,
        micros=4,
    )
    shards = gather_joined(plan, mod_first, second)
    halves = len(plan.peers) if plan.direct else 1
    sides = plan.sides
    outs = call(
        functools.partial(mlp_both, plan),
        [((halves * 2 * plan.ffb * r, d), BF)] * sides
        + [
            ((n, ff), BF),
            ((n, ff), BF),
            ((n, d), BF),
            ((n, d), F32),
            ((n, d), F32),
            ((group, 4 * d), F32),
            ((d, ff), BF),
            ((ff, d), BF),
            ((n, d), BF),
            ((n, d), BF),
            ((d, d), BF),
            ((d, 4 * d), BF),
        ],
        [live, x_near, cot_near, mixed, bias, cond] + shards,
        [
            pltpu.VMEM((n, d), BF),
            pltpu.VMEM((d, n), BF),
            pltpu.VMEM((d, ff), BF),
            pltpu.VMEM((ff, d), BF),
            pltpu.VMEM((d, 4 * d), BF),
            pltpu.SemaphoreType.DMA((1,)),
        ],
        far_outs=(sides + 11,),
        room=5,
        micros=10,
    )
    mlp_chunk = outs[:sides]
    (act, grad_pre, grad_out, middle, attn_out, mod_second, fc1, fc2, mixed, cot_near, proj,
     ada_second) = outs[sides:]
    block_out, grad_gate = call(
        functools.partial(mlp_close, plan),
        [((n, d), BF), ((group, d), F32)],
        [live, cot_near, act, fc2, middle, mod_second, bias],
        room=5,
        micros=1.5,
    )
    if plan.direct:
        mlp_own, mlp_pieces = chunk_siblings(plan, *mlp_chunk, grad_gate)
        (grad_pre,) = behind([grad_pre], mlp_own)
    grad_mixed, grad_middle, grad_proj, misc, grad_mod = call(
        functools.partial(mlp_back, plan),
        [
            ((n, d), BF),
            ((n, d), F32),
            ((d, d), BF),
            ((16, d), F32),
            ((group, 3 * d), F32),
        ],
        [live, cot_near, grad_pre, fc1, middle, attn_out, mod_second, mixed, proj, grad_out],
        [pltpu.VMEM((n, d), BF)],
        room=5,
        micros=3,
    )
    parts = []
    for g in range(group):
        parts += call(
            functools.partial(attn_back, plan, g),
            [((plan.seq, 3 * d), BF)],
            [projected, behind([grad_mixed], *parts)[0]],
            room=5,
            micros=3.3,
        )
    latents_grad, mods, attn_in = call(
        functools.partial(attn_close, plan),
        [((n, d), BF), ((MOD_ROWS, d), BF), ((n, d), BF)],
        [x, cond, grad_middle, qkv, mod_first, grad_mod, grad_gate] + parts,
        [pltpu.VMEM((MOD_ROWS, d), F32), pltpu.VMEM((group, d), F32)],
        room=5,
        micros=2,
    )
    (cond_grad,) = call(
        functools.partial(cond_back, plan),
        [((group, d), BF)],
        [cond, mods, ada_first, ada_second],
        micros=2,
    )
    if plan.direct:
        parts = behind(parts, *mlp_pieces)
    last_chunk = call(
        functools.partial(attn_grads, plan),
        [((halves * (4 * r + 16), d), BF)] * sides,
        [attn_in, grad_proj, misc] + parts,
        [
            pltpu.VMEM((d, 3 * d), BF),
            pltpu.VMEM((16, d), F32),
            pltpu.VMEM((d, n), BF),
        ],
        room=5,
        micros=1.5,
    )
    if plan.direct:
        layout = ((plan.ffb, r), (1, plan.ffb * r))
        weight_grads, bias_grads = finish(
            plan, mlp_own, mlp_pieces, layout, *last_chunk, mods, cond_grad
        )
        grads = [grad for pair in zip(weight_grads, bias_grads) for grad in pair]
    else:
        grads = reduce_whole(plan, mlp_chunk[0], last_chunk[0], mods)
    return (
        block_out.reshape(latents.shape),
        latents_grad.reshape(latents.shape),
        cond_grad.reshape(condition.shape),
        *grads,
    )


def solution(mesh):
    tokens = P(None, ("dp", "fsdp"), None, None)
    per_latent = P(None, ("dp", "fsdp"), None)
    weight, bias = P("fsdp", None), P("fsdp")
    in_specs = (tokens, per_latent, tokens, P(None, ("dp", "fsdp"))) + (weight, bias) * 5
    out_specs = (tokens, tokens, per_latent) + (weight, bias) * 5
    body = functools.partial(shards, mesh.shape["fsdp"], mesh.shape["dp"])
    return jax.shard_map(body, mesh=mesh, in_specs=in_specs, out_specs=out_specs, check_vma=False)
```

```python
import functools
import math

import jax
import jax.numpy as jnp
from jax import lax
from jax.experimental import pallas as pl
from jax.experimental.pallas import tpu as pltpu
from jax.sharding import PartitionSpec as P

HEADS = 6
EPSILON = 1e-06
BF = jnp.bfloat16
F32 = jnp.float32
SQRT_2_PI = 0.7978845608028654
CUBIC = 0.044715
MARGIN = 0.0
PACK_LIMIT = 56 * 1024 * 1024
MOD_USED = 14
MOD_ROWS = 16


def dot(a, b):
    return lax.dot_general(a, b, (((1,), (0,)), ((), ())), preferred_element_type=F32)


def dot_nt(a, b):
    return lax.dot_general(a, b, (((1,), (1,)), ((), ())), preferred_element_type=F32)


def dot_tn(a, b):
    return lax.dot_general(a, b, (((0,), (0,)), ((), ())), preferred_element_type=F32)


def normalize(inputs):
    center = inputs - jnp.mean(inputs, axis=-1, keepdims=True)
    spread = jnp.mean(center * center, axis=-1, keepdims=True)
    inv_root = lax.rsqrt(spread + EPSILON)
    return center * inv_root, inv_root


def norm_back(grad_norm, normed, inv_root):
    first_mean = jnp.mean(grad_norm, axis=-1, keepdims=True)
    second_mean = jnp.mean(grad_norm * normed, axis=-1, keepdims=True)
    return inv_root * (grad_norm - first_mean - normed * second_mean)


def silu(v):
    return v / (1.0 + jnp.exp(-v))


def call(body, outs, ins, scratch=(), smem=(), far=(), far_outs=(), room=2, micros=0.2, limit=0):
    specs = [
        pl.BlockSpec(
            memory_space=pltpu.SMEM if i in smem else pltpu.HBM if i in far else pltpu.VMEM
        )
        for i in range(len(ins))
    ]
    def size(shape, kind):
        width = -(-shape[-1] // 128) * 128
        return math.prod(shape[:-1]) * width * jnp.dtype(kind).itemsize

    held = sum(size(v.shape, v.dtype) for v in scratch if len(v.shape) > 1)
    held += MARGIN * (sum(size(v.shape, v.dtype) for v in ins) + sum(size(*out) for out in outs))
    made = pl.pallas_call(
        body,
        out_shape=[jax.ShapeDtypeStruct(shape, kind) for shape, kind in outs],
        in_specs=specs,
        out_specs=[
            pl.BlockSpec(memory_space=pltpu.HBM if i in far_outs else pltpu.VMEM)
            for i in range(len(outs))
        ],
        scratch_shapes=list(scratch),
        compiler_params=pltpu.CompilerParams(vmem_limit_bytes=limit or int(held) + room * 1024 * 1024),
        cost_estimate=pl.CostEstimate(
            flops=0, bytes_accessed=int(micros * 3.69e6), transcendentals=0
        ),
    )(*ins)
    return list(made)


class Plan:
    def __init__(self, latents, ada_weight, fc1_weight, fsdp, dp):
        self.fsdp, self.dp = fsdp, dp
        self.mb, self.slots, self.seq, self.d = latents.shape
        self.group = self.mb * self.slots
        self.tokens = self.group * self.seq
        self.ff = fc1_weight.shape[1]
        self.ffb = self.ff // self.d
        own = ada_weight.shape[0]
        power = fsdp >= 2 and fsdp & (fsdp - 1) == 0 and dp & (dp - 1) == 0 and dp >= 2
        self.direct = power and own % 16 == 0 and (own * 4) % (16 * dp) == 0 and self.group == 2
        self.shards = fsdp if self.direct else 1
        self.rows = own if self.direct else self.d
        self.peers = [2 * m for m in range(fsdp // 2)]
        self.sides = 2 if self.direct else 1
        self.bias_rows = [6, 2, 1, self.ffb, 1]


def shard_of(plan, k):
    if not plan.direct:
        return 0
    return lax.axis_index("fsdp") ^ k


def pack_weights(
    plan, ada, qkv, proj, fc1, fc2, biases, counts, first, second, live, rows_s, sems
):
    d, r = plan.d, plan.rows

    def cut(ref, start, stop):
        return [ref.at[:, pl.ds(j * d, d)] for j in range(start, stop)]

    copies = []
    for packed, blocks in (
        (first, cut(qkv, 0, 3) + cut(ada, 0, 2)),
        (second, cut(fc1, 0, plan.ffb) + cut(ada, 2, 6) + [proj, fc2]),
    ):
        at = 0
        for block in blocks:
            target = packed.at[pl.ds(at, block.shape[0]), :]
            copies.append(pltpu.make_async_copy(block, target, sems.at[len(copies)]))
            at += block.shape[0]
    for copy in copies:
        copy.start()
    for g in range(plan.group):
        alive = jnp.where(g % plan.slots < counts[0, g // plan.slots], 1.0, 0.0).astype(F32)
        live[g : g + 1, :] = jnp.full((1, 128), alive)
    rows_s[...] = jnp.zeros_like(rows_s)
    line = jnp.broadcast_to(biases[...], (8, biases.shape[1]))
    at, start = 0, 0
    for count in plan.bias_rows:
        width = max(count * d, line.shape[1])
        wide = line
        if width > line.shape[1]:
            wide = jnp.concatenate([line, jnp.zeros((8, width - line.shape[1]), F32)], axis=1)
        if plan.direct:
            own = count * d // plan.fsdp
            me = lax.axis_index("fsdp")
            wide = pltpu.roll(wide, lax.rem(me * own + (width - start), width), 1)
            lane = lax.broadcasted_iota(jnp.int32, (8, width), 1)
            wide = jnp.where((lane >= me * own) & (lane < (me + 1) * own), wide, 0.0)
            start += own
        else:
            wide = line[:, start : start + count * d]
            start += count * d
        for j in range(count):
            rows_s[at + j : at + j + 1, :] = wide[0:1, j * d : (j + 1) * d]
        at += count
    first[5 * r : 5 * r + 16, :] = rows_s[...].astype(BF)
    for copy in copies:
        copy.wait()


def join(*refs):
    out, at = refs[-1], 0
    for ref in refs[:-1]:
        out[at : at + ref.shape[0], :] = ref[...]
        at += ref.shape[0]


def join_after(gate, *refs):
    del gate
    join(*refs)


def views(plan, joined):
    if not plan.direct:
        return joined
    found = []
    rows = sum(ref.shape[0] for ref in joined) // plan.shards
    for mine, sibling in zip(joined[::2], joined[1::2]):
        for m in range(mine.shape[0] // rows):
            found += [ref.at[pl.ds(m * rows, rows), :] for ref in (mine, sibling)]
    return found


def place(plan, shards, block, target, column):
    d, r = plan.d, plan.rows
    for k, shard in enumerate(shards):
        at = pl.multiple_of(shard_of(plan, k) * r, 16)
        target[pl.ds(at, r), column * d : (column + 1) * d] = shard[block * r : (block + 1) * r, :]


def emit(plan, grads, blocks, send, keep, rows):
    r = plan.rows
    for name, xor in ((keep, 0),) if send is None else ((send, 1), (keep, 0)):
        for m in range(len(plan.peers) if plan.direct else 1):
            owner = shard_of(plan, 2 * m + xor)
            for at, ref, column, stride, offset in blocks:
                start = pl.multiple_of(owner * (stride * r) + offset * r, 16)
                name[m * rows + at * r : m * rows + (at + 1) * r, :] = ref[
                    pl.ds(start, r), column * plan.d : (column + 1) * plan.d
                ]


def attn_forward(plan, *refs):
    s = plan.shards
    x, cond, cot = refs[:3]
    shards = refs[3 : 3 + s]
    (projected, mixed, modulation, bias, qkv_out, ada_out, x_out, cot_out, qkv, ada,
     sems) = refs[3 + s :]
    x_out[...] = x[...]
    cot_out[...] = cot[...]
    d, length, r = plan.d, plan.seq, plan.rows
    for j in range(3):
        place(plan, shards, j, qkv, j)
    for j in range(2):
        place(plan, shards, 3 + j, ada, j)
    copies = [
        pltpu.make_async_copy(qkv, qkv_out, sems.at[0]),
        pltpu.make_async_copy(ada, ada_out, sems.at[1]),
    ]
    for copy in copies:
        copy.start()
    total = shards[0][5 * r : 5 * r + 16, :].astype(F32)
    for shard in shards[1:]:
        total = total + shard[5 * r : 5 * r + 16, :].astype(F32)
    bias[...] = total
    cond_act = silu(cond[...].astype(F32)).astype(BF)
    mod = dot(cond_act, ada[...])
    for j in range(2):
        modulation[:, j * d : (j + 1) * d] = mod[:, j * d : (j + 1) * d] + bias[j : j + 1, :]
    left = lax.broadcasted_iota(jnp.int32, (1, 128), 1) < 64

    def latent(g, carry):
        at = pl.ds(pl.multiple_of(g * length, length), length)
        shift = modulation[pl.ds(g, 1), 0:d]
        scale = modulation[pl.ds(g, 1), d : 2 * d]
        normed, _ = normalize(x[at, :].astype(F32))
        rounded = (normed * (1.0 + scale) + shift).astype(BF)
        for j in range(3):
            piece = dot(rounded, qkv[:, j * d : (j + 1) * d])
            if j != 1:
                piece = piece + bias[6 + j // 2 : 7 + j // 2, :]
            projected[at, j * d : (j + 1) * d] = piece.astype(BF)
        for pair in range(HEADS // 2):
            lanes = slice(pair * 128, (pair + 1) * 128)
            q = projected[at, lanes] * jnp.asarray(0.125, BF)
            k = projected[at, d + pair * 128 : d + (pair + 1) * 128]
            v = projected[at, 2 * d + pair * 128 : 2 * d + (pair + 1) * 128]
            halves = []
            for side in (left, ~left):
                scores = dot_nt(jnp.where(side, q, jnp.zeros_like(q)), k)
                exponent = jnp.exp(scores - jnp.max(scores, axis=-1, keepdims=True))
                probs = exponent * (1.0 / jnp.sum(exponent, axis=-1, keepdims=True))
                halves.append(dot(probs.astype(BF), v))
            mixed[at, lanes] = jnp.where(left, halves[0], halves[1]).astype(BF)
        return carry

    lax.fori_loop(0, plan.group, latent, 0)
    for copy in copies:
        copy.wait()


def mlp_both(plan, *refs):
    s = 4 if plan.direct else 1
    lives, x, cot, mixed, bias, cond = refs[:6]
    shards, refs = views(plan, refs[6 : 6 + s]), refs[6 + s :]
    (send, refs) = (refs[0], refs[1:]) if plan.direct else (None, refs)
    (keep, act, grad_pre, grad_out, middle, attn_out, modulation, fc1, fc2, mixed_out, cot_out,
     proj, ada_out, mlp_in, turned, grad_fc1, grad_fc2, ada, sems) = refs
    mixed_out[...] = mixed[...]
    cot_out[...] = cot[...]
    d, length, ffb, r = plan.d, plan.seq, plan.ffb, plan.rows
    r4 = r * ffb
    for j in range(ffb):
        place(plan, shards, j, fc1, j)
    for k, shard in enumerate(shards):
        at = pl.multiple_of(shard_of(plan, k) * r4, 16)
        fc2[pl.ds(at, r4), :] = shard[(ffb + 5) * r : (ffb + 5) * r + r4, :]
    for j in range(4):
        place(plan, shards, ffb + j, ada, j)
    copy = pltpu.make_async_copy(ada, ada_out, sems.at[0])
    copy.start()
    place(plan, shards, ffb + 4, proj, 0)
    mod = dot(silu(cond[...].astype(F32)).astype(BF), ada[...])
    for j in range(4):
        modulation[:, j * d : (j + 1) * d] = mod[:, j * d : (j + 1) * d] + bias[2 + j : 3 + j, :]

    def latent(g, carry):
        at = pl.ds(pl.multiple_of(g * length, length), length)
        gate_attn, shift, scale, gate = [
            modulation[pl.ds(g, 1), j * d : (j + 1) * d] for j in range(4)
        ]
        live = lives[pl.ds(g, 1), 0:1]
        out = dot(mixed[at, :], proj[...]) + bias[8:9, :]
        attn_out[at, :] = out
        mid = x[at, :].astype(F32) + gate_attn * out
        middle[at, :] = mid
        normed, _ = normalize(mid)
        mlp_in[at, :] = (normed * (1.0 + scale) + shift).astype(BF)
        grad_out[at, :] = ((gate * live) * cot[at, :].astype(F32)).astype(BF)
        return carry

    lax.fori_loop(0, plan.group, latent, 0)
    turned[...] = mlp_in[...].T
    step = 256
    for c in range(plan.ff // step):
        cols = slice(c * step, (c + 1) * step)
        pieces = []
        start, rest = c * step, step
        while rest:
            row, lane = divmod(start, d)
            width = min(rest, d - lane)
            pieces.append(bias[9 + row : 10 + row, lane : lane + width])
            start, rest = start + width, rest - width
        shift = pieces[0] if len(pieces) == 1 else jnp.concatenate(pieces, axis=1)
        pre = dot(mlp_in[...], fc1[:, cols]) + shift
        square = pre * pre
        bend = jnp.tanh(pre * (SQRT_2_PI + (SQRT_2_PI * CUBIC) * square))
        half = 0.5 + 0.5 * bend
        value = (pre * half).astype(BF)
        act[:, cols] = value
        slope = (0.5 * SQRT_2_PI) + (1.5 * SQRT_2_PI * CUBIC) * square
        gelu_back = half + pre * (1.0 - bend * bend) * slope
        grad = (dot_nt(grad_out[...], fc2[cols, :]) * gelu_back).astype(BF)
        grad_pre[:, cols] = grad
        grad_fc2[cols, :] = dot_tn(value, grad_out[...]).astype(BF)
        grad_fc1[:, cols] = dot(turned[...], grad).astype(BF)
    blocks = [(j, grad_fc1, j, 1, 0) for j in range(ffb)]
    blocks += [(ffb + j, grad_fc2, 0, ffb, j) for j in range(ffb)]
    emit(plan, None, blocks, send, keep, 2 * r4)
    copy.wait()


def mlp_close(plan, lives, cot, act, fc2, middle, modulation, bias, block_out, grad_gate):
    d, length = plan.d, plan.seq

    def latent(g, carry):
        at = pl.ds(pl.multiple_of(g * length, length), length)
        gate = modulation[pl.ds(g, 1), 3 * d : 4 * d]
        live = lives[pl.ds(g, 1), 0:1]
        mlp_out = dot(act[at, :], fc2[...]) + bias[9 + plan.ffb : 10 + plan.ffb, :]
        block_out[at, :] = (live * (middle[at, :] + gate * mlp_out)).astype(BF)
        upstream = cot[at, :].astype(F32) * live
        grad_gate[pl.ds(g, 1), :] = jnp.sum(upstream * mlp_out, axis=0, keepdims=True)
        return carry

    lax.fori_loop(0, plan.group, latent, 0)


def mlp_back(plan, lives, cot, grad_pre, fc1, middle, attn_out, modulation, mixed, proj, grad_out,
             grad_mixed, grad_middle, grad_proj, misc, grad_mod, grad_gates):
    d, length = plan.d, plan.seq
    misc[...] = jnp.zeros_like(misc)
    sums = jnp.sum(grad_pre[...].astype(F32), axis=0, keepdims=True)
    for j in range(plan.ffb):
        misc[3 + j : 4 + j, :] = sums[:, j * d : (j + 1) * d]
    misc[3 + plan.ffb : 4 + plan.ffb, :] = jnp.sum(
        grad_out[...].astype(F32), axis=0, keepdims=True
    )

    def latent(g, carry):
        at = pl.ds(pl.multiple_of(g * length, length), length)
        gate_attn, _, scale = [modulation[pl.ds(g, 1), j * d : (j + 1) * d] for j in range(3)]
        live = lives[pl.ds(g, 1), 0:1]
        upstream = cot[at, :].astype(F32) * live
        normed, rstd = normalize(middle[at, :])
        grad_in = dot_nt(grad_pre[at, :], fc1[...])
        grad_mid = upstream + norm_back(grad_in * (1.0 + scale), normed, rstd)
        grad_middle[at, :] = grad_mid
        rounded = (gate_attn * grad_mid).astype(BF)
        grad_gates[at, :] = rounded
        grad_mixed[at, :] = dot_nt(rounded, proj[...]).astype(BF)
        pieces = [grad_mid * attn_out[at, :], grad_in, grad_in * normed]
        for j, piece in enumerate(pieces):
            grad_mod[pl.ds(g, 1), j * d : (j + 1) * d] = jnp.sum(piece, axis=0, keepdims=True)
        return carry

    lax.fori_loop(0, plan.group, latent, 0)
    misc[2:3, :] = jnp.sum(grad_gates[...].astype(F32), axis=0, keepdims=True)
    grad_proj[...] = dot_tn(mixed[...], grad_gates[...]).astype(BF)


def attn_core_back(plan, at, projected, grad_mixed, out, where):
    d = plan.d
    left = lax.broadcasted_iota(jnp.int32, (1, 128), 1) < 64
    for pair in range(HEADS // 2):
        lanes = slice(pair * 128, (pair + 1) * 128)
        q = projected[at, lanes] * jnp.asarray(0.125, BF)
        k = projected[at, d + pair * 128 : d + (pair + 1) * 128]
        v = projected[at, 2 * d + pair * 128 : 2 * d + (pair + 1) * 128]
        gm = grad_mixed[at, lanes]
        grads_q, grads_k, grads_v = [], [], []
        for side in (left, ~left):
            scores = dot_nt(jnp.where(side, q, jnp.zeros_like(q)), k)
            exponent = jnp.exp(scores - jnp.max(scores, axis=-1, keepdims=True))
            probs = exponent * (1.0 / jnp.sum(exponent, axis=-1, keepdims=True))
            grad_probs = dot_nt(jnp.where(side, gm, jnp.zeros_like(gm)), v)
            inner = jnp.sum(probs * grad_probs, axis=-1, keepdims=True)
            grad_scores = (probs * (grad_probs - inner)).astype(BF)
            grads_q.append(dot(grad_scores, k))
            grads_k.append(dot_tn(grad_scores, q))
            grads_v.append(dot_tn(probs.astype(BF), gm))
        for j, (pieces, factor) in enumerate(((grads_q, 0.125), (grads_k, 1.0), (grads_v, 1.0))):
            merged = jnp.where(left, pieces[0], pieces[1]) * factor
            out[where, j * d + pair * 128 : j * d + (pair + 1) * 128] = merged.astype(BF)


def attn_back(plan, g, projected, grad_mixed, out):
    at = slice(g * plan.seq, (g + 1) * plan.seq)
    attn_core_back(plan, at, projected, grad_mixed, out, slice(0, plan.seq))


def attn_close(plan, *refs):
    (x, cond, grad_middle, qkv, modulation, grad_mod, grad_gate) = refs[:7]
    parts, outs = refs[7 : 7 + plan.group], refs[7 + plan.group :]
    latents_grad, mods, attn_in, rows_s, cond_s = outs
    d, length = plan.d, plan.seq
    rows_s[...] = jnp.zeros_like(rows_s)
    cond_s[...] = silu(cond[...].astype(F32))
    for g, part in enumerate(parts):
        at = slice(g * length, (g + 1) * length)
        shift = modulation[g : g + 1, 0:d]
        scale = modulation[g : g + 1, d : 2 * d]
        normed, rstd = normalize(x[at, :].astype(F32))
        attn_in[at, :] = (normed * (1.0 + scale) + shift).astype(BF)
        grad_in = dot_nt(part[...], qkv[...])
        grad = grad_middle[at, :] + norm_back(grad_in * (1.0 + scale), normed, rstd)
        latents_grad[at, :] = grad.astype(BF)
        pieces = [cond_s[g : g + 1, :], jnp.sum(grad_in, axis=0, keepdims=True)]
        pieces += [jnp.sum(grad_in * normed, axis=0, keepdims=True)]
        pieces += [grad_mod[g : g + 1, j * d : (j + 1) * d] for j in range(3)]
        pieces += [grad_gate[g : g + 1, :]]
        for j, piece in enumerate(pieces):
            rows_s[g * 7 + j : g * 7 + j + 1, :] = piece
    mods[...] = rows_s[...].astype(BF)


def attn_grads(plan, *refs):
    attn_in, grad_proj, misc = refs[:3]
    parts, outs = refs[3 : 3 + plan.group], refs[3 + plan.group :]
    (send, outs) = (outs[0], outs[1:]) if plan.direct else (None, outs)
    keep, grad_qkv, misc_s, turned = outs
    d, length, r = plan.d, plan.seq, plan.rows
    misc_s[...] = misc[...]
    turned[...] = attn_in[...].T
    for j in range(3):
        cols = slice(j * d, (j + 1) * d)
        total, sums = 0.0, 0.0
        for g, part in enumerate(parts):
            piece = part[:, cols]
            total = total + dot(turned[:, g * length : (g + 1) * length], piece)
            sums = sums + jnp.sum(piece.astype(F32), axis=0, keepdims=True)
        grad_qkv[:, cols] = total.astype(BF)
        if j != 1:
            misc_s[j // 2 : j // 2 + 1, :] = sums
    blocks = [(j, grad_qkv, j, 1, 0) for j in range(3)] + [(3, grad_proj, 0, 1, 0)]
    rows = 4 * r + 16
    emit(plan, None, blocks, send, keep, rows)
    low = misc_s[...].astype(BF)
    for name in (keep,) if send is None else (send, keep):
        for m in range(len(plan.peers) if plan.direct else 1):
            name[m * rows + 4 * r : (m + 1) * rows, :] = low


def cond_back(plan, cond, mods, first, second, grad):
    d = plan.d
    rows = mods[...].astype(F32)
    total = None
    kept = []
    for g in range(plan.group):
        total = jnp.zeros((1, d), F32)
        for j in range(6):
            weight = first[:, j * d : (j + 1) * d] if j < 2 else second[:, (j - 2) * d : (j - 1) * d]
            line = jnp.broadcast_to(rows[g * 7 + 1 + j : g * 7 + 2 + j, :], (8, d)).astype(BF)
            total = total + dot_nt(line, weight)[0:1, :]
        kept.append(total)
    for g in range(plan.group):
        v = cond[g : g + 1, :].astype(F32)
        gate = 1.0 / (1.0 + jnp.exp(-v))
        grad[g : g + 1, :] = (kept[g] * (gate * (1.0 + v * (1.0 - gate)))).astype(BF)


def add_siblings(peers, rows, *refs):
    keep, received, own = refs[:3]
    outs = refs[3:]
    for m in range(peers):
        at = slice(m * rows, (m + 1) * rows)
        total = keep[at, :].astype(F32) + received[at, :].astype(F32)
        if m == 0:
            own[...] = total
        else:
            outs[m - 1][...] = total.astype(BF)


def add_chips(count, dp, quarter, own, *refs):
    received, (mine, sent, total_s) = refs[:count], refs[count:]
    total = own[...]
    for piece in received:
        total = total + piece[...].astype(F32)
    total_s[...] = total
    me = lax.axis_index("dp")
    for j in range(dp):
        part = total_s[pl.ds(pl.multiple_of((me ^ j) * quarter, 16), quarter), :]
        out = sent if j % 2 else mine
        out[j // 2 * quarter : (j // 2 + 1) * quarter, :] = part.astype(out.dtype)


def halve(quarter, held, received, mine, sent):
    for j in range(held.shape[0] // quarter):
        at = slice(j * quarter, (j + 1) * quarter)
        out = sent if j % 2 else mine
        total = held[at, :] + received[at, :].astype(F32)
        out[j // 2 * quarter : (j // 2 + 1) * quarter, :] = total.astype(out.dtype)


def gather_groups(dp, orders, layouts, *refs):
    count = sum(len(order) for order in orders)
    arrays, outs, scratch = list(refs[:count]), list(refs[count : -len(orders)]), refs[-len(orders) :]
    me = lax.axis_index("dp")
    for order, layout, rows_s in zip(orders, layouts, scratch):
        quarter, d = rows_s.shape[0] // dp, rows_s.shape[1]
        for some in order:
            array = arrays.pop(0)
            for i, j in enumerate(some):
                at = pl.multiple_of((me ^ j) * quarter, 16)
                piece = array[i * quarter : (i + 1) * quarter, :]
                rows_s[pl.ds(at, quarter), :] = piece.astype(F32)
        at = 0
        for blocks, rows in layout:
            out = outs.pop(0)
            for j in range(blocks):
                out[:, j * d : (j + 1) * d] = rows_s[at : at + rows, :]
                at += rows


def last_sibling(peers, rows, keep, received, mods, own, *outs):
    for m in range(peers):
        at = slice(m * rows, (m + 1) * rows)
        total = keep[at, :].astype(F32) + received[at, :].astype(F32)
        if m == 0:
            own[0:rows, :] = total
            own[rows : rows + MOD_ROWS, :] = mods[...].astype(F32)
        else:
            outs[m - 1][0:rows, :] = total.astype(BF)
            outs[m - 1][rows : rows + MOD_ROWS, :] = mods[...]


def last_chips(count, dp, quarter, rows, own, *refs):
    received, mine, outs = refs[:count], refs[count], refs[count + 1 : count + dp]
    total_s, tail_s = refs[count + dp :]
    tail_s[...] = jnp.zeros_like(tail_s)
    total = own[0:rows, :]
    for piece in received:
        total = total + piece[0:rows, :].astype(F32)
    total_s[...] = total[: rows - 16]
    for i, piece in enumerate((own,) + received):
        lines = piece[rows:, :].astype(F32)
        tail_s[i * MOD_USED : (i + 1) * MOD_USED, :] = lines[0:MOD_USED]
    end = (count + 1) * MOD_USED
    tail_s[end : end + 8, :] = total[rows - 16 : rows - 8]
    me = lax.axis_index("dp")
    for j in range(dp):
        part = total_s[pl.ds(pl.multiple_of((me ^ j) * quarter, 16), quarter), :]
        name = mine if j == 0 else outs[j - 1]
        name[0:quarter, :] = part.astype(name.dtype)
        name[quarter:, :] = tail_s[...].astype(name.dtype)


def add_two(first, second, out):
    out[...] = (first[...] + second[...].astype(F32)).astype(BF)


def add_groups(dp, quarter, *refs):
    pieces, (low, mods) = refs[:dp], refs[dp:]
    total = pieces[0][0:quarter, :]
    for piece in pieces[1:]:
        total = total + piece[0:quarter, :].astype(F32)
    low[...] = total.astype(BF)
    each = pieces[0].shape[0] - quarter
    for j, piece in enumerate(pieces):
        mods[j * each : (j + 1) * each, :] = piece[quarter:, :].astype(BF)


def ada_grads(plan, quarter, *refs):
    dp, d, r = plan.dp, plan.d, plan.rows
    pieces, mods = refs[:dp], refs[dp : dp + 2]
    ada, ada_bias, qv, proj, fc1, fc2 = refs[dp + 2 : dp + 8]
    rows_s, turned_s = refs[dp + 8 :]
    block = pieces[0].shape[0] - quarter
    used = len(plan.peers) * MOD_USED
    each = dp * block
    total = pieces[0][quarter + used : quarter + used + 8, :].astype(F32)
    for piece in pieces[1:]:
        total = total + piece[quarter:, :].astype(F32)[used : used + 8]
    for j, rows in enumerate(mods):
        rows_s[j * each : (j + 1) * each, :] = rows[...]
    count = 2 * each
    row = lax.broadcasted_iota(jnp.int32, (count, count), 0)
    column = lax.broadcasted_iota(jnp.int32, (count, count), 1)
    slot = row % block
    pick = ((column == row - slot % 7) & (slot < used)).astype(BF)
    turned_s[...] = dot(pick, rows_s[...]).T
    me = lax.axis_index("fsdp")
    mine = turned_s[pl.ds(pl.multiple_of(me * r, 16), r), :].astype(BF)
    lane = lax.broadcasted_iota(jnp.int32, (1, count), 1) % block
    tall = lax.broadcasted_iota(jnp.int32, (count, 1), 0) % block
    values = rows_s[...]
    sums = []
    for j in range(6):
        here = (lane % 7 == 1 + j) & (lane < used)
        ada[:, j * d : (j + 1) * d] = dot(jnp.where(here, mine, jnp.zeros_like(mine)), values)
        there = (tall % 7 == 1 + j) & (tall < used)
        sums.append(
            jnp.sum(jnp.where(there, values.astype(F32), 0.0), axis=0, keepdims=True)
        )
    lists = [
        (ada_bias, sums),
        (qv, [total[0:1], total[1:2]]),
        (proj, [total[2:3]]),
        (fc1, [total[3 + j : 4 + j] for j in range(plan.ffb)]),
        (fc2, [total[3 + plan.ffb : 4 + plan.ffb]]),
    ]
    for out, lines in lists:
        wide = lines[0] if len(lines) == 1 else jnp.concatenate(lines, axis=1)
        width = wide.shape[1]
        own = width // plan.fsdp
        wide = jnp.broadcast_to(wide, (8, width))
        wide = pltpu.roll(wide, lax.rem(width - me * own, width), 1)
        out[...] = wide[0:1, :own]


def swap(plan, value, k, axis="fsdp"):
    size = plan.fsdp if axis == "fsdp" else plan.dp
    return lax.ppermute(value, axis, [(i, i ^ k) for i in range(size)])


def behind(values, *gates):
    gates = [gate for gate in gates if gate is not None]
    return list(lax.optimization_barrier((tuple(values), tuple(gates)))[0])


def gather_chips(plan, value):
    if not plan.direct:
        return [value]
    return [value] + [swap(plan, value, k) for k in plan.peers[1:]]


def gather_joined(plan, gate, chips):
    if not plan.direct:
        return chips
    joined = []
    count = len(chips) // 2
    for some in (chips[:count], chips[count:]):
        shape = (sum(v.shape[0] for v in some), plan.d)
        (mine,) = call(join_after, [(shape, BF)], [gate] + some, micros=0.4)
        joined += [mine, swap(plan, mine, 1)]
    return joined


def gather_cores(plan, chips):
    if not plan.direct:
        return chips
    cores = [swap(plan, shard, 1) for shard in chips]
    return [shard for pair in zip(chips, cores) for shard in pair]


def chunk_siblings(plan, send, keep, gate):
    d, peers = plan.d, len(plan.peers)
    rows = keep.shape[0] // peers
    received = swap(plan, send, 1)
    keep, received = behind([keep, received], gate)
    own, *pieces = call(
        functools.partial(add_siblings, peers, rows),
        [((rows, d), F32)] + [((rows, d), BF)] * (peers - 1),
        [keep, received],
    )
    return own, [swap(plan, piece, k) for piece, k in zip(pieces, plan.peers[1:])]


def chunk_chips(plan, own, pieces):
    d, dp = plan.d, plan.dp
    rows = own.shape[0]
    mine, sent = call(
        functools.partial(add_chips, len(pieces), dp, rows // dp),
        [((rows // 2, d), F32), ((rows // 2, d), BF)],
        [own] + pieces,
        [pltpu.VMEM((rows, d), F32)],
    )
    return mine, swap(plan, sent, 1, "dp")


def chunk_halves(plan, mine, received):
    dp, step = plan.dp, 2
    quarter = 2 * mine.shape[0] // dp
    while mine.shape[0] > quarter:
        shape = (mine.shape[0] // 2, plan.d)
        mine, sent = call(
            functools.partial(halve, quarter), [(shape, F32), (shape, BF)], [mine, received]
        )
        received, step = swap(plan, sent, step, "dp"), 2 * step
    return mine, received


def finish(plan, mlp_own, mlp_pieces, mlp_layout, send, keep, mods, cond_grad):
    d, dp, peers, r = plan.d, plan.dp, len(plan.peers), plan.rows
    rows = keep.shape[0] // peers
    quarter = (rows - 16) // dp
    received = swap(plan, send, 1)
    mlp_mine, mlp_half = chunk_chips(plan, mlp_own, mlp_pieces)
    received, keep = behind([received, keep], mlp_mine)
    mlp_mine, mlp_half = chunk_halves(plan, mlp_mine, mlp_half)
    long = rows + MOD_ROWS
    own, *pieces = call(
        functools.partial(last_sibling, peers, rows),
        [((long, d), F32)] + [((long, d), BF)] * (peers - 1),
        [keep, received, mods],
    )
    pieces = [swap(plan, piece, k) for piece, k in zip(pieces, plan.peers[1:])]
    pieces = behind(pieces, cond_grad, mlp_half)
    tail = -(-(peers * MOD_USED + 8) // 16) * 16
    mine, *quarters = call(
        functools.partial(last_chips, peers - 1, dp, quarter, rows),
        [((quarter + tail, d), F32)] + [((quarter + tail, d), BF)] * (dp - 1),
        [own] + pieces,
        [pltpu.VMEM((rows - 16, d), F32), pltpu.VMEM((tail, d), F32)],
    )
    quarters = [swap(plan, part, j + 1, "dp") for j, part in enumerate(quarters)]
    mlp_mine, mlp_half = behind([mlp_mine, mlp_half], mine)
    (held,) = call(add_two, [(mlp_mine.shape, BF)], [mlp_mine, mlp_half])
    order, step = [0], dp // 2
    while step > 1:
        found = [held, swap(plan, held, step, "dp")]
        order, step = order + [j ^ step for j in order], step // 2
        (held,) = call(join, [((2 * held.shape[0], d), BF)], found)
    half = dp * tail
    low, mods = call(
        functools.partial(add_groups, dp, quarter),
        [((quarter, d), BF), ((half, d), BF)],
        [mine] + quarters,
    )
    parts = [swap(plan, low, j, "dp") for j in range(1, dp)] + [swap(plan, held, 1, "dp")]
    orders = ((order, [j ^ 1 for j in order]), [[j] for j in range(dp)])
    ada, *biases = call(
        functools.partial(ada_grads, plan, quarter),
        [((r, 6 * d), F32)] + [((1, w * d // plan.fsdp), F32) for w in plan.bias_rows],
        [mine] + quarters + [mods, swap(plan, mods, 1)],
        [pltpu.VMEM((2 * half, d), BF), pltpu.VMEM((d, 2 * half), F32)],
        micros=2,
    )
    biases = [bias.reshape(-1) for bias in biases]
    *parts, other = behind(parts, ada, *biases)
    layouts = (mlp_layout, ((3, r), (1, r)))
    fc1, fc2, qkv, proj = call(
        functools.partial(gather_groups, dp, orders, layouts),
        [((height, blocks * d), F32) for layout in layouts for blocks, height in layout],
        [held, other, low] + parts,
        [pltpu.VMEM((size, d), F32) for size in (held.shape[0] * 2, quarter * dp)],
    )
    return [ada, qkv, proj, fc1, fc2], biases


def reduce_whole(plan, mlp, last, mods):
    d, ffb = plan.d, plan.ffb
    fc1_rows, fc2_rows = mlp[: ffb * d], mlp[ffb * d :]

    def unpack(rows, blocks):
        return rows.reshape(blocks, d, d).transpose(1, 0, 2).reshape(d, blocks * d)

    mods = mods[: 7 * plan.group].reshape(plan.group, 7, d)
    cond_act, grad_mod = mods[:, 0], mods[:, 1:].reshape(plan.group, 6 * d)
    ada = jnp.dot(cond_act.T, grad_mod, preferred_element_type=F32)
    misc = last[4 * d : 4 * d + 16]
    grads = (
        ada,
        jnp.sum(grad_mod.astype(F32), axis=0),
        unpack(last[: 3 * d], 3),
        misc[0:2].reshape(-1),
        last[3 * d : 4 * d],
        misc[2],
        unpack(fc1_rows, ffb),
        misc[3 : 3 + ffb].reshape(-1),
        fc2_rows,
        misc[3 + ffb],
    )
    owned = [
        lax.psum_scatter(grad.astype(BF), "fsdp", scatter_dimension=0, tiled=True) for grad in grads
    ]
    return [lax.psum(grad, "dp").astype(F32) for grad in owned]


def shards(
    fsdp,
    dp,
    latents,
    condition,
    cotangent,
    counts,
    ada_weight,
    ada_bias,
    qkv_weight,
    qv_bias,
    proj_weight,
    proj_bias,
    fc1_weight,
    fc1_bias,
    fc2_weight,
    fc2_bias,
):
    plan = Plan(latents, ada_weight, fc1_weight, fsdp, dp)
    d, n, group, ff, r = plan.d, plan.tokens, plan.group, plan.ff, plan.rows
    x = latents.reshape(n, d)
    cot = cotangent.reshape(n, d)
    cond = condition.reshape(group, d)
    biases = [ada_bias, qv_bias, proj_bias, fc1_bias, fc2_bias]
    weights = [ada_weight, qkv_weight, proj_weight, fc1_weight]
    third = fc2_weight
    if not plan.direct:
        def whole(v):
            return lax.all_gather(v, "fsdp", axis=0, tiled=True)

        biases, weights, third = [whole(v) for v in biases], [whole(v) for v in weights], whole(third)
    lengths = [bias.shape[0] for bias in biases]
    width = -(-sum(lengths) // 1024) * 1024
    line = sum(
        jnp.pad(bias.astype(F32), (sum(lengths[:i]), width - sum(lengths[: i + 1])))
        for i, bias in enumerate(biases)
    )
    first, second, live = call(
        functools.partial(pack_weights, plan),
        [((5 * r + 16, d), BF), (((2 * plan.ffb + 5) * r, d), BF), ((group, 128), F32)],
        weights + [third, line.reshape(1, -1), counts.T],
        [pltpu.VMEM((16, d), F32), pltpu.SemaphoreType.DMA((plan.ffb + 11,))],
        smem=(6,),
        far=(0, 1, 2, 3, 4),
        limit=PACK_LIMIT,
        micros=1.0,
    )
    first = gather_cores(plan, gather_chips(plan, first))
    second = gather_chips(plan, second)

    projected, mixed, mod_first, bias, qkv, ada_first, x_near, cot_near = call(
        functools.partial(attn_forward, plan),
        [
            ((n, 3 * d), BF),
            ((n, d), BF),
            ((group, 2 * d), F32),
            ((16, d), F32),
            ((d, 3 * d), BF),
            ((d, 2 * d), BF),
            ((n, d), BF),
            ((n, d), BF),
        ],
        [x, cond, cot] + first,
        [
            pltpu.VMEM((d, 3 * d), BF),
            pltpu.VMEM((d, 2 * d), BF),
            pltpu.SemaphoreType.DMA((2,)),
        ],
        far_outs=(4, 5),
        room=5,
        micros=4,
    )
    shards = gather_joined(plan, mod_first, second)
    halves = len(plan.peers) if plan.direct else 1
    sides = plan.sides
    outs = call(
        functools.partial(mlp_both, plan),
        [((halves * 2 * plan.ffb * r, d), BF)] * sides
        + [
            ((n, ff), BF),
            ((n, ff), BF),
            ((n, d), BF),
            ((n, d), F32),
            ((n, d), F32),
            ((group, 4 * d), F32),
            ((d, ff), BF),
            ((ff, d), BF),
            ((n, d), BF),
            ((n, d), BF),
            ((d, d), BF),
            ((d, 4 * d), BF),
        ],
        [live, x_near, cot_near, mixed, bias, cond] + shards,
        [
            pltpu.VMEM((n, d), BF),
            pltpu.VMEM((d, n), BF),
            pltpu.VMEM((d, ff), BF),
            pltpu.VMEM((ff, d), BF),
            pltpu.VMEM((d, 4 * d), BF),
            pltpu.SemaphoreType.DMA((1,)),
        ],
        far_outs=(sides + 11,),
        room=5,
        micros=10,
    )
    mlp_chunk = outs[:sides]
    (act, grad_pre, grad_out, middle, attn_out, mod_second, fc1, fc2, mixed, cot_near, proj,
     ada_second) = outs[sides:]
    block_out, grad_gate = call(
        functools.partial(mlp_close, plan),
        [((n, d), BF), ((group, d), F32)],
        [live, cot_near, act, fc2, middle, mod_second, bias],
        room=5,
        micros=1.5,
    )
    if plan.direct:
        mlp_own, mlp_pieces = chunk_siblings(plan, *mlp_chunk, grad_gate)
        (grad_pre,) = behind([grad_pre], mlp_own)
    grad_mixed, grad_middle, grad_proj, misc, grad_mod = call(
        functools.partial(mlp_back, plan),
        [
            ((n, d), BF),
            ((n, d), F32),
            ((d, d), BF),
            ((16, d), F32),
            ((group, 3 * d), F32),
        ],
        [live, cot_near, grad_pre, fc1, middle, attn_out, mod_second, mixed, proj, grad_out],
        [pltpu.VMEM((n, d), BF)],
        room=5,
        micros=3,
    )
    parts = []
    for g in range(group):
        parts += call(
            functools.partial(attn_back, plan, g),
            [((plan.seq, 3 * d), BF)],
            [projected, behind([grad_mixed], *parts)[0]],
            room=5,
            micros=3.3,
        )
    latents_grad, mods, attn_in = call(
        functools.partial(attn_close, plan),
        [((n, d), BF), ((MOD_ROWS, d), BF), ((n, d), BF)],
        [x, cond, grad_middle, qkv, mod_first, grad_mod, grad_gate] + parts,
        [pltpu.VMEM((MOD_ROWS, d), F32), pltpu.VMEM((group, d), F32)],
        room=5,
        micros=2,
    )
    (cond_grad,) = call(
        functools.partial(cond_back, plan),
        [((group, d), BF)],
        [cond, mods, ada_first, ada_second],
        micros=2,
    )
    if plan.direct:
        parts = behind(parts, *mlp_pieces)
    last_chunk = call(
        functools.partial(attn_grads, plan),
        [((halves * (4 * r + 16), d), BF)] * sides,
        [attn_in, grad_proj, misc] + parts,
        [
            pltpu.VMEM((d, 3 * d), BF),
            pltpu.VMEM((16, d), F32),
            pltpu.VMEM((d, n), BF),
        ],
        room=5,
        micros=1.5,
    )
    if plan.direct:
        layout = ((plan.ffb, r), (1, plan.ffb * r))
        weight_grads, bias_grads = finish(
            plan, mlp_own, mlp_pieces, layout, *last_chunk, mods, cond_grad
        )
        grads = [grad for pair in zip(weight_grads, bias_grads) for grad in pair]
    else:
        grads = reduce_whole(plan, mlp_chunk[0], last_chunk[0], mods)
    return (
        block_out.reshape(latents.shape),
        latents_grad.reshape(latents.shape),
        cond_grad.reshape(condition.shape),
        *grads,
    )


def solution(mesh):
    tokens = P(None, ("dp", "fsdp"), None, None)
    per_latent = P(None, ("dp", "fsdp"), None)
    weight, bias = P("fsdp", None), P("fsdp")
    in_specs = (tokens, per_latent, tokens, P(None, ("dp", "fsdp"))) + (weight, bias) * 5
    out_specs = (tokens, tokens, per_latent) + (weight, bias) * 5
    body = functools.partial(shards, mesh.shape["fsdp"], mesh.shape["dp"])
    return jax.shard_map(body, mesh=mesh, in_specs=in_specs, out_specs=out_specs, check_vma=False)
```

```python
import functools
import math

import jax
import jax.numpy as jnp
from jax import lax
from jax.experimental import pallas as pl
from jax.experimental.pallas import tpu as pltpu
from jax.sharding import PartitionSpec as P

HEADS = 6
EPSILON = 1e-06
BF = jnp.bfloat16
F32 = jnp.float32
SQRT_2_PI = 0.7978845608028654
CUBIC = 0.044715
MARGIN = 0.0
PACK_LIMIT = 56 * 1024 * 1024
MOD_USED = 14
MOD_ROWS = 16


def dot(a, b):
    return lax.dot_general(a, b, (((1,), (0,)), ((), ())), preferred_element_type=F32)


def dot_nt(a, b):
    return lax.dot_general(a, b, (((1,), (1,)), ((), ())), preferred_element_type=F32)


def dot_tn(a, b):
    return lax.dot_general(a, b, (((0,), (0,)), ((), ())), preferred_element_type=F32)


def normalize(inputs):
    center = inputs - jnp.mean(inputs, axis=-1, keepdims=True)
    spread = jnp.mean(center * center, axis=-1, keepdims=True)
    inv_root = lax.rsqrt(spread + EPSILON)
    return center * inv_root, inv_root


def norm_back(grad_norm, normed, inv_root):
    first_mean = jnp.mean(grad_norm, axis=-1, keepdims=True)
    second_mean = jnp.mean(grad_norm * normed, axis=-1, keepdims=True)
    return inv_root * (grad_norm - first_mean - normed * second_mean)


def silu(v):
    return v / (1.0 + jnp.exp(-v))


def call(body, outs, ins, scratch=(), smem=(), far=(), far_outs=(), room=2, micros=0.2, limit=0):
    specs = [
        pl.BlockSpec(
            memory_space=pltpu.SMEM if i in smem else pltpu.HBM if i in far else pltpu.VMEM
        )
        for i in range(len(ins))
    ]
    def size(shape, kind):
        width = -(-shape[-1] // 128) * 128
        return math.prod(shape[:-1]) * width * jnp.dtype(kind).itemsize

    held = sum(size(v.shape, v.dtype) for v in scratch if len(v.shape) > 1)
    held += MARGIN * (sum(size(v.shape, v.dtype) for v in ins) + sum(size(*out) for out in outs))
    made = pl.pallas_call(
        body,
        out_shape=[jax.ShapeDtypeStruct(shape, kind) for shape, kind in outs],
        in_specs=specs,
        out_specs=[
            pl.BlockSpec(memory_space=pltpu.HBM if i in far_outs else pltpu.VMEM)
            for i in range(len(outs))
        ],
        scratch_shapes=list(scratch),
        compiler_params=pltpu.CompilerParams(vmem_limit_bytes=limit or int(held) + room * 1024 * 1024),
        cost_estimate=pl.CostEstimate(
            flops=0, bytes_accessed=int(micros * 3.69e6), transcendentals=0
        ),
    )(*ins)
    return list(made)


class Plan:
    def __init__(self, latents, ada_weight, fc1_weight, fsdp, dp):
        self.fsdp, self.dp = fsdp, dp
        self.mb, self.slots, self.seq, self.d = latents.shape
        self.group = self.mb * self.slots
        self.tokens = self.group * self.seq
        self.ff = fc1_weight.shape[1]
        self.ffb = self.ff // self.d
        own = ada_weight.shape[0]
        power = fsdp >= 2 and fsdp & (fsdp - 1) == 0 and dp & (dp - 1) == 0 and dp >= 2
        self.direct = power and own % 16 == 0 and (own * 4) % (16 * dp) == 0 and self.group == 2
        self.shards = fsdp if self.direct else 1
        self.rows = own if self.direct else self.d
        self.peers = [2 * m for m in range(fsdp // 2)]
        self.sides = 2 if self.direct else 1
        self.bias_rows = [6, 2, 1, self.ffb, 1]


def shard_of(plan, k):
    if not plan.direct:
        return 0
    return lax.axis_index("fsdp") ^ k


def pack_weights(
    plan, ada, qkv, proj, fc1, fc2, biases, counts, first, second, live, rows_s, sems
):
    d, r = plan.d, plan.rows

    def cut(ref, start, stop):
        return [ref.at[:, pl.ds(j * d, d)] for j in range(start, stop)]

    copies = []
    for packed, blocks in (
        (first, cut(qkv, 0, 3) + cut(ada, 0, 2)),
        (second, cut(fc1, 0, plan.ffb) + cut(ada, 2, 6) + [proj, fc2]),
    ):
        at = 0
        for block in blocks:
            target = packed.at[pl.ds(at, block.shape[0]), :]
            copies.append(pltpu.make_async_copy(block, target, sems.at[len(copies)]))
            at += block.shape[0]
    for copy in copies:
        copy.start()
    for g in range(plan.group):
        alive = jnp.where(g % plan.slots < counts[0, g // plan.slots], 1.0, 0.0).astype(F32)
        live[g : g + 1, :] = jnp.full((1, 128), alive)
    rows_s[...] = jnp.zeros_like(rows_s)
    line = jnp.broadcast_to(biases[...], (8, biases.shape[1]))
    at, start = 0, 0
    for count in plan.bias_rows:
        width = max(count * d, line.shape[1])
        wide = line
        if width > line.shape[1]:
            wide = jnp.concatenate([line, jnp.zeros((8, width - line.shape[1]), F32)], axis=1)
        if plan.direct:
            own = count * d // plan.fsdp
            me = lax.axis_index("fsdp")
            wide = pltpu.roll(wide, lax.rem(me * own + (width - start), width), 1)
            lane = lax.broadcasted_iota(jnp.int32, (8, width), 1)
            wide = jnp.where((lane >= me * own) & (lane < (me + 1) * own), wide, 0.0)
            start += own
        else:
            wide = line[:, start : start + count * d]
            start += count * d
        for j in range(count):
            rows_s[at + j : at + j + 1, :] = wide[0:1, j * d : (j + 1) * d]
        at += count
    first[5 * r : 5 * r + 16, :] = rows_s[...].astype(BF)
    for copy in copies:
        copy.wait()


def join(*refs):
    out, at = refs[-1], 0
    for ref in refs[:-1]:
        out[at : at + ref.shape[0], :] = ref[...]
        at += ref.shape[0]


def join_after(gate, *refs):
    del gate
    join(*refs)


def views(plan, joined):
    if not plan.direct:
        return joined
    found = []
    rows = sum(ref.shape[0] for ref in joined) // plan.shards
    for mine, sibling in zip(joined[::2], joined[1::2]):
        for m in range(mine.shape[0] // rows):
            found += [ref.at[pl.ds(m * rows, rows), :] for ref in (mine, sibling)]
    return found


def place(plan, shards, block, target, column):
    d, r = plan.d, plan.rows
    for k, shard in enumerate(shards):
        at = pl.multiple_of(shard_of(plan, k) * r, 16)
        target[pl.ds(at, r), column * d : (column + 1) * d] = shard[block * r : (block + 1) * r, :]


def emit(plan, grads, blocks, send, keep, rows):
    r = plan.rows
    for name, xor in ((keep, 0),) if send is None else ((send, 1), (keep, 0)):
        for m in range(len(plan.peers) if plan.direct else 1):
            owner = shard_of(plan, 2 * m + xor)
            for at, ref, column, stride, offset in blocks:
                start = pl.multiple_of(owner * (stride * r) + offset * r, 16)
                name[m * rows + at * r : m * rows + (at + 1) * r, :] = ref[
                    pl.ds(start, r), column * plan.d : (column + 1) * plan.d
                ]


def attn_forward(plan, *refs):
    s = plan.shards
    x, cond, cot = refs[:3]
    shards = refs[3 : 3 + s]
    (projected, mixed, modulation, bias, qkv_out, ada_out, x_out, cot_out, qkv, ada,
     sems) = refs[3 + s :]
    x_out[...] = x[...]
    cot_out[...] = cot[...]
    d, length, r = plan.d, plan.seq, plan.rows
    for j in range(3):
        place(plan, shards, j, qkv, j)
    for j in range(2):
        place(plan, shards, 3 + j, ada, j)
    copies = [
        pltpu.make_async_copy(qkv, qkv_out, sems.at[0]),
        pltpu.make_async_copy(ada, ada_out, sems.at[1]),
    ]
    for copy in copies:
        copy.start()
    total = shards[0][5 * r : 5 * r + 16, :].astype(F32)
    for shard in shards[1:]:
        total = total + shard[5 * r : 5 * r + 16, :].astype(F32)
    bias[...] = total
    cond_act = silu(cond[...].astype(F32)).astype(BF)
    mod = dot(cond_act, ada[...])
    for j in range(2):
        modulation[:, j * d : (j + 1) * d] = mod[:, j * d : (j + 1) * d] + bias[j : j + 1, :]
    left = lax.broadcasted_iota(jnp.int32, (1, 128), 1) < 64

    def latent(g, carry):
        at = pl.ds(pl.multiple_of(g * length, length), length)
        shift = modulation[pl.ds(g, 1), 0:d]
        scale = modulation[pl.ds(g, 1), d : 2 * d]
        normed, _ = normalize(x[at, :].astype(F32))
        rounded = (normed * (1.0 + scale) + shift).astype(BF)
        for j in range(3):
            piece = dot(rounded, qkv[:, j * d : (j + 1) * d])
            if j != 1:
                piece = piece + bias[6 + j // 2 : 7 + j // 2, :]
            projected[at, j * d : (j + 1) * d] = piece.astype(BF)
        for pair in range(HEADS // 2):
            lanes = slice(pair * 128, (pair + 1) * 128)
            q = projected[at, lanes] * jnp.asarray(0.125, BF)
            k = projected[at, d + pair * 128 : d + (pair + 1) * 128]
            v = projected[at, 2 * d + pair * 128 : 2 * d + (pair + 1) * 128]
            halves = []
            for side in (left, ~left):
                scores = dot_nt(jnp.where(side, q, jnp.zeros_like(q)), k)
                exponent = jnp.exp(scores - jnp.max(scores, axis=-1, keepdims=True))
                probs = exponent * (1.0 / jnp.sum(exponent, axis=-1, keepdims=True))
                halves.append(dot(probs.astype(BF), v))
            mixed[at, lanes] = jnp.where(left, halves[0], halves[1]).astype(BF)
        return carry

    lax.fori_loop(0, plan.group, latent, 0)
    for copy in copies:
        copy.wait()


def mlp_both(plan, *refs):
    s = 4 if plan.direct else 1
    lives, x, cot, mixed, bias, cond = refs[:6]
    shards, refs = views(plan, refs[6 : 6 + s]), refs[6 + s :]
    (send, refs) = (refs[0], refs[1:]) if plan.direct else (None, refs)
    (keep, act, grad_pre, grad_out, middle, attn_out, modulation, fc1, fc2, mixed_out, cot_out,
     proj, ada_out, mlp_in, turned, grad_fc1, grad_fc2, ada, sems) = refs
    mixed_out[...] = mixed[...]
    cot_out[...] = cot[...]
    d, length, ffb, r = plan.d, plan.seq, plan.ffb, plan.rows
    r4 = r * ffb
    for j in range(ffb):
        place(plan, shards, j, fc1, j)
    for k, shard in enumerate(shards):
        at = pl.multiple_of(shard_of(plan, k) * r4, 16)
        fc2[pl.ds(at, r4), :] = shard[(ffb + 5) * r : (ffb + 5) * r + r4, :]
    for j in range(4):
        place(plan, shards, ffb + j, ada, j)
    copy = pltpu.make_async_copy(ada, ada_out, sems.at[0])
    copy.start()
    place(plan, shards, ffb + 4, proj, 0)
    mod = dot(silu(cond[...].astype(F32)).astype(BF), ada[...])
    for j in range(4):
        modulation[:, j * d : (j + 1) * d] = mod[:, j * d : (j + 1) * d] + bias[2 + j : 3 + j, :]

    def latent(g, carry):
        at = pl.ds(pl.multiple_of(g * length, length), length)
        gate_attn, shift, scale, gate = [
            modulation[pl.ds(g, 1), j * d : (j + 1) * d] for j in range(4)
        ]
        live = lives[pl.ds(g, 1), 0:1]
        out = dot(mixed[at, :], proj[...]) + bias[8:9, :]
        attn_out[at, :] = out
        mid = x[at, :].astype(F32) + gate_attn * out
        middle[at, :] = mid
        normed, _ = normalize(mid)
        mlp_in[at, :] = (normed * (1.0 + scale) + shift).astype(BF)
        grad_out[at, :] = ((gate * live) * cot[at, :].astype(F32)).astype(BF)
        return carry

    lax.fori_loop(0, plan.group, latent, 0)
    turned[...] = mlp_in[...].T
    step = 256
    for c in range(plan.ff // step):
        cols = slice(c * step, (c + 1) * step)
        pieces = []
        start, rest = c * step, step
        while rest:
            row, lane = divmod(start, d)
            width = min(rest, d - lane)
            pieces.append(bias[9 + row : 10 + row, lane : lane + width])
            start, rest = start + width, rest - width
        shift = pieces[0] if len(pieces) == 1 else jnp.concatenate(pieces, axis=1)
        pre = dot(mlp_in[...], fc1[:, cols]) + shift
        square = pre * pre
        bend = jnp.tanh(pre * (SQRT_2_PI + (SQRT_2_PI * CUBIC) * square))
        half = 0.5 + 0.5 * bend
        value = (pre * half).astype(BF)
        act[:, cols] = value
        slope = (0.5 * SQRT_2_PI) + (1.5 * SQRT_2_PI * CUBIC) * square
        gelu_back = half + pre * (1.0 - bend * bend) * slope
        grad = (dot_nt(grad_out[...], fc2[cols, :]) * gelu_back).astype(BF)
        grad_pre[:, cols] = grad
        grad_fc2[cols, :] = dot_tn(value, grad_out[...]).astype(BF)
        grad_fc1[:, cols] = dot(turned[...], grad).astype(BF)
    blocks = [(j, grad_fc1, j, 1, 0) for j in range(ffb)]
    blocks += [(ffb + j, grad_fc2, 0, ffb, j) for j in range(ffb)]
    emit(plan, None, blocks, send, keep, 2 * r4)
    copy.wait()


def mlp_close(plan, lives, cot, act, fc2, middle, modulation, bias, block_out, grad_gate):
    d, length = plan.d, plan.seq

    def latent(g, carry):
        at = pl.ds(pl.multiple_of(g * length, length), length)
        gate = modulation[pl.ds(g, 1), 3 * d : 4 * d]
        live = lives[pl.ds(g, 1), 0:1]
        mlp_out = dot(act[at, :], fc2[...]) + bias[9 + plan.ffb : 10 + plan.ffb, :]
        block_out[at, :] = (live * (middle[at, :] + gate * mlp_out)).astype(BF)
        upstream = cot[at, :].astype(F32) * live
        grad_gate[pl.ds(g, 1), :] = jnp.sum(upstream * mlp_out, axis=0, keepdims=True)
        return carry

    lax.fori_loop(0, plan.group, latent, 0)


def mlp_back(plan, lives, cot, grad_pre, fc1, middle, attn_out, modulation, mixed, proj, grad_out,
             grad_mixed, grad_middle, grad_proj, misc, grad_mod, grad_gates):
    d, length = plan.d, plan.seq
    misc[...] = jnp.zeros_like(misc)
    sums = jnp.sum(grad_pre[...].astype(F32), axis=0, keepdims=True)
    for j in range(plan.ffb):
        misc[3 + j : 4 + j, :] = sums[:, j * d : (j + 1) * d]
    misc[3 + plan.ffb : 4 + plan.ffb, :] = jnp.sum(
        grad_out[...].astype(F32), axis=0, keepdims=True
    )

    def latent(g, carry):
        at = pl.ds(pl.multiple_of(g * length, length), length)
        gate_attn, _, scale = [modulation[pl.ds(g, 1), j * d : (j + 1) * d] for j in range(3)]
        live = lives[pl.ds(g, 1), 0:1]
        upstream = cot[at, :].astype(F32) * live
        normed, rstd = normalize(middle[at, :])
        grad_in = dot_nt(grad_pre[at, :], fc1[...])
        grad_mid = upstream + norm_back(grad_in * (1.0 + scale), normed, rstd)
        grad_middle[at, :] = grad_mid
        rounded = (gate_attn * grad_mid).astype(BF)
        grad_gates[at, :] = rounded
        grad_mixed[at, :] = dot_nt(rounded, proj[...]).astype(BF)
        pieces = [grad_mid * attn_out[at, :], grad_in, grad_in * normed]
        for j, piece in enumerate(pieces):
            grad_mod[pl.ds(g, 1), j * d : (j + 1) * d] = jnp.sum(piece, axis=0, keepdims=True)
        return carry

    lax.fori_loop(0, plan.group, latent, 0)
    misc[2:3, :] = jnp.sum(grad_gates[...].astype(F32), axis=0, keepdims=True)
    grad_proj[...] = dot_tn(mixed[...], grad_gates[...]).astype(BF)


def attn_core_back(plan, at, projected, grad_mixed, out, where):
    d = plan.d
    left = lax.broadcasted_iota(jnp.int32, (1, 128), 1) < 64
    for pair in range(HEADS // 2):
        lanes = slice(pair * 128, (pair + 1) * 128)
        q = projected[at, lanes] * jnp.asarray(0.125, BF)
        k = projected[at, d + pair * 128 : d + (pair + 1) * 128]
        v = projected[at, 2 * d + pair * 128 : 2 * d + (pair + 1) * 128]
        gm = grad_mixed[at, lanes]
        grads_q, grads_k, grads_v = [], [], []
        for side in (left, ~left):
            scores = dot_nt(jnp.where(side, q, jnp.zeros_like(q)), k)
            exponent = jnp.exp(scores - jnp.max(scores, axis=-1, keepdims=True))
            probs = exponent * (1.0 / jnp.sum(exponent, axis=-1, keepdims=True))
            grad_probs = dot_nt(jnp.where(side, gm, jnp.zeros_like(gm)), v)
            inner = jnp.sum(probs * grad_probs, axis=-1, keepdims=True)
            grad_scores = (probs * (grad_probs - inner)).astype(BF)
            grads_q.append(dot(grad_scores, k))
            grads_k.append(dot_tn(grad_scores, q))
            grads_v.append(dot_tn(probs.astype(BF), gm))
        for j, (pieces, factor) in enumerate(((grads_q, 0.125), (grads_k, 1.0), (grads_v, 1.0))):
            merged = jnp.where(left, pieces[0], pieces[1]) * factor
            out[where, j * d + pair * 128 : j * d + (pair + 1) * 128] = merged.astype(BF)


def attn_back(plan, g, projected, grad_mixed, out):
    at = slice(g * plan.seq, (g + 1) * plan.seq)
    attn_core_back(plan, at, projected, grad_mixed, out, slice(0, plan.seq))


def attn_close(plan, *refs):
    (x, cond, grad_middle, qkv, modulation, grad_mod, grad_gate) = refs[:7]
    parts, outs = refs[7 : 7 + plan.group], refs[7 + plan.group :]
    latents_grad, mods, attn_in, rows_s, cond_s = outs
    d, length = plan.d, plan.seq
    rows_s[...] = jnp.zeros_like(rows_s)
    cond_s[...] = silu(cond[...].astype(F32))
    for g, part in enumerate(parts):
        at = slice(g * length, (g + 1) * length)
        shift = modulation[g : g + 1, 0:d]
        scale = modulation[g : g + 1, d : 2 * d]
        normed, rstd = normalize(x[at, :].astype(F32))
        attn_in[at, :] = (normed * (1.0 + scale) + shift).astype(BF)
        grad_in = dot_nt(part[...], qkv[...])
        grad = grad_middle[at, :] + norm_back(grad_in * (1.0 + scale), normed, rstd)
        latents_grad[at, :] = grad.astype(BF)
        pieces = [cond_s[g : g + 1, :], jnp.sum(grad_in, axis=0, keepdims=True)]
        pieces += [jnp.sum(grad_in * normed, axis=0, keepdims=True)]
        pieces += [grad_mod[g : g + 1, j * d : (j + 1) * d] for j in range(3)]
        pieces += [grad_gate[g : g + 1, :]]
        for j, piece in enumerate(pieces):
            rows_s[g * 7 + j : g * 7 + j + 1, :] = piece
    mods[...] = rows_s[...].astype(BF)


def attn_grads(plan, *refs):
    attn_in, grad_proj, misc = refs[:3]
    parts, outs = refs[3 : 3 + plan.group], refs[3 + plan.group :]
    (send, outs) = (outs[0], outs[1:]) if plan.direct else (None, outs)
    keep, grad_qkv, misc_s, turned = outs
    d, length, r = plan.d, plan.seq, plan.rows
    misc_s[...] = misc[...]
    turned[...] = attn_in[...].T
    for j in range(3):
        cols = slice(j * d, (j + 1) * d)
        total, sums = 0.0, 0.0
        for g, part in enumerate(parts):
            piece = part[:, cols]
            total = total + dot(turned[:, g * length : (g + 1) * length], piece)
            sums = sums + jnp.sum(piece.astype(F32), axis=0, keepdims=True)
        grad_qkv[:, cols] = total.astype(BF)
        if j != 1:
            misc_s[j // 2 : j // 2 + 1, :] = sums
    blocks = [(j, grad_qkv, j, 1, 0) for j in range(3)] + [(3, grad_proj, 0, 1, 0)]
    rows = 4 * r + 16
    emit(plan, None, blocks, send, keep, rows)
    low = misc_s[...].astype(BF)
    for name in (keep,) if send is None else (send, keep):
        for m in range(len(plan.peers) if plan.direct else 1):
            name[m * rows + 4 * r : (m + 1) * rows, :] = low


def cond_back(plan, cond, mods, first, second, grad):
    d = plan.d
    rows = mods[...].astype(F32)
    total = None
    kept = []
    for g in range(plan.group):
        total = jnp.zeros((1, d), F32)
        for j in range(6):
            weight = first[:, j * d : (j + 1) * d] if j < 2 else second[:, (j - 2) * d : (j - 1) * d]
            line = jnp.broadcast_to(rows[g * 7 + 1 + j : g * 7 + 2 + j, :], (8, d)).astype(BF)
            total = total + dot_nt(line, weight)[0:1, :]
        kept.append(total)
    for g in range(plan.group):
        v = cond[g : g + 1, :].astype(F32)
        gate = 1.0 / (1.0 + jnp.exp(-v))
        grad[g : g + 1, :] = (kept[g] * (gate * (1.0 + v * (1.0 - gate)))).astype(BF)


def add_siblings(peers, rows, *refs):
    keep, received, own = refs[:3]
    outs = refs[3:]
    for m in range(peers):
        at = slice(m * rows, (m + 1) * rows)
        total = keep[at, :].astype(F32) + received[at, :].astype(F32)
        if m == 0:
            own[...] = total
        else:
            outs[m - 1][...] = total.astype(BF)


def add_chips(count, dp, quarter, own, *refs):
    received, (mine, sent, total_s) = refs[:count], refs[count:]
    total = own[...]
    for piece in received:
        total = total + piece[...].astype(F32)
    total_s[...] = total
    me = lax.axis_index("dp")
    for j in range(dp):
        part = total_s[pl.ds(pl.multiple_of((me ^ j) * quarter, 16), quarter), :]
        out = sent if j % 2 else mine
        out[j // 2 * quarter : (j // 2 + 1) * quarter, :] = part.astype(out.dtype)


def halve(quarter, held, received, mine, sent):
    for j in range(held.shape[0] // quarter):
        at = slice(j * quarter, (j + 1) * quarter)
        out = sent if j % 2 else mine
        total = held[at, :] + received[at, :].astype(F32)
        out[j // 2 * quarter : (j // 2 + 1) * quarter, :] = total.astype(out.dtype)


def gather_groups(dp, orders, layouts, *refs):
    count = sum(len(order) for order in orders)
    arrays, outs, scratch = list(refs[:count]), list(refs[count : -len(orders)]), refs[-len(orders) :]
    me = lax.axis_index("dp")
    for order, layout, rows_s in zip(orders, layouts, scratch):
        quarter, d = rows_s.shape[0] // dp, rows_s.shape[1]
        for some in order:
            array = arrays.pop(0)
            for i, j in enumerate(some):
                at = pl.multiple_of((me ^ j) * quarter, 16)
                piece = array[i * quarter : (i + 1) * quarter, :]
                rows_s[pl.ds(at, quarter), :] = piece.astype(F32)
        at = 0
        for blocks, rows in layout:
            out = outs.pop(0)
            for j in range(blocks):
                out[:, j * d : (j + 1) * d] = rows_s[at : at + rows, :]
                at += rows


def last_sibling(peers, rows, keep, received, mods, own, *outs):
    for m in range(peers):
        at = slice(m * rows, (m + 1) * rows)
        total = keep[at, :].astype(F32) + received[at, :].astype(F32)
        if m == 0:
            own[0:rows, :] = total
            own[rows : rows + MOD_ROWS, :] = mods[...].astype(F32)
        else:
            outs[m - 1][0:rows, :] = total.astype(BF)
            outs[m - 1][rows : rows + MOD_ROWS, :] = mods[...]


def last_chips(count, dp, quarter, rows, own, *refs):
    received, mine, outs = refs[:count], refs[count], refs[count + 1 : count + dp]
    total_s, tail_s = refs[count + dp :]
    tail_s[...] = jnp.zeros_like(tail_s)
    total = own[0:rows, :]
    for piece in received:
        total = total + piece[0:rows, :].astype(F32)
    total_s[...] = total[: rows - 16]
    for i, piece in enumerate((own,) + received):
        lines = piece[rows:, :].astype(F32)
        tail_s[i * MOD_USED : (i + 1) * MOD_USED, :] = lines[0:MOD_USED]
    end = (count + 1) * MOD_USED
    tail_s[end : end + 8, :] = total[rows - 16 : rows - 8]
    me = lax.axis_index("dp")
    for j in range(dp):
        part = total_s[pl.ds(pl.multiple_of((me ^ j) * quarter, 16), quarter), :]
        name = mine if j == 0 else outs[j - 1]
        name[0:quarter, :] = part.astype(name.dtype)
        name[quarter:, :] = tail_s[...].astype(name.dtype)


def add_two(first, second, out):
    out[...] = (first[...] + second[...].astype(F32)).astype(BF)


def add_groups(dp, quarter, *refs):
    pieces, (low, mods) = refs[:dp], refs[dp:]
    total = pieces[0][0:quarter, :]
    for piece in pieces[1:]:
        total = total + piece[0:quarter, :].astype(F32)
    low[...] = total.astype(BF)
    each = pieces[0].shape[0] - quarter
    for j, piece in enumerate(pieces):
        mods[j * each : (j + 1) * each, :] = piece[quarter:, :].astype(BF)


def ada_grads(plan, quarter, *refs):
    dp, d, r = plan.dp, plan.d, plan.rows
    pieces, mods = refs[:dp], refs[dp : dp + 2]
    ada, ada_bias, qv, proj, fc1, fc2 = refs[dp + 2 : dp + 8]
    rows_s, turned_s = refs[dp + 8 :]
    block = pieces[0].shape[0] - quarter
    used = len(plan.peers) * MOD_USED
    each = dp * block
    total = pieces[0][quarter + used : quarter + used + 8, :].astype(F32)
    for piece in pieces[1:]:
        total = total + piece[quarter:, :].astype(F32)[used : used + 8]
    for j, rows in enumerate(mods):
        rows_s[j * each : (j + 1) * each, :] = rows[...]
    count = 2 * each
    row = lax.broadcasted_iota(jnp.int32, (count, count), 0)
    column = lax.broadcasted_iota(jnp.int32, (count, count), 1)
    slot = row % block
    pick = ((column == row - slot % 7) & (slot < used)).astype(BF)
    turned_s[...] = dot(pick, rows_s[...]).T
    me = lax.axis_index("fsdp")
    mine = turned_s[pl.ds(pl.multiple_of(me * r, 16), r), :].astype(BF)
    lane = lax.broadcasted_iota(jnp.int32, (1, count), 1) % block
    tall = lax.broadcasted_iota(jnp.int32, (count, 1), 0) % block
    values = rows_s[...]
    sums = []
    for j in range(6):
        here = (lane % 7 == 1 + j) & (lane < used)
        ada[:, j * d : (j + 1) * d] = dot(jnp.where(here, mine, jnp.zeros_like(mine)), values)
        there = (tall % 7 == 1 + j) & (tall < used)
        sums.append(
            jnp.sum(jnp.where(there, values.astype(F32), 0.0), axis=0, keepdims=True)
        )
    lists = [
        (ada_bias, sums),
        (qv, [total[0:1], total[1:2]]),
        (proj, [total[2:3]]),
        (fc1, [total[3 + j : 4 + j] for j in range(plan.ffb)]),
        (fc2, [total[3 + plan.ffb : 4 + plan.ffb]]),
    ]
    for out, lines in lists:
        wide = lines[0] if len(lines) == 1 else jnp.concatenate(lines, axis=1)
        width = wide.shape[1]
        own = width // plan.fsdp
        wide = jnp.broadcast_to(wide, (8, width))
        wide = pltpu.roll(wide, lax.rem(width - me * own, width), 1)
        out[...] = wide[0:1, :own]


def swap(plan, value, k, axis="fsdp"):
    size = plan.fsdp if axis == "fsdp" else plan.dp
    return lax.ppermute(value, axis, [(i, i ^ k) for i in range(size)])


def behind(values, *gates):
    gates = [gate for gate in gates if gate is not None]
    return list(lax.optimization_barrier((tuple(values), tuple(gates)))[0])


def gather_chips(plan, value):
    if not plan.direct:
        return [value]
    return [value] + [swap(plan, value, k) for k in plan.peers[1:]]


def gather_joined(plan, gate, chips):
    if not plan.direct:
        return chips
    joined = []
    count = len(chips) // 2
    for some in (chips[:count], chips[count:]):
        shape = (sum(v.shape[0] for v in some), plan.d)
        (mine,) = call(join_after, [(shape, BF)], [gate] + some, micros=0.4)
        joined += [mine, swap(plan, mine, 1)]
    return joined


def gather_cores(plan, chips):
    if not plan.direct:
        return chips
    cores = [swap(plan, shard, 1) for shard in chips]
    return [shard for pair in zip(chips, cores) for shard in pair]


def chunk_siblings(plan, send, keep, gate):
    d, peers = plan.d, len(plan.peers)
    rows = keep.shape[0] // peers
    received = swap(plan, send, 1)
    keep, received = behind([keep, received], gate)
    own, *pieces = call(
        functools.partial(add_siblings, peers, rows),
        [((rows, d), F32)] + [((rows, d), BF)] * (peers - 1),
        [keep, received],
    )
    return own, [swap(plan, piece, k) for piece, k in zip(pieces, plan.peers[1:])]


def chunk_chips(plan, own, pieces):
    d, dp = plan.d, plan.dp
    rows = own.shape[0]
    mine, sent = call(
        functools.partial(add_chips, len(pieces), dp, rows // dp),
        [((rows // 2, d), F32), ((rows // 2, d), BF)],
        [own] + pieces,
        [pltpu.VMEM((rows, d), F32)],
    )
    return mine, swap(plan, sent, 1, "dp")


def chunk_halves(plan, mine, received):
    dp, step = plan.dp, 2
    quarter = 2 * mine.shape[0] // dp
    while mine.shape[0] > quarter:
        shape = (mine.shape[0] // 2, plan.d)
        mine, sent = call(
            functools.partial(halve, quarter), [(shape, F32), (shape, BF)], [mine, received]
        )
        received, step = swap(plan, sent, step, "dp"), 2 * step
    return mine, received


def finish(plan, mlp_own, mlp_pieces, mlp_layout, send, keep, mods, cond_grad):
    d, dp, peers, r = plan.d, plan.dp, len(plan.peers), plan.rows
    rows = keep.shape[0] // peers
    quarter = (rows - 16) // dp
    received = swap(plan, send, 1)
    mlp_mine, mlp_half = chunk_chips(plan, mlp_own, mlp_pieces)
    received, keep = behind([received, keep], mlp_mine)
    mlp_mine, mlp_half = chunk_halves(plan, mlp_mine, mlp_half)
    long = rows + MOD_ROWS
    own, *pieces = call(
        functools.partial(last_sibling, peers, rows),
        [((long, d), F32)] + [((long, d), BF)] * (peers - 1),
        [keep, received, mods],
    )
    pieces = [swap(plan, piece, k) for piece, k in zip(pieces, plan.peers[1:])]
    pieces = behind(pieces, cond_grad, mlp_half)
    tail = -(-(peers * MOD_USED + 8) // 16) * 16
    mine, *quarters = call(
        functools.partial(last_chips, peers - 1, dp, quarter, rows),
        [((quarter + tail, d), F32)] + [((quarter + tail, d), BF)] * (dp - 1),
        [own] + pieces,
        [pltpu.VMEM((rows - 16, d), F32), pltpu.VMEM((tail, d), F32)],
    )
    quarters = [swap(plan, part, j + 1, "dp") for j, part in enumerate(quarters)]
    mlp_mine, mlp_half = behind([mlp_mine, mlp_half], mine)
    (held,) = call(add_two, [(mlp_mine.shape, BF)], [mlp_mine, mlp_half])
    order, step = [0], dp // 2
    while step > 1:
        found = [held, swap(plan, held, step, "dp")]
        order, step = order + [j ^ step for j in order], step // 2
        (held,) = call(join, [((2 * held.shape[0], d), BF)], found)
    half = dp * tail
    low, mods = call(
        functools.partial(add_groups, dp, quarter),
        [((quarter, d), BF), ((half, d), BF)],
        [mine] + quarters,
    )
    parts = [swap(plan, low, j, "dp") for j in range(1, dp)] + [swap(plan, held, 1, "dp")]
    orders = ((order, [j ^ 1 for j in order]), [[j] for j in range(dp)])
    ada, *biases = call(
        functools.partial(ada_grads, plan, quarter),
        [((r, 6 * d), F32)] + [((1, w * d // plan.fsdp), F32) for w in plan.bias_rows],
        [mine] + quarters + [mods, swap(plan, mods, 1)],
        [pltpu.VMEM((2 * half, d), BF), pltpu.VMEM((d, 2 * half), F32)],
        micros=2,
    )
    biases = [bias.reshape(-1) for bias in biases]
    *parts, other = behind(parts, ada, *biases)
    layouts = (mlp_layout, ((3, r), (1, r)))
    fc1, fc2, qkv, proj = call(
        functools.partial(gather_groups, dp, orders, layouts),
        [((height, blocks * d), F32) for layout in layouts for blocks, height in layout],
        [held, other, low] + parts,
        [pltpu.VMEM((size, d), F32) for size in (held.shape[0] * 2, quarter * dp)],
    )
    return [ada, qkv, proj, fc1, fc2], biases


def reduce_whole(plan, mlp, last, mods):
    d, ffb = plan.d, plan.ffb
    fc1_rows, fc2_rows = mlp[: ffb * d], mlp[ffb * d :]

    def unpack(rows, blocks):
        return rows.reshape(blocks, d, d).transpose(1, 0, 2).reshape(d, blocks * d)

    mods = mods[: 7 * plan.group].reshape(plan.group, 7, d)
    cond_act, grad_mod = mods[:, 0], mods[:, 1:].reshape(plan.group, 6 * d)
    ada = jnp.dot(cond_act.T, grad_mod, preferred_element_type=F32)
    misc = last[4 * d : 4 * d + 16]
    grads = (
        ada,
        jnp.sum(grad_mod.astype(F32), axis=0),
        unpack(last[: 3 * d], 3),
        misc[0:2].reshape(-1),
        last[3 * d : 4 * d],
        misc[2],
        unpack(fc1_rows, ffb),
        misc[3 : 3 + ffb].reshape(-1),
        fc2_rows,
        misc[3 + ffb],
    )
    owned = [
        lax.psum_scatter(grad.astype(BF), "fsdp", scatter_dimension=0, tiled=True) for grad in grads
    ]
    return [lax.psum(grad, "dp").astype(F32) for grad in owned]


def shards(
    fsdp,
    dp,
    latents,
    condition,
    cotangent,
    counts,
    ada_weight,
    ada_bias,
    qkv_weight,
    qv_bias,
    proj_weight,
    proj_bias,
    fc1_weight,
    fc1_bias,
    fc2_weight,
    fc2_bias,
):
    plan = Plan(latents, ada_weight, fc1_weight, fsdp, dp)
    d, n, group, ff, r = plan.d, plan.tokens, plan.group, plan.ff, plan.rows
    x = latents.reshape(n, d)
    cot = cotangent.reshape(n, d)
    cond = condition.reshape(group, d)
    biases = [ada_bias, qv_bias, proj_bias, fc1_bias, fc2_bias]
    weights = [ada_weight, qkv_weight, proj_weight, fc1_weight]
    third = fc2_weight
    if not plan.direct:
        def whole(v):
            return lax.all_gather(v, "fsdp", axis=0, tiled=True)

        biases, weights, third = [whole(v) for v in biases], [whole(v) for v in weights], whole(third)
    lengths = [bias.shape[0] for bias in biases]
    width = -(-sum(lengths) // 1024) * 1024
    line = sum(
        jnp.pad(bias.astype(F32), (sum(lengths[:i]), width - sum(lengths[: i + 1])))
        for i, bias in enumerate(biases)
    )
    first, second, live = call(
        functools.partial(pack_weights, plan),
        [((5 * r + 16, d), BF), (((2 * plan.ffb + 5) * r, d), BF), ((group, 128), F32)],
        weights + [third, line.reshape(1, -1), counts.T],
        [pltpu.VMEM((16, d), F32), pltpu.SemaphoreType.DMA((plan.ffb + 11,))],
        smem=(6,),
        far=(0, 1, 2, 3, 4),
        limit=PACK_LIMIT,
        micros=1.0,
    )
    first = gather_cores(plan, gather_chips(plan, first))
    second = gather_chips(plan, second)

    projected, mixed, mod_first, bias, qkv, ada_first, x_near, cot_near = call(
        functools.partial(attn_forward, plan),
        [
            ((n, 3 * d), BF),
            ((n, d), BF),
            ((group, 2 * d), F32),
            ((16, d), F32),
            ((d, 3 * d), BF),
            ((d, 2 * d), BF),
            ((n, d), BF),
            ((n, d), BF),
        ],
        [x, cond, cot] + first,
        [
            pltpu.VMEM((d, 3 * d), BF),
            pltpu.VMEM((d, 2 * d), BF),
            pltpu.SemaphoreType.DMA((2,)),
        ],
        far_outs=(4, 5),
        room=5,
        micros=4,
    )
    shards = gather_joined(plan, mod_first, second)
    halves = len(plan.peers) if plan.direct else 1
    sides = plan.sides
    outs = call(
        functools.partial(mlp_both, plan),
        [((halves * 2 * plan.ffb * r, d), BF)] * sides
        + [
            ((n, ff), BF),
            ((n, ff), BF),
            ((n, d), BF),
            ((n, d), F32),
            ((n, d), F32),
            ((group, 4 * d), F32),
            ((d, ff), BF),
            ((ff, d), BF),
            ((n, d), BF),
            ((n, d), BF),
            ((d, d), BF),
            ((d, 4 * d), BF),
        ],
        [live, x_near, cot_near, mixed, bias, cond] + shards,
        [
            pltpu.VMEM((n, d), BF),
            pltpu.VMEM((d, n), BF),
            pltpu.VMEM((d, ff), BF),
            pltpu.VMEM((ff, d), BF),
            pltpu.VMEM((d, 4 * d), BF),
            pltpu.SemaphoreType.DMA((1,)),
        ],
        far_outs=(sides + 11,),
        room=5,
        micros=10,
    )
    mlp_chunk = outs[:sides]
    (act, grad_pre, grad_out, middle, attn_out, mod_second, fc1, fc2, mixed, cot_near, proj,
     ada_second) = outs[sides:]
    block_out, grad_gate = call(
        functools.partial(mlp_close, plan),
        [((n, d), BF), ((group, d), F32)],
        [live, cot_near, act, fc2, middle, mod_second, bias],
        room=5,
        micros=1.5,
    )
    if plan.direct:
        mlp_own, mlp_pieces = chunk_siblings(plan, *mlp_chunk, grad_gate)
        (grad_pre,) = behind([grad_pre], mlp_own)
    grad_mixed, grad_middle, grad_proj, misc, grad_mod = call(
        functools.partial(mlp_back, plan),
        [
            ((n, d), BF),
            ((n, d), F32),
            ((d, d), BF),
            ((16, d), F32),
            ((group, 3 * d), F32),
        ],
        [live, cot_near, grad_pre, fc1, middle, attn_out, mod_second, mixed, proj, grad_out],
        [pltpu.VMEM((n, d), BF)],
        room=5,
        micros=3,
    )
    parts = []
    for g in range(group):
        parts += call(
            functools.partial(attn_back, plan, g),
            [((plan.seq, 3 * d), BF)],
            [projected, behind([grad_mixed], *parts)[0]],
            room=5,
            micros=3.3,
        )
    latents_grad, mods, attn_in = call(
        functools.partial(attn_close, plan),
        [((n, d), BF), ((MOD_ROWS, d), BF), ((n, d), BF)],
        [x, cond, grad_middle, qkv, mod_first, grad_mod, grad_gate] + parts,
        [pltpu.VMEM((MOD_ROWS, d), F32), pltpu.VMEM((group, d), F32)],
        room=5,
        micros=2,
    )
    (cond_grad,) = call(
        functools.partial(cond_back, plan),
        [((group, d), BF)],
        [cond, mods, ada_first, ada_second],
        micros=2,
    )
    last_chunk = call(
        functools.partial(attn_grads, plan),
        [((halves * (4 * r + 16), d), BF)] * sides,
        [attn_in, grad_proj, misc] + parts,
        [
            pltpu.VMEM((d, 3 * d), BF),
            pltpu.VMEM((16, d), F32),
            pltpu.VMEM((d, n), BF),
        ],
        room=5,
        micros=0.1,
    )
    if plan.direct:
        layout = ((plan.ffb, r), (1, plan.ffb * r))
        weight_grads, bias_grads = finish(
            plan, mlp_own, mlp_pieces, layout, *last_chunk, mods, cond_grad
        )
        grads = [grad for pair in zip(weight_grads, bias_grads) for grad in pair]
    else:
        grads = reduce_whole(plan, mlp_chunk[0], last_chunk[0], mods)
    return (
        block_out.reshape(latents.shape),
        latents_grad.reshape(latents.shape),
        cond_grad.reshape(condition.shape),
        *grads,
    )


def solution(mesh):
    tokens = P(None, ("dp", "fsdp"), None, None)
    per_latent = P(None, ("dp", "fsdp"), None)
    weight, bias = P("fsdp", None), P("fsdp")
    in_specs = (tokens, per_latent, tokens, P(None, ("dp", "fsdp"))) + (weight, bias) * 5
    out_specs = (tokens, tokens, per_latent) + (weight, bias) * 5
    body = functools.partial(shards, mesh.shape["fsdp"], mesh.shape["dp"])
    return jax.shard_map(body, mesh=mesh, in_specs=in_specs, out_specs=out_specs, check_vma=False)
```
